32 devices in a mesh: wide: 4 (over y, x), narrow: 8 (over z, core).
Axes of the slice: x: 2, y: 2, z: 4, core: 2. Of those that a mesh axis runs over, the one named last changes fastest.
Arguments:
- tokens: bfloat16 [16384, 768], P(('wide', 'narrow')), may hold values from -6 to 6
- cotangent: bfloat16 [16384, 768], P(('wide', 'narrow')), may hold values from -6 to 6
- time_emb: bfloat16 [16, 128], replicated, may hold values from -5 to 5
- seq_table: int32 [16], P('wide'), may hold values from 0 to 15, each once
- lengths: int32 [4, 4], P('wide'), may hold values from 1 to 2048, 4096 in all within a row
- positions: int32 [16384], P(('wide', 'narrow')), may hold values from 0 to 8191
- norm1_gain: bfloat16 [768], P('narrow'), may hold values from 0.5 to 1.5
- norm2_gain: bfloat16 [768], P('narrow'), may hold values from 0.5 to 1.5
- ada_weight: bfloat16 [128, 4608], P('narrow'), may hold values from -0.5 to 0.5
- ada_bias: bfloat16 [4608], P('narrow'), may hold values from -3 to 3
- qkv_weight: bfloat16 [768, 2304], P('narrow'), may hold values from -0.21875 to 0.21875
- out_weight: bfloat16 [768, 768], P('narrow'), may hold values from -1.75 to 1.75
- fc1_weight: bfloat16 [768, 3072], P('narrow'), may hold values from -0.21875 to 0.21875
- fc1_bias: bfloat16 [3072], P('narrow'), may hold values from -3 to 3
- fc2_weight: bfloat16 [3072, 768], P('narrow'), may hold values from -0.109375 to 0.109375
- fc2_bias: bfloat16 [768], P('narrow'), may hold values from -5 to 5
Outputs:
- layer_out: bfloat16 [16384, 768], P(('wide', 'narrow'))
- grad_tokens: float32 [16384, 768], P(('wide', 'narrow'))
- grad_time: float32 [16, 128], P('narrow')
- grad_norm1: float32 [768], P('narrow')
- grad_norm2: float32 [768], P('narrow')
- grad_ada_weight: float32 [128, 4608], P('narrow')
- grad_ada_bias: float32 [4608], P('narrow')
- grad_qkv_weight: float32 [768, 2304], P('narrow')
- grad_out_weight: float32 [768, 768], P('narrow')
- grad_fc1_weight: float32 [768, 3072], P('narrow')
- grad_fc1_bias: float32 [3072], P('narrow')
- grad_fc2_weight: float32 [3072, 768], P('narrow')
- grad_fc2_bias: float32 [768], P('narrow')
The draws below stay inside these ranges and needn't reach their ends.
Inputs may be any that keep to these rules, and one draw needn't show every extreme that they name: `seq_table`: each group's 4 entries name the sequences that fill its slots; every sequence is named once. `lengths`: each row sums to 4096.
All inputs are finite; a program needn't handle non-finite values.
Results may differ from the reference program's by a relative error of at most 0.025.
The reference program's roundings to bfloat16 on the way count: a program that leaves them out, or rounds other values in their place, can miss the bound.
Values may be sent and summed in bfloat16 or wider, within the bound.
A program may use at most 192 MiB of HBM per device.

```python
import math
import jax
import jax.numpy as jnp
import numpy as np
from jax import lax

D = 768
HEADS = 12
HEAD_DIM = 64
FF = 3072
COND = 128
GROUPS = 4
GROUP_TOK = 4096
SLOTS = 4
MOST = 2048
SEQS = 16
TOKENS = 16384


def plant(result, key, smallest, largest):
    place = [jax.random.randint(jax.random.fold_in(key, axis), (), 0, length) for axis, length in enumerate(result.shape)]
    longest = result.shape.index(max(result.shape))
    next_to = place[:longest] + [(place[longest] + 1) % result.shape[longest]] + place[longest + 1:]
    return result.at[tuple(place)].set(smallest).at[tuple(next_to)].set(largest)


def block_scale(own_key, extent, cuts, least, high):
    gain = 1.0
    for dim, blocks in cuts:
        draws = jax.random.uniform(jax.random.fold_in(jax.random.fold_in(own_key, 6), dim), (blocks,), jnp.float32, least / len(cuts), high / len(cuts))
        gain = gain * jnp.repeat(jnp.exp(draws), extent[dim] // blocks).reshape((-1,) + (1,) * (len(extent) - 1 - dim))
    return gain


def split_up(amount, total, limit, lean):
    portions = [(1 << 20) // math.isqrt(standing ** lean) + 1 for standing in range(2, amount + 1)]
    spare, given = total - limit - (amount - 1), [1] * (amount - 1)
    while spare > 0:
        movable = [i for i in range(amount - 1) if given[i] < limit]
        mass, remaining = sum([portions[i] for i in movable]), spare
        for i in movable:
            addition = min(limit - given[i], max(1, remaining * portions[i] // mass), spare)
            given[i] = given[i] + addition
            spare = spare - addition
    return np.array([limit] + given)


def uneven(rng, amount, total, bound, lean):
    if amount == 2:
        one = jax.random.randint(rng, (), max(1, total - bound), min(bound, total - 1) + 1)
        return jnp.stack([one, total - one])
    tallies = jnp.asarray(split_up(amount, total, bound, lean), jnp.int32)
    twos = (amount - 1) // 2
    donor, taker = tallies[1:1 + 2 * twos:2], tallies[2:2 + 2 * twos:2]
    slack = jnp.minimum(donor - 1, bound - taker)
    passed = jax.random.randint(jax.random.fold_in(rng, 1), (twos,), 0, 1 << 20) % (slack + 1)
    tallies = tallies.at[1:1 + 2 * twos:2].set(donor - passed).at[2:2 + 2 * twos:2].set(taker + passed)
    return tallies[jax.random.permutation(jax.random.fold_in(rng, 2), amount)]


def gaussian(key, dims, scale, most, cuts=(), kind=jnp.bfloat16):
    gain = block_scale(key, dims, cuts, -0.22, 0.18) if cuts else 1.0
    drawn = jax.random.normal(key, dims, jnp.float32) * scale * gain
    return jnp.minimum(jnp.maximum(drawn, -most), most).astype(kind)


def setup_inputs(seed: int = 0) -> dict:
    seeds = jax.random.split(jax.random.key(seed), 17)
    tokens = gaussian(seeds[0], (TOKENS, D), 1.0, 6.0, ((0, 32),))
    cotangent = gaussian(seeds[1], (TOKENS, D), 1.0, 6.0, ((0, 32),))
    time_emb = gaussian(seeds[2], (SEQS, COND), 1.0, 5.0)
    seq_table = jax.random.permutation(seeds[3], SEQS).astype(jnp.int32)
    lengths = jax.vmap(lambda own: uneven(own, SLOTS, GROUP_TOK, MOST, 2))(jax.random.split(seeds[4], GROUPS)).reshape((GROUPS, SLOTS)).astype(jnp.int32)
    positions = plant(jax.random.randint(seeds[5], (TOKENS,), 0, 8192), jax.random.fold_in(seeds[5], 1), 0, 8191).astype(jnp.int32)
    norm1_gain = jnp.clip(1.0 + 0.1 * jax.random.normal(seeds[6], (D,), jnp.float32), 0.5, 1.5).astype(jnp.bfloat16)
    norm2_gain = jnp.clip(1.0 + 0.1 * jax.random.normal(seeds[7], (D,), jnp.float32), 0.5, 1.5).astype(jnp.bfloat16)
    ada_weight = gaussian(seeds[8], (COND, 6 * D), COND ** -0.5, 0.5, ((0, 8),))
    ada_bias = gaussian(seeds[9], (6 * D,), 0.5, 3.0, ((0, 8),))
    qkv_weight = gaussian(seeds[10], (D, 3 * D), D ** -0.5, 0.21875, ((0, 8),))
    out_weight = gaussian(seeds[11], (D, D), (D // 64) ** -0.5, 1.75, ((0, 8),))
    fc1_weight = gaussian(seeds[12], (D, FF), D ** -0.5, 0.21875, ((0, 8),))
    fc1_bias = gaussian(seeds[13], (FF,), 0.5, 3.0, ((0, 8),))
    fc2_weight = gaussian(seeds[14], (FF, D), FF ** -0.5, 0.109375, ((0, 8),))
    fc2_bias = gaussian(seeds[15], (D,), 1.0, 5.0, ((0, 8),))
    return dict(tokens=tokens, cotangent=cotangent, time_emb=time_emb, seq_table=seq_table, lengths=lengths, positions=positions, norm1_gain=norm1_gain, norm2_gain=norm2_gain, ada_weight=ada_weight, ada_bias=ada_bias, qkv_weight=qkv_weight, out_weight=out_weight, fc1_weight=fc1_weight, fc1_bias=fc1_bias, fc2_weight=fc2_weight, fc2_bias=fc2_bias)


@jax.custom_vjp
def low(v):
    return lax.optimization_barrier(v.astype(jnp.bfloat16)).astype(jnp.float32)

@jax.custom_vjp
def low_back(v):
    return v

def low_keep(v):
    return (low(v), None)

def low_pass(kept, grad):
    return (grad,)

def back_keep(v):
    return (v, None)

def back_low(kept, grad):
    return (low(grad),)
low.defvjp(low_keep, low_pass)
low_back.defvjp(back_keep, back_low)
HIGH = lax.Precision.HIGHEST
EPSILON = 1e-05
NEGATIVE = -1e+30

def norm_rows(values):
    center = values - lax.optimization_barrier(jnp.mean(values, axis=-1, keepdims=True))
    spread = lax.optimization_barrier(jnp.mean(center * center, axis=-1, keepdims=True))
    return center * lax.rsqrt(spread + EPSILON)

def modulated(values, norm_gain, scale_part, shift_part):
    return norm_rows(values) * norm_gain * (1.0 + scale_part) + shift_part

def segment_of(indices, seq_ends):
    return lax.optimization_barrier(jnp.sum((indices[:, None] >= seq_ends[None, :]).astype(jnp.int32), axis=1))

def rotary_tables(positions):
    half_dim = HEAD_DIM // 2
    inverse = 10000.0 ** (-(jnp.arange(half_dim, dtype=jnp.float32) * 2.0) / HEAD_DIM)
    angles = positions.astype(jnp.float32)[:, None] * inverse[None, :]
    return (jnp.cos(angles), jnp.sin(angles))

def rotate(values, cosine, sine):
    half_dim = values.shape[-1] // 2
    first_half = values[..., :half_dim]
    second_half = values[..., half_dim:]
    cos_rows = cosine[:, None, :]
    sin_rows = sine[:, None, :]
    return jnp.concatenate([first_half * cos_rows - second_half * sin_rows, second_half * cos_rows + first_half * sin_rows], axis=-1)

def group_attention(queries, keys_in, values_in, seg_group):
    total_rows = queries.shape[0]
    block_rows = math.gcd(total_rows, 512)

    def one_block(pieces):
        query_block, seg_block = pieces
        scores = jnp.einsum('qhd,khd->hqk', query_block, keys_in, precision=HIGH) * HEAD_DIM ** (-0.5)
        scores = low_back(scores)
        allowed = (seg_block[:, None] == seg_group[None, :])[None]
        scores = jnp.where(allowed, scores, NEGATIVE)
        probs = low(jax.nn.softmax(scores, axis=-1))
        return jnp.einsum('hqk,khd->qhd', probs, values_in, precision=HIGH)
    blocks_in = (queries.reshape(total_rows // block_rows, block_rows, HEADS, HEAD_DIM), seg_group.reshape(total_rows // block_rows, block_rows))
    outputs = lax.map(jax.checkpoint(one_block), blocks_in)
    return outputs.reshape(total_rows, HEADS, HEAD_DIM)

def reference(tokens, cotangent, time_emb, seq_table, lengths, positions, norm1_gain, norm2_gain, ada_weight, ada_bias, qkv_weight, out_weight, fc1_weight, fc1_bias, fc2_weight, fc2_bias):
    seq_ends = jnp.cumsum(lengths, axis=1).astype(jnp.int32)
    indices = jnp.arange(GROUP_TOK, dtype=jnp.int32)
    seg_all = jax.vmap(lambda row_ends: segment_of(indices, row_ends))(seq_ends)
    seq_of = jnp.take_along_axis(seq_table.reshape(GROUPS, SLOTS), seg_all, axis=1).reshape(-1)
    cosine, sine = rotary_tables(positions)

    def attend_group(pieces):
        return group_attention(pieces[0], pieces[1], pieces[2], pieces[3])

    def layer(inputs, time_in, gain_one, gain_two, ada_w, ada_b, qkv_w, out_w, up_w, up_b, down_w, down_b):
        modulation = jnp.dot(time_in, ada_w, precision=HIGH) + ada_b
        per_token = modulation[seq_of]
        parts = jnp.split(per_token, 6, axis=1)
        first_in = low(modulated(inputs, gain_one, parts[1], parts[0]))
        qkv_all = low_back(jnp.dot(first_in, qkv_w, precision=HIGH))
        shaped = (-1, HEADS, HEAD_DIM)
        queries = low(rotate(qkv_all[:, :D].reshape(shaped), cosine, sine))
        keys_all = low(rotate(qkv_all[:, D:2 * D].reshape(shaped), cosine, sine))
        values_all = low(qkv_all[:, 2 * D:].reshape(shaped))
        grouped = (GROUPS, GROUP_TOK, HEADS, HEAD_DIM)
        attended = lax.map(jax.checkpoint(attend_group), (queries.reshape(grouped), keys_all.reshape(grouped), values_all.reshape(grouped), seg_all))
        attended = low(low_back(attended.reshape(-1, D)))
        branch_one = low_back(jnp.dot(attended, out_w, precision=HIGH))
        middle = inputs + parts[2] * branch_one
        second_in = low(modulated(middle, gain_two, parts[4], parts[3]))
        hidden_pre = low_back(jnp.dot(second_in, up_w, precision=HIGH) + up_b)
        hidden_act = low(jax.nn.gelu(hidden_pre, approximate=True))
        branch_two = low_back(jnp.dot(hidden_act, down_w, precision=HIGH) + down_b)
        return middle + parts[5] * branch_two
    floats = [array_in.astype(jnp.float32) for array_in in (tokens, time_emb, norm1_gain, norm2_gain, ada_weight, ada_bias, qkv_weight, out_weight, fc1_weight, fc1_bias, fc2_weight, fc2_bias)]
    layer_out, pullback = jax.vjp(layer, *floats)
    grads = pullback(cotangent.astype(jnp.float32))
    return (layer_out.astype(jnp.bfloat16), grads[0], grads[1], grads[2], grads[3], grads[4], grads[5], grads[6], grads[7], grads[8], grads[9], grads[10], grads[11])
```

```python
import functools
import math

import jax
import jax.numpy as jnp
import numpy as np
from jax import lax
from jax.experimental import pallas as pl
from jax.experimental.pallas import tpu as pltpu
from jax.sharding import PartitionSpec as P

HEADS = 12
HEAD_DIM = 64
EPSILON = 1e-05
FAR = -(2.0**100)
F32 = jnp.float32
BF16 = jnp.bfloat16
HIGH = lax.Precision.HIGHEST
VMEM_LIMIT = 56 * 2**20
TILE = 128
QUERY_ROWS = 256
KEY_ROWS = 256
BLOCK = 512


def params(grid_dims=1):
    return pltpu.CompilerParams(
        dimension_semantics=("arbitrary",) * grid_dims, vmem_limit_bytes=VMEM_LIMIT
    )


def dot(left, right, contract=((1,), (0,)), precision=None):
    return lax.dot_general(
        left, right, (contract, ((), ())), preferred_element_type=F32, precision=precision
    )


def thirds(values):
    high = values.astype(BF16)
    rest = values - high.astype(F32)
    middle = rest.astype(BF16)
    low = (rest - middle.astype(F32)).astype(BF16)
    return high, middle, low


def slot_of(rows, info):
    zero = jnp.zeros_like(rows)
    slot = zero
    for which in range(3):
        slot = slot + jnp.where(rows >= info[which], 1, zero)
    return slot


def scalar_slot(row, info):
    slot = jnp.int32(0)
    for which in range(3):
        slot = slot + jnp.where(row >= info[which], 1, 0)
    return slot


def key_range(first, last, info):
    low_slot = scalar_slot(first, info)
    high_slot = scalar_slot(last, info)
    start = jnp.where(
        low_slot == 0, 0, jnp.where(low_slot == 1, info[0], jnp.where(low_slot == 2, info[1], info[2]))
    )
    end = jnp.where(
        high_slot == 0,
        info[0],
        jnp.where(high_slot == 1, info[1], jnp.where(high_slot == 2, info[2], info[3])),
    )
    return start, end


def block_active(block, info, row_count):
    first = info[4]
    start, end = key_range(first, first + row_count - 1, info)
    return jnp.logical_and(block * BLOCK < end, (block + 1) * BLOCK > start)


def slot_picks(row_count, first_row, info):
    rows = first_row + lax.broadcasted_iota(jnp.int32, (row_count, 16), 0)
    lane = lax.broadcasted_iota(jnp.int32, (row_count, 16), 1)
    return jnp.where(
        jnp.logical_and(slot_of(rows, info) == lane % 4, lane < 12), 1.0, 0.0
    ).astype(BF16)


def pick_table(values):
    high, middle, low = thirds(values)
    zero = jnp.zeros_like(high[:4])
    return jnp.concatenate([high[:4], middle[:4], low[:4], zero], axis=0)


def normed(values):
    center = values - jnp.mean(values, axis=1, keepdims=True)
    spread = jnp.mean(center * center, axis=1, keepdims=True)
    inverse = lax.rsqrt(spread + EPSILON)
    return center * inverse, inverse


def rotary_constants():
    half = HEAD_DIM // 2
    inverse = 10000.0 ** (-(np.arange(half, dtype=np.float64) * 2.0) / HEAD_DIM)
    inverse = inverse.astype(np.float32).astype(np.float64)
    tables = []
    for count, step in ((128, 64), (64, 1)):
        angles = (np.arange(count, dtype=np.float64) * step)[:, None] * inverse[None, :]
        full = np.concatenate(
            [np.tile(np.cos(angles), (1, 4)), np.tile(np.sin(angles), (1, 4))], axis=1
        ).astype(np.float32)
        high = full.astype(jnp.bfloat16)
        low = (full - high.astype(np.float32)).astype(jnp.bfloat16)
        tables.append(np.concatenate([high, low], axis=1))
    return tables


def rotary(position_row, coarse_ref, fine_ref):
    count = position_row.shape[1]
    parts = []
    for picks, table in ((position_row // 64, coarse_ref), (position_row % 64, fine_ref)):
        depth = table.shape[0]
        onehot = (lax.broadcasted_iota(jnp.int32, (depth, count), 0) == picks).astype(F32)
        both = dot(onehot.astype(BF16), table[...], ((0,), (0,)))
        parts.append(both[:, :256] + both[:, 256:])
    coarse, fine = parts
    cosine = coarse[:, :128] * fine[:, :128] - coarse[:, 128:] * fine[:, 128:]
    sine = coarse[:, 128:] * fine[:, :128] + coarse[:, :128] * fine[:, 128:]
    lane = lax.broadcasted_iota(jnp.int32, (count, TILE), 1)
    return cosine, jnp.where(lane % 64 < 32, -sine, sine)


def swapped(values):
    lane = lax.broadcasted_iota(jnp.int32, values.shape, 1)
    return jnp.where(
        lane % 64 < 32, pltpu.roll(values, TILE - 32, 1), pltpu.roll(values, 32, 1)
    )


def turn(values, cosine, sine):
    return values * cosine + swapped(values) * sine


def turn_back(values, cosine, sine):
    return values * cosine - swapped(values) * sine


def project_kernel(
    info, x_ref, position_ref, cond_ref, ada_ref, bias_ref, gain_ref, weight_ref, coarse_ref,
    fine_ref, keys_ref, values_ref, first_ref, query_ref, table_ref,
):
    block = pl.program_id(0)
    width = x_ref.shape[1]
    row_count = query_ref.shape[0]

    @pl.when(block == 0)
    def _():
        modulation = dot(cond_ref[...], ada_ref[...]) + bias_ref[...]
        scale = (1.0 + modulation[:, width:]) * gain_ref[...]
        table_ref[:, :width] = pick_table(scale)
        table_ref[:, width:] = pick_table(modulation[:, :width])

    @pl.when(block_active(block, info, row_count))
    def _():
        x = x_ref[...].astype(F32)
        picks = slot_picks(BLOCK, block * BLOCK, info)
        mods = dot(picks, table_ref[...])
        xh, _ = normed(x)
        first = (xh * mods[:, :width] + mods[:, width:]).astype(BF16)
        first_ref[...] = first
        cosine, sine = rotary(position_ref[pl.ds(block, 1), :], coarse_ref, fine_ref)
        keys = dot(first, weight_ref[:, width : 2 * width])
        for tile in range(width // TILE):
            cut = slice(tile * TILE, (tile + 1) * TILE)
            keys_ref[:, cut] = turn(keys[:, cut], cosine, sine).astype(BF16)
        values_ref[...] = dot(first, weight_ref[:, 2 * width :]).astype(BF16)

        @pl.when(block * BLOCK == info[4])
        def _():
            queries = dot(first, weight_ref[:, :width])
            for tile in range(width // TILE):
                cut = slice(tile * TILE, (tile + 1) * TILE)
                turned = turn(queries[:, cut], cosine, sine).astype(BF16)
                query_ref[:, cut] = (turned.astype(F32) * HEAD_DIM**-0.5).astype(BF16)


def project(info, x_all, positions, cond, ada, bias, gain, weight, tables, row_count):
    total, width = x_all.shape
    rows = pl.BlockSpec((BLOCK, width), lambda i, *_: (i, 0))

    def whole(array):
        return pl.BlockSpec(array.shape, lambda i, *_: (0,) * array.ndim)

    shape = jax.ShapeDtypeStruct((total, width), BF16)
    return pl.pallas_call(
        project_kernel,
        grid_spec=pltpu.PrefetchScalarGridSpec(
            num_scalar_prefetch=1,
            grid=(total // BLOCK,),
            in_specs=[
                rows,
                whole(positions),
                whole(cond),
                pl.BlockSpec((ada.shape[0], 2 * width), lambda i, *_: (0, 0)),
                pl.BlockSpec((1, 2 * width), lambda i, *_: (0, 0)),
                whole(gain),
                whole(weight),
                whole(tables[0]),
                whole(tables[1]),
            ],
            out_specs=[
                rows,
                rows,
                rows,
                pl.BlockSpec((row_count, width), lambda i, *_: (0, 0)),
            ],
            scratch_shapes=[pltpu.VMEM((16, 2 * width), BF16)],
        ),
        out_shape=[shape, shape, shape, jax.ShapeDtypeStruct((row_count, width), BF16)],
        compiler_params=params(),
        name="project",
    )(info, x_all, positions, cond, ada, bias, gain, weight, *tables)


def fill_key_features(feature_ref, info):
    total = feature_ref.shape[0]

    @pl.loop(0, total // KEY_ROWS)
    def _(chunk):
        start = pl.multiple_of(chunk * KEY_ROWS, KEY_ROWS)
        rows = start + lax.broadcasted_iota(jnp.int32, (KEY_ROWS, TILE), 0)
        lane = lax.broadcasted_iota(jnp.int32, (KEY_ROWS, TILE), 1)
        slot = slot_of(rows, info)
        masked = jnp.where(slot == lane, 0.0, FAR)
        ones = jnp.where(lane < 8, 1.0, 0.0)
        feature_ref[pl.ds(start, KEY_ROWS), :] = jnp.where(lane < 4, masked, ones).astype(BF16)


def stacked_heads(flipped):
    sub = lax.broadcasted_iota(jnp.int32, flipped.shape, 0)
    zero = jnp.zeros_like(flipped)
    return jnp.concatenate(
        [jnp.where(sub < HEAD_DIM, flipped, zero), jnp.where(sub < HEAD_DIM, zero, flipped)],
        axis=1,
    )


def slot_rows(first, count, info):
    sub = lax.broadcasted_iota(jnp.int32, (TILE, 2 * count), 0)
    lane = lax.broadcasted_iota(jnp.int32, (TILE, 2 * count), 1)
    return jnp.where(slot_of(first + lane % count, info) == sub, 1.0, 0.0), sub


def attend_kernel(info, q_ref, k_ref, v_ref, out_ref, mass_ref, feature_ref, sum_ref):
    @pl.when(pl.program_id(0) == 0)
    def _():
        fill_key_features(feature_ref, info)

    row_count = q_ref.shape[0]
    wide = 2 * QUERY_ROWS
    for part in range(row_count // QUERY_ROWS):
        first = info[4] + part * QUERY_ROWS
        cut = pl.ds(part * QUERY_ROWS, QUERY_ROWS)
        flipped = q_ref[cut, :].astype(F32).T
        onehot, _ = slot_rows(first, QUERY_ROWS, info)
        queries = jnp.concatenate([stacked_heads(flipped), onehot], axis=0).astype(BF16)
        start, end = key_range(first, first + QUERY_ROWS - 1, info)
        sum_ref[...] = jnp.zeros_like(sum_ref)

        def step(chunk, carried):
            most, mass = carried
            rows = pl.ds(pl.multiple_of(chunk * KEY_ROWS, KEY_ROWS), KEY_ROWS)
            keys = jnp.concatenate([k_ref[rows, :], feature_ref[rows, :]], axis=1)
            scores = dot(keys, queries)
            new_most = jnp.maximum(most, jnp.max(scores, axis=0, keepdims=True))
            shrink = jnp.exp(most - new_most)
            weights = jnp.exp(scores - new_most)
            mass = mass * shrink + jnp.sum(weights, axis=0, keepdims=True)
            sum_ref[...] = sum_ref[...] * shrink + dot(
                v_ref[rows, :], weights.astype(BF16), ((0,), (0,))
            )
            return new_most, mass

        most, mass = lax.fori_loop(
            start // KEY_ROWS,
            (end + KEY_ROWS - 1) // KEY_ROWS,
            step,
            (jnp.full((1, wide), FAR * 2, F32), jnp.zeros((1, wide), F32)),
        )
        result = sum_ref[...] / mass
        joined = jnp.concatenate(
            [result[:HEAD_DIM, :QUERY_ROWS], result[HEAD_DIM:, QUERY_ROWS:]], axis=0
        )
        out_ref[cut, :] = joined.T
        mass_ref[0, pl.ds(part, 1), :] = most + jnp.log(mass)


def attend(info, queries, keys, values):
    row_count, width = queries.shape
    total = keys.shape[0]
    pairs = width // TILE
    parts = row_count // QUERY_ROWS
    narrow = pl.BlockSpec((row_count, TILE), lambda i, *_: (0, i))
    tall = pl.BlockSpec((total, TILE), lambda i, *_: (0, i))
    return pl.pallas_call(
        attend_kernel,
        grid_spec=pltpu.PrefetchScalarGridSpec(
            num_scalar_prefetch=1,
            grid=(pairs,),
            in_specs=[narrow, tall, tall],
            out_specs=[
                narrow,
                pl.BlockSpec((1, parts, 2 * QUERY_ROWS), lambda i, *_: (i, 0, 0)),
            ],
            scratch_shapes=[
                pltpu.VMEM((total, TILE), BF16),
                pltpu.VMEM((TILE, 2 * QUERY_ROWS), F32),
            ],
        ),
        out_shape=[
            jax.ShapeDtypeStruct((row_count, width), F32),
            jax.ShapeDtypeStruct((pairs, parts, 2 * QUERY_ROWS), F32),
        ],
        compiler_params=params(),
        name="attend",
    )(info, queries, keys, values)


def attend_back_kernel(
    info, q_ref, k_ref, v_ref, grad_ref, out_ref, mass_ref, dq_ref, dk_ref, dv_ref,
    feature_ref, dk_sum, dv_sum, dq_sum,
):
    @pl.when(pl.program_id(0) == 0)
    def _():
        fill_key_features(feature_ref, info)

    row_count = q_ref.shape[0]
    total = k_ref.shape[0]
    for block in range(total // BLOCK):

        @pl.when(block_active(block, info, row_count))
        def _():
            rows = pl.ds(block * BLOCK, BLOCK)
            dk_sum[rows, :] = jnp.zeros((BLOCK, TILE), F32)
            dv_sum[rows, :] = jnp.zeros((BLOCK, TILE), F32)

    for part in range(row_count // QUERY_ROWS):
        first = info[4] + part * QUERY_ROWS
        cut = pl.ds(part * QUERY_ROWS, QUERY_ROWS)
        q_rows = q_ref[cut, :].astype(F32)
        g_rows = grad_ref[cut, :].astype(F32)
        q_flip = q_rows.T
        g_flip = g_rows.T
        product = g_flip * out_ref[cut, :].T
        delta = jnp.concatenate(
            [
                jnp.sum(product[:HEAD_DIM], axis=0, keepdims=True),
                jnp.sum(product[HEAD_DIM:], axis=0, keepdims=True),
            ],
            axis=1,
        )
        onehot, sub = slot_rows(first, QUERY_ROWS, info)

        def with_parts(base, row):
            for place, piece in enumerate(thirds(-row)):
                base = jnp.where(sub == 4 + place, piece.astype(F32), base)
            return base

        queries = jnp.concatenate(
            [stacked_heads(q_flip), with_parts(onehot, mass_ref[0, pl.ds(part, 1), :])], axis=0
        ).astype(BF16)
        grads = jnp.concatenate(
            [stacked_heads(g_flip), with_parts(jnp.zeros_like(onehot), delta)], axis=0
        ).astype(BF16)
        lane = lax.broadcasted_iota(jnp.int32, (QUERY_ROWS, TILE), 1)

        def stacked(rows):
            zero = jnp.zeros_like(rows)
            return jnp.concatenate(
                [jnp.where(lane < HEAD_DIM, rows, zero), jnp.where(lane < HEAD_DIM, zero, rows)],
                axis=0,
            ).astype(BF16)

        q_stack = stacked(q_rows)
        g_stack = stacked(g_rows)
        start, end = key_range(first, first + QUERY_ROWS - 1, info)
        dq_sum[...] = jnp.zeros_like(dq_sum)

        def step(chunk, carried):
            rows = pl.ds(pl.multiple_of(chunk * KEY_ROWS, KEY_ROWS), KEY_ROWS)
            keys = k_ref[rows, :]
            features = feature_ref[rows, :]
            probs = jnp.exp(dot(jnp.concatenate([keys, features], axis=1), queries))
            change = dot(jnp.concatenate([v_ref[rows, :], features], axis=1), grads)
            grad_scores = (probs * change).astype(BF16)
            dv_sum[rows, :] += dot(probs.astype(BF16), g_stack)
            dk_sum[rows, :] += dot(grad_scores, q_stack)
            dq_sum[...] += dot(keys, grad_scores, ((0,), (0,)))
            return carried

        lax.fori_loop(start // KEY_ROWS, (end + KEY_ROWS - 1) // KEY_ROWS, step, 0)
        result = dq_sum[...]
        joined = jnp.concatenate(
            [result[:HEAD_DIM, :QUERY_ROWS], result[HEAD_DIM:, QUERY_ROWS:]], axis=0
        )
        dq_ref[cut, :] = joined.T * HEAD_DIM**-0.5

    for block in range(total // BLOCK):

        @pl.when(block_active(block, info, row_count))
        def _():
            rows = pl.ds(block * BLOCK, BLOCK)
            dk_ref[rows, :] = dk_sum[rows, :].astype(BF16)
            dv_ref[rows, :] = dv_sum[rows, :].astype(BF16)


def attend_back(info, queries, keys, values, grads, attended, mass):
    row_count, width = queries.shape
    total = keys.shape[0]
    pairs = width // TILE
    parts = row_count // QUERY_ROWS
    narrow = pl.BlockSpec((row_count, TILE), lambda i, *_: (0, i))
    tall = pl.BlockSpec((total, TILE), lambda i, *_: (0, i))
    return pl.pallas_call(
        attend_back_kernel,
        grid_spec=pltpu.PrefetchScalarGridSpec(
            num_scalar_prefetch=1,
            grid=(pairs,),
            in_specs=[
                narrow,
                tall,
                tall,
                narrow,
                narrow,
                pl.BlockSpec((1, parts, 2 * QUERY_ROWS), lambda i, *_: (i, 0, 0)),
            ],
            out_specs=[narrow, tall, tall],
            scratch_shapes=[
                pltpu.VMEM((total, TILE), BF16),
                pltpu.VMEM((total, TILE), F32),
                pltpu.VMEM((total, TILE), F32),
                pltpu.VMEM((TILE, 2 * QUERY_ROWS), F32),
            ],
        ),
        out_shape=[
            jax.ShapeDtypeStruct((row_count, width), F32),
            jax.ShapeDtypeStruct((total, width), BF16),
            jax.ShapeDtypeStruct((total, width), BF16),
        ],
        compiler_params=params(),
        name="attend_back",
    )(info, queries, keys, values, grads, attended, mass)


def slot_sums(first_row, info, values):
    count = values.shape[0]
    rows = first_row + lax.broadcasted_iota(jnp.int32, (8, count), 1)
    which = lax.broadcasted_iota(jnp.int32, (8, count), 0)
    picks = jnp.where(slot_of(rows, info) == which, 1.0, 0.0).astype(BF16)
    high, middle, low = thirds(values)
    return dot(picks, high) + dot(picks, middle) + dot(picks, low)


def mlp_kernel(
    info, x_ref, attended_ref, cot_ref, cond_ref, ada_ref, bias_ref, gain_ref, out_w_ref,
    fc1_ref, fc1_b_ref, fc2_ref, fc2_b_ref,
    layer_ref, g_fc1_ref, g_fc2_ref, g_fc1_b_ref, g_out_ref, g_att_ref, g_mid_ref, small_ref,
    slots_ref,
    mods_ref, second_ref, second_t_ref, grad2_ref, branch_ref, middle_ref, xh_ref, inverse_ref,
    sum2_ref, gsum_ref,
):
    step = pl.program_id(0)
    width = x_ref.shape[1]
    row_count = x_ref.shape[0]
    first_row = info[4]

    def mod(which):
        picks = slot_picks(row_count, first_row, info)
        return dot(picks, mods_ref[:, which * width : (which + 1) * width])

    @pl.when(step == 0)
    def _():
        mods = dot(cond_ref[...], ada_ref[:, 2 * width :]) + bias_ref[:, 2 * width :]
        mods_ref[:, : 4 * width] = pick_table(mods)
        mods_ref[:, 4 * width :] = pick_table(
            (1.0 + mods[:, 2 * width : 3 * width]) * gain_ref[...]
        )
        attended_low = attended_ref[...].astype(BF16)
        branch = dot(attended_low, out_w_ref[...])
        branch_ref[...] = branch
        middle = x_ref[...].astype(F32) + mod(0) * branch
        middle_ref[...] = middle
        xh, inverse = normed(middle)
        xh_ref[...] = xh
        inverse_ref[...] = jnp.broadcast_to(inverse, inverse_ref.shape)
        second = xh * mod(4) + mod(1)
        second_ref[...] = second.astype(BF16)
        second_t_ref[...] = second.T.astype(BF16)
        grad2 = (cot_ref[...].astype(F32) * mod(3)).astype(BF16)
        grad2_ref[...] = grad2
        small_ref[0:1, :] = jnp.sum(grad2.astype(F32), axis=0, keepdims=True)
        sum2_ref[...] = jnp.zeros_like(sum2_ref)
        gsum_ref[...] = jnp.zeros_like(gsum_ref)

    pre = dot(second_ref[...], fc1_ref[...]) + fc1_b_ref[...]
    root = math.sqrt(2.0 / math.pi)
    square = pre * pre
    bend = jnp.tanh(root * pre * (1.0 + 0.044715 * square))
    half = 0.5 * (1.0 + bend)
    act = (pre * half).astype(BF16)
    slope = half + 0.5 * pre * (1.0 - bend * bend) * (root * (1.0 + 0.134145 * square))
    sum2_ref[...] += dot(act, fc2_ref[...])
    grad_act = dot(grad2_ref[...], fc2_ref[...], ((1,), (1,)))
    grad_pre = (grad_act * slope).astype(BF16)
    g_fc1_b_ref[...] = jnp.sum(grad_pre.astype(F32), axis=0, keepdims=True)
    g_fc2_ref[...] = dot(act, grad2_ref[...], ((0,), (0,))).astype(BF16)
    g_fc1_ref[...] = dot(second_t_ref[...], grad_pre).astype(BF16)
    gsum_ref[...] += dot(grad_pre, fc1_ref[...], ((1,), (1,)))

    @pl.when(step == pl.num_programs(0) - 1)
    def _():
        branch2 = sum2_ref[...] + fc2_b_ref[...]
        layer_ref[...] = (middle_ref[...] + mod(3) * branch2).astype(BF16)
        upstream = cot_ref[...].astype(F32)
        slots_ref[:, 3 * width :] = slot_sums(first_row, info, upstream * branch2)
        grad = gsum_ref[...]
        xh = xh_ref[...]
        picks = slot_picks(row_count, first_row, info)
        slots_ref[:, width : 2 * width] = slot_sums(first_row, info, grad)
        moved = grad * xh
        slots_ref[:, 2 * width : 3 * width] = slot_sums(first_row, info, moved * gain_ref[...])
        small_ref[1:2, :] = jnp.sum(moved * (1.0 + mod(2)), axis=0, keepdims=True)
        h = grad * mod(4)
        inverse = inverse_ref[:, 0:1]
        g_mid = upstream + inverse * (
            h - jnp.mean(h, axis=1, keepdims=True) - xh * jnp.mean(h * xh, axis=1, keepdims=True)
        )
        g_mid_ref[...] = g_mid
        slots_ref[:, :width] = slot_sums(first_row, info, g_mid * branch_ref[...])
        g_branch = (g_mid * mod(0)).astype(BF16)
        g_out_ref[...] = dot(attended_ref[...].astype(BF16), g_branch, ((0,), (0,))).astype(BF16)
        g_att_ref[...] = dot(g_branch, out_w_ref[...], ((1,), (1,))).astype(BF16)


def mlp(info, x, attended, cot, cond, ada, bias, gain, out_w, fc1, fc1_b, fc2, fc2_b):
    row_count, width = x.shape
    hidden = fc1.shape[1]
    chunk = 512

    def whole(shape):
        return pl.BlockSpec(shape, lambda i, *_: (0,) * len(shape))

    columns = pl.BlockSpec((width, chunk), lambda i, *_: (0, i))
    lines = pl.BlockSpec((chunk, width), lambda i, *_: (i, 0))
    part = pl.BlockSpec((1, chunk), lambda i, *_: (0, i))
    rows = (row_count, width)
    return pl.pallas_call(
        mlp_kernel,
        grid_spec=pltpu.PrefetchScalarGridSpec(
            num_scalar_prefetch=1,
            grid=(hidden // chunk,),
            in_specs=[
                whole(rows), whole(rows), whole(rows), whole(cond.shape), whole(ada.shape),
                whole(bias.shape), whole(gain.shape), whole(out_w.shape), columns, part, lines,
                whole(fc2_b.shape),
            ],
            out_specs=[
                whole(rows), columns, lines, part, whole(out_w.shape), whole(rows), whole(rows),
                whole((8, width)), whole((8, 4 * width)),
            ],
            scratch_shapes=[
                pltpu.VMEM((16, 5 * width), BF16),
                pltpu.VMEM(rows, BF16),
                pltpu.VMEM((width, row_count), BF16),
                pltpu.VMEM(rows, BF16),
                pltpu.VMEM(rows, F32),
                pltpu.VMEM(rows, F32),
                pltpu.VMEM(rows, F32),
                pltpu.VMEM((row_count, TILE), F32),
                pltpu.VMEM(rows, F32),
                pltpu.VMEM(rows, F32),
            ],
        ),
        out_shape=[
            jax.ShapeDtypeStruct(rows, BF16),
            jax.ShapeDtypeStruct(fc1.shape, BF16),
            jax.ShapeDtypeStruct(fc2.shape, BF16),
            jax.ShapeDtypeStruct((1, hidden), F32),
            jax.ShapeDtypeStruct(out_w.shape, BF16),
            jax.ShapeDtypeStruct(rows, BF16),
            jax.ShapeDtypeStruct(rows, F32),
            jax.ShapeDtypeStruct((8, width), F32),
            jax.ShapeDtypeStruct((8, 4 * width), F32),
        ],
        compiler_params=params(),
        name="mlp",
    )(info, x, attended, cot, cond, ada, bias, gain, out_w, fc1, fc1_b, fc2, fc2_b)


def spread_kernel(
    info, first_ref, dk_ref, dv_ref, dq_ref, weight_ref, position_ref, coarse_ref, fine_ref,
    dx_ref, own_ref, dw_ref, sum_ref,
):
    block = pl.program_id(0)
    row_count, width = dq_ref.shape

    @pl.when(block == 0)
    def _():
        sum_ref[...] = jnp.zeros_like(sum_ref)

    @pl.when(jnp.logical_not(block_active(block, info, row_count)))
    def _():
        dx_ref[...] = jnp.zeros_like(dx_ref)

    @pl.when(block_active(block, info, row_count))
    def _():
        cosine, sine = rotary(position_ref[pl.ds(block, 1), :], coarse_ref, fine_ref)

        def back(ref):
            tiles = []
            for tile in range(width // TILE):
                cut = slice(tile * TILE, (tile + 1) * TILE)
                tiles.append(turn_back(ref[:, cut].astype(F32), cosine, sine).astype(BF16))
            return jnp.concatenate(tiles, axis=1)

        dk = back(dk_ref)
        dv = dv_ref[...]
        first = first_ref[...]
        total = dot(dk, weight_ref[:, width : 2 * width], ((1,), (1,))) + dot(
            dv, weight_ref[:, 2 * width :], ((1,), (1,))
        )
        sum_ref[:, width : 2 * width] += dot(first, dk, ((0,), (0,)))
        sum_ref[:, 2 * width :] += dot(first, dv, ((0,), (0,)))
        dx_ref[...] = total.astype(BF16)

        @pl.when(block * BLOCK == info[4])
        def _():
            dq = back(dq_ref)
            sum_ref[:, :width] += dot(first, dq, ((0,), (0,)))
            own = dot(dq, weight_ref[:, :width], ((1,), (1,)))
            dx_ref[...] = (total + own).astype(BF16)
            own_ref[...] = total + own

    @pl.when(block == pl.num_programs(0) - 1)
    def _():
        dw_ref[...] = sum_ref[...].astype(BF16)


def spread(info, first, dk, dv, dq, weight, positions, tables):
    row_count, width = dq.shape
    total = first.shape[0]
    rows = pl.BlockSpec((BLOCK, width), lambda i, *_: (i, 0))

    def whole(shape):
        return pl.BlockSpec(shape, lambda i, *_: (0,) * len(shape))

    return pl.pallas_call(
        spread_kernel,
        grid_spec=pltpu.PrefetchScalarGridSpec(
            num_scalar_prefetch=1,
            grid=(total // BLOCK,),
            in_specs=[
                rows, rows, rows, whole(dq.shape), whole(weight.shape), whole(positions.shape),
                whole(tables[0].shape), whole(tables[1].shape),
            ],
            out_specs=[rows, whole(dq.shape), whole(weight.shape)],
            scratch_shapes=[pltpu.VMEM(weight.shape, F32)],
        ),
        out_shape=[
            jax.ShapeDtypeStruct((total, width), BF16),
            jax.ShapeDtypeStruct(dq.shape, F32),
            jax.ShapeDtypeStruct(weight.shape, BF16),
        ],
        compiler_params=params(),
        name="spread",
    )(info, first, dk, dv, dq, weight, positions, *tables)


def finish_kernel(
    info, grad_ref, x_ref, g_mid_ref, cond_ref, ada_ref, bias_ref, gain_ref,
    tokens_ref, small_ref, slots_ref,
):
    width = x_ref.shape[1]
    first_row = info[4]
    mods = dot(cond_ref[...], ada_ref[...]) + bias_ref[...]
    scale = 1.0 + mods[:, width:]
    picks = slot_picks(x_ref.shape[0], first_row, info)
    grad = grad_ref[...].astype(F32)
    xh, inverse = normed(x_ref[...].astype(F32))
    slots_ref[:, :width] = slot_sums(first_row, info, grad)
    moved = grad * xh
    slots_ref[:, width:] = slot_sums(first_row, info, moved * gain_ref[...])
    small_ref[0:1, :] = jnp.sum(moved * dot(picks, pick_table(scale)), axis=0, keepdims=True)
    h = grad * dot(picks, pick_table(scale * gain_ref[...]))
    tokens_ref[...] = g_mid_ref[...] + inverse * (
        h - jnp.mean(h, axis=1, keepdims=True) - xh * jnp.mean(h * xh, axis=1, keepdims=True)
    )


def finish(info, grad, x, g_mid, cond, ada, bias, gain):
    row_count, width = x.shape

    def whole(shape):
        return pl.BlockSpec(shape, lambda i, *_: (0,) * len(shape))

    return pl.pallas_call(
        finish_kernel,
        grid_spec=pltpu.PrefetchScalarGridSpec(
            num_scalar_prefetch=1,
            grid=(1,),
            in_specs=[
                whole(grad.shape), whole(x.shape), whole(x.shape), whole(cond.shape),
                whole((ada.shape[0], 2 * width)), whole((1, 2 * width)), whole(gain.shape),
            ],
            out_specs=[whole(x.shape), whole((8, width)), whole((8, 2 * width))],
        ),
        out_shape=[
            jax.ShapeDtypeStruct(x.shape, F32),
            jax.ShapeDtypeStruct((8, width), F32),
            jax.ShapeDtypeStruct((8, 2 * width), F32),
        ],
        compiler_params=params(),
        name="finish",
    )(info, grad, x, g_mid, cond, ada, bias, gain)


def body(
    tokens, cotangent, time_emb, seq_table, lengths, positions, norm1_gain, norm2_gain,
    ada_weight, ada_bias, qkv_weight, out_weight, fc1_weight, fc1_bias, fc2_weight, fc2_bias,
):
    row_count, width = tokens.shape
    me = lax.axis_index("narrow")
    first_row = me * row_count
    slots = lengths.shape[1]
    below = np.tril(np.ones((slots, slots), np.int32))
    seq_ends = jnp.sum(jnp.asarray(below) * lengths[0][None, :], axis=1)
    info = jnp.concatenate(
        [seq_ends, first_row[None], jnp.zeros((3,), jnp.int32)]
    ).astype(jnp.int32)
    onehot_table = (
        seq_table[:, None] == jnp.arange(time_emb.shape[0], dtype=jnp.int32)[None, :]
    ).astype(BF16)
    cond = jnp.dot(onehot_table, time_emb, preferred_element_type=F32).astype(BF16)
    cond8 = jnp.concatenate([cond, jnp.zeros_like(cond)], axis=0)
    tables = tuple(jnp.asarray(t) for t in rotary_constants())

    def gather(shard):
        return lax.all_gather(shard, "narrow", axis=0, tiled=True)

    x_all = gather(tokens)
    position_all = gather(positions.reshape(1, row_count))
    ada = gather(ada_weight)
    qkv_w = gather(qkv_weight)
    out_w = gather(out_weight)
    fc1 = gather(fc1_weight)
    fc2 = gather(fc2_weight)
    vector = gather(jnp.concatenate([norm1_gain, norm2_gain, ada_bias, fc1_bias, fc2_bias])[None])
    cuts = np.cumsum([norm1_gain.size, norm2_gain.size, ada_bias.size, fc1_bias.size])
    gain1, gain2, bias, fc1_b, fc2_b = (
        piece.reshape(1, -1).astype(F32) for piece in jnp.split(vector, cuts, axis=1)
    )

    keys, values, first, queries = project(
        info, x_all, position_all, cond8, ada, bias, gain1, qkv_w, tables, row_count
    )
    attended, mass = attend(info, queries, keys, values)
    layer_out, g_fc1, g_fc2, g_fc1_b, g_out, g_att, g_mid, small2, slots2 = mlp(
        info, tokens, attended, cotangent, cond8, ada, bias, gain2, out_w, fc1, fc1_b, fc2, fc2_b
    )
    dq, dk, dv = attend_back(info, queries, keys, values, g_att, attended, mass)
    dx, own, g_qkv = spread(info, first, dk, dv, dq, qkv_w, position_all, tables)
    grad_first = lax.psum_scatter(dx, "narrow", scatter_dimension=0, tiled=True)
    grad_tokens, small1, slots1 = finish(
        info, grad_first, tokens, g_mid, cond8, ada, bias, gain1
    )
    grad_slot = jnp.concatenate([slots1[:slots], slots2[:slots]], axis=1)
    grad_ada_bias = jnp.sum(grad_slot, axis=0)
    grad_ada = jnp.einsum("sc,se->ce", cond.astype(F32), grad_slot, precision=HIGH)
    grad_cond = jnp.einsum("se,ce->sc", grad_slot, ada.astype(F32), precision=HIGH)
    grad_time = jnp.einsum("sn,sc->nc", onehot_table.astype(F32), grad_cond, precision=HIGH)
    partial = (
        grad_time, small1[0], small2[1], grad_ada, grad_ada_bias, g_qkv, g_out, g_fc1,
        g_fc1_b[0], g_fc2, small2[0],
    )
    shards = tuple(
        lax.psum_scatter(part.astype(BF16), "narrow", scatter_dimension=0, tiled=True)
        for part in partial
    )
    sums = jax.tree.map(lambda part: part.astype(F32), lax.psum(shards, "wide"))
    return (layer_out, grad_tokens) + tuple(sums)


def solution(mesh):
    both = P(("wide", "narrow"), None)
    row = P("narrow")
    table = P("narrow", None)
    return jax.shard_map(
        body,
        mesh=mesh,
        in_specs=(
            both, both, P(), P("wide"), P("wide", None), P(("wide", "narrow")), row, row,
            table, row, table, table, table, row, table, row,
        ),
        out_specs=(both, both, table, row, row, table, row, table, table, table, row, table, row),
        check_vma=False,
    )
```

```python
import functools
import math

import jax
import jax.numpy as jnp
import numpy as np
from jax import lax
from jax.experimental import pallas as pl
from jax.experimental.pallas import tpu as pltpu
from jax.sharding import PartitionSpec as P

HEADS = 12
HEAD_DIM = 64
EPSILON = 1e-05
FAR = -(2.0**100)
F32 = jnp.float32
BF16 = jnp.bfloat16
HIGH = lax.Precision.HIGHEST
VMEM_LIMIT = 56 * 2**20
TILE = 128
QUERY_ROWS = 256
KEY_ROWS = 256
BLOCK = 512


def params(grid_dims=1):
    return pltpu.CompilerParams(
        dimension_semantics=("arbitrary",) * grid_dims, vmem_limit_bytes=VMEM_LIMIT
    )


def dot(left, right, contract=((1,), (0,)), precision=None):
    return lax.dot_general(
        left, right, (contract, ((), ())), preferred_element_type=F32, precision=precision
    )


def thirds(values):
    high = values.astype(BF16)
    rest = values - high.astype(F32)
    middle = rest.astype(BF16)
    low = (rest - middle.astype(F32)).astype(BF16)
    return high, middle, low


def slot_of(rows, info):
    zero = jnp.zeros_like(rows)
    slot = zero
    for which in range(3):
        slot = slot + jnp.where(rows >= info[which], 1, zero)
    return slot


def scalar_slot(row, info):
    slot = jnp.int32(0)
    for which in range(3):
        slot = slot + jnp.where(row >= info[which], 1, 0)
    return slot


def key_range(first, last, info):
    low_slot = scalar_slot(first, info)
    high_slot = scalar_slot(last, info)
    start = jnp.where(
        low_slot == 0, 0, jnp.where(low_slot == 1, info[0], jnp.where(low_slot == 2, info[1], info[2]))
    )
    end = jnp.where(
        high_slot == 0,
        info[0],
        jnp.where(high_slot == 1, info[1], jnp.where(high_slot == 2, info[2], info[3])),
    )
    return start, end


def block_active(block, info, row_count):
    first = info[4]
    start, end = key_range(first, first + row_count - 1, info)
    return jnp.logical_and(block * BLOCK < end, (block + 1) * BLOCK > start)


def slot_picks(row_count, first_row, info):
    rows = first_row + lax.broadcasted_iota(jnp.int32, (row_count, 16), 0)
    lane = lax.broadcasted_iota(jnp.int32, (row_count, 16), 1)
    return jnp.where(
        jnp.logical_and(slot_of(rows, info) == lane % 4, lane < 12), 1.0, 0.0
    ).astype(BF16)


def pick_table(values):
    high, middle, low = thirds(values)
    zero = jnp.zeros_like(high[:4])
    return jnp.concatenate([high[:4], middle[:4], low[:4], zero], axis=0)


def normed(values):
    center = values - jnp.mean(values, axis=1, keepdims=True)
    spread = jnp.mean(center * center, axis=1, keepdims=True)
    inverse = lax.rsqrt(spread + EPSILON)
    return center * inverse, inverse


def rotary_constants():
    half = HEAD_DIM // 2
    inverse = 10000.0 ** (-(np.arange(half, dtype=np.float64) * 2.0) / HEAD_DIM)
    inverse = inverse.astype(np.float32).astype(np.float64)
    tables = []
    for count, step in ((128, 64), (64, 1)):
        angles = (np.arange(count, dtype=np.float64) * step)[:, None] * inverse[None, :]
        full = np.concatenate(
            [np.tile(np.cos(angles), (1, 4)), np.tile(np.sin(angles), (1, 4))], axis=1
        ).astype(np.float32)
        high = full.astype(jnp.bfloat16)
        low = (full - high.astype(np.float32)).astype(jnp.bfloat16)
        tables.append(np.concatenate([high, low], axis=1))
    return tables


def rotary(position_row, coarse_ref, fine_ref):
    count = position_row.shape[1]
    parts = []
    for picks, table in ((position_row // 64, coarse_ref), (position_row % 64, fine_ref)):
        depth = table.shape[0]
        onehot = (lax.broadcasted_iota(jnp.int32, (depth, count), 0) == picks).astype(F32)
        both = dot(onehot.astype(BF16), table[...], ((0,), (0,)))
        parts.append(both[:, :256] + both[:, 256:])
    coarse, fine = parts
    cosine = coarse[:, :128] * fine[:, :128] - coarse[:, 128:] * fine[:, 128:]
    sine = coarse[:, 128:] * fine[:, :128] + coarse[:, :128] * fine[:, 128:]
    lane = lax.broadcasted_iota(jnp.int32, (count, TILE), 1)
    return cosine, jnp.where(lane % 64 < 32, -sine, sine)


def swapped(values):
    lane = lax.broadcasted_iota(jnp.int32, values.shape, 1)
    return jnp.where(
        lane % 64 < 32, pltpu.roll(values, TILE - 32, 1), pltpu.roll(values, 32, 1)
    )


def turn(values, cosine, sine):
    return values * cosine + swapped(values) * sine


def turn_back(values, cosine, sine):
    return values * cosine - swapped(values) * sine


def project_kernel(
    info, x_ref, position_ref, cond_ref, ada_ref, bias_ref, gain_ref, weight_ref, coarse_ref,
    fine_ref, keys_ref, values_ref, first_ref, query_ref, table_ref,
):
    block = pl.program_id(0)
    width = x_ref.shape[1]
    row_count = query_ref.shape[0]

    @pl.when(block == 0)
    def _():
        modulation = dot(cond_ref[...], ada_ref[...]) + bias_ref[...]
        scale = (1.0 + modulation[:, width:]) * gain_ref[...]
        table_ref[:, :width] = pick_table(scale)
        table_ref[:, width:] = pick_table(modulation[:, :width])

    @pl.when(block_active(block, info, row_count))
    def _():
        x = x_ref[...].astype(F32)
        picks = slot_picks(BLOCK, block * BLOCK, info)
        mods = dot(picks, table_ref[...])
        xh, _ = normed(x)
        first = (xh * mods[:, :width] + mods[:, width:]).astype(BF16)
        first_ref[...] = first
        cosine, sine = rotary(position_ref[pl.ds(block, 1), :], coarse_ref, fine_ref)
        keys = dot(first, weight_ref[:, width : 2 * width])
        for tile in range(width // TILE):
            cut = slice(tile * TILE, (tile + 1) * TILE)
            keys_ref[:, cut] = turn(keys[:, cut], cosine, sine).astype(BF16)
        values_ref[...] = dot(first, weight_ref[:, 2 * width :]).astype(BF16)

        @pl.when(block * BLOCK == info[4])
        def _():
            queries = dot(first, weight_ref[:, :width])
            for tile in range(width // TILE):
                cut = slice(tile * TILE, (tile + 1) * TILE)
                turned = turn(queries[:, cut], cosine, sine).astype(BF16)
                query_ref[:, cut] = (turned.astype(F32) * HEAD_DIM**-0.5).astype(BF16)


def project(info, x_all, positions, cond, ada, bias, gain, weight, tables, row_count):
    total, width = x_all.shape
    rows = pl.BlockSpec((BLOCK, width), lambda i, *_: (i, 0))

    def whole(array):
        return pl.BlockSpec(array.shape, lambda i, *_: (0,) * array.ndim)

    shape = jax.ShapeDtypeStruct((total, width), BF16)
    return pl.pallas_call(
        project_kernel,
        grid_spec=pltpu.PrefetchScalarGridSpec(
            num_scalar_prefetch=1,
            grid=(total // BLOCK,),
            in_specs=[
                rows,
                whole(positions),
                whole(cond),
                pl.BlockSpec((ada.shape[0], 2 * width), lambda i, *_: (0, 0)),
                pl.BlockSpec((1, 2 * width), lambda i, *_: (0, 0)),
                whole(gain),
                whole(weight),
                whole(tables[0]),
                whole(tables[1]),
            ],
            out_specs=[
                rows,
                rows,
                rows,
                pl.BlockSpec((row_count, width), lambda i, *_: (0, 0)),
            ],
            scratch_shapes=[pltpu.VMEM((16, 2 * width), BF16)],
        ),
        out_shape=[shape, shape, shape, jax.ShapeDtypeStruct((row_count, width), BF16)],
        compiler_params=params(),
        name="project",
    )(info, x_all, positions, cond, ada, bias, gain, weight, *tables)


def fill_key_features(feature_ref, info):
    total = feature_ref.shape[0]

    @pl.loop(0, total // KEY_ROWS)
    def _(chunk):
        start = pl.multiple_of(chunk * KEY_ROWS, KEY_ROWS)
        rows = start + lax.broadcasted_iota(jnp.int32, (KEY_ROWS, TILE), 0)
        lane = lax.broadcasted_iota(jnp.int32, (KEY_ROWS, TILE), 1)
        slot = slot_of(rows, info)
        masked = jnp.where(slot == lane, 0.0, FAR)
        ones = jnp.where(lane < 8, 1.0, 0.0)
        feature_ref[pl.ds(start, KEY_ROWS), :] = jnp.where(lane < 4, masked, ones).astype(BF16)


def stacked_heads(flipped):
    sub = lax.broadcasted_iota(jnp.int32, flipped.shape, 0)
    zero = jnp.zeros_like(flipped)
    return jnp.concatenate(
        [jnp.where(sub < HEAD_DIM, flipped, zero), jnp.where(sub < HEAD_DIM, zero, flipped)],
        axis=1,
    )


def slot_rows(first, count, info):
    sub = lax.broadcasted_iota(jnp.int32, (TILE, 2 * count), 0)
    lane = lax.broadcasted_iota(jnp.int32, (TILE, 2 * count), 1)
    return jnp.where(slot_of(first + lane % count, info) == sub, 1.0, 0.0), sub


def attend_kernel(info, q_ref, k_ref, v_ref, out_ref, mass_ref, feature_ref, sum_ref):
    @pl.when(pl.program_id(0) == 0)
    def _():
        fill_key_features(feature_ref, info)

    row_count = q_ref.shape[0]
    wide = 2 * QUERY_ROWS
    for part in range(row_count // QUERY_ROWS):
        first = info[4] + part * QUERY_ROWS
        cut = pl.ds(part * QUERY_ROWS, QUERY_ROWS)
        flipped = q_ref[cut, :].astype(F32).T
        onehot, _ = slot_rows(first, QUERY_ROWS, info)
        queries = jnp.concatenate([stacked_heads(flipped), onehot], axis=0).astype(BF16)
        start, end = key_range(first, first + QUERY_ROWS - 1, info)
        sum_ref[...] = jnp.zeros_like(sum_ref)

        def step(chunk, carried):
            most, mass = carried
            rows = pl.ds(pl.multiple_of(chunk * KEY_ROWS, KEY_ROWS), KEY_ROWS)
            keys = jnp.concatenate([k_ref[rows, :], feature_ref[rows, :]], axis=1)
            scores = dot(keys, queries)
            new_most = jnp.maximum(most, jnp.max(scores, axis=0, keepdims=True))
            shrink = jnp.exp(most - new_most)
            weights = jnp.exp(scores - new_most)
            mass = mass * shrink + jnp.sum(weights, axis=0, keepdims=True)
            sum_ref[...] = sum_ref[...] * shrink + dot(
                v_ref[rows, :], weights.astype(BF16), ((0,), (0,))
            )
            return new_most, mass

        most, mass = lax.fori_loop(
            start // KEY_ROWS,
            (end + KEY_ROWS - 1) // KEY_ROWS,
            step,
            (jnp.full((1, wide), FAR * 2, F32), jnp.zeros((1, wide), F32)),
        )
        result = sum_ref[...] / mass
        joined = jnp.concatenate(
            [result[:HEAD_DIM, :QUERY_ROWS], result[HEAD_DIM:, QUERY_ROWS:]], axis=0
        )
        out_ref[cut, :] = joined.T
        mass_ref[0, pl.ds(part, 1), :] = most + jnp.log(mass)


def attend(info, queries, keys, values):
    row_count, width = queries.shape
    total = keys.shape[0]
    pairs = width // TILE
    parts = row_count // QUERY_ROWS
    narrow = pl.BlockSpec((row_count, TILE), lambda i, *_: (0, i))
    tall = pl.BlockSpec((total, TILE), lambda i, *_: (0, i))
    return pl.pallas_call(
        attend_kernel,
        grid_spec=pltpu.PrefetchScalarGridSpec(
            num_scalar_prefetch=1,
            grid=(pairs,),
            in_specs=[narrow, tall, tall],
            out_specs=[
                narrow,
                pl.BlockSpec((1, parts, 2 * QUERY_ROWS), lambda i, *_: (i, 0, 0)),
            ],
            scratch_shapes=[
                pltpu.VMEM((total, TILE), BF16),
                pltpu.VMEM((TILE, 2 * QUERY_ROWS), F32),
            ],
        ),
        out_shape=[
            jax.ShapeDtypeStruct((row_count, width), F32),
            jax.ShapeDtypeStruct((pairs, parts, 2 * QUERY_ROWS), F32),
        ],
        compiler_params=params(),
        name="attend",
    )(info, queries, keys, values)


def attend_back_kernel(
    info, q_ref, k_ref, v_ref, grad_ref, out_ref, mass_ref, dq_ref, dk_ref, dv_ref,
    feature_ref, dk_sum, dv_sum, dq_sum,
):
    @pl.when(pl.program_id(0) == 0)
    def _():
        fill_key_features(feature_ref, info)

    row_count = q_ref.shape[0]
    total = k_ref.shape[0]
    for block in range(total // BLOCK):

        @pl.when(block_active(block, info, row_count))
        def _():
            rows = pl.ds(block * BLOCK, BLOCK)
            dk_sum[rows, :] = jnp.zeros((BLOCK, TILE), F32)
            dv_sum[rows, :] = jnp.zeros((BLOCK, TILE), F32)

    for part in range(row_count // QUERY_ROWS):
        first = info[4] + part * QUERY_ROWS
        cut = pl.ds(part * QUERY_ROWS, QUERY_ROWS)
        q_rows = q_ref[cut, :].astype(F32)
        g_rows = grad_ref[cut, :].astype(F32)
        q_flip = q_rows.T
        g_flip = g_rows.T
        product = g_flip * out_ref[cut, :].T
        delta = jnp.concatenate(
            [
                jnp.sum(product[:HEAD_DIM], axis=0, keepdims=True),
                jnp.sum(product[HEAD_DIM:], axis=0, keepdims=True),
            ],
            axis=1,
        )
        onehot, sub = slot_rows(first, QUERY_ROWS, info)

        def with_parts(base, row):
            for place, piece in enumerate(thirds(-row)):
                base = jnp.where(sub == 4 + place, piece.astype(F32), base)
            return base

        queries = jnp.concatenate(
            [stacked_heads(q_flip), with_parts(onehot, mass_ref[0, pl.ds(part, 1), :])], axis=0
        ).astype(BF16)
        grads = jnp.concatenate(
            [stacked_heads(g_flip), with_parts(jnp.zeros_like(onehot), delta)], axis=0
        ).astype(BF16)
        lane = lax.broadcasted_iota(jnp.int32, (QUERY_ROWS, TILE), 1)

        def stacked(rows):
            zero = jnp.zeros_like(rows)
            return jnp.concatenate(
                [jnp.where(lane < HEAD_DIM, rows, zero), jnp.where(lane < HEAD_DIM, zero, rows)],
                axis=0,
            ).astype(BF16)

        q_stack = stacked(q_rows)
        g_stack = stacked(g_rows)
        start, end = key_range(first, first + QUERY_ROWS - 1, info)
        dq_sum[...] = jnp.zeros_like(dq_sum)

        def step(chunk, carried):
            rows = pl.ds(pl.multiple_of(chunk * KEY_ROWS, KEY_ROWS), KEY_ROWS)
            keys = k_ref[rows, :]
            features = feature_ref[rows, :]
            probs = jnp.exp(dot(jnp.concatenate([keys, features], axis=1), queries))
            change = dot(jnp.concatenate([v_ref[rows, :], features], axis=1), grads)
            grad_scores = (probs * change).astype(BF16)
            dv_sum[rows, :] += dot(probs.astype(BF16), g_stack)
            dk_sum[rows, :] += dot(grad_scores, q_stack)
            dq_sum[...] += dot(keys, grad_scores, ((0,), (0,)))
            return carried

        lax.fori_loop(start // KEY_ROWS, (end + KEY_ROWS - 1) // KEY_ROWS, step, 0)
        result = dq_sum[...]
        joined = jnp.concatenate(
            [result[:HEAD_DIM, :QUERY_ROWS], result[HEAD_DIM:, QUERY_ROWS:]], axis=0
        )
        dq_ref[cut, :] = joined.T * HEAD_DIM**-0.5

    for block in range(total // BLOCK):

        @pl.when(block_active(block, info, row_count))
        def _():
            rows = pl.ds(block * BLOCK, BLOCK)
            dk_ref[rows, :] = dk_sum[rows, :].astype(BF16)
            dv_ref[rows, :] = dv_sum[rows, :].astype(BF16)


def attend_back(info, queries, keys, values, grads, attended, mass):
    row_count, width = queries.shape
    total = keys.shape[0]
    pairs = width // TILE
    parts = row_count // QUERY_ROWS
    narrow = pl.BlockSpec((row_count, TILE), lambda i, *_: (0, i))
    tall = pl.BlockSpec((total, TILE), lambda i, *_: (0, i))
    return pl.pallas_call(
        attend_back_kernel,
        grid_spec=pltpu.PrefetchScalarGridSpec(
            num_scalar_prefetch=1,
            grid=(pairs,),
            in_specs=[
                narrow,
                tall,
                tall,
                narrow,
                narrow,
                pl.BlockSpec((1, parts, 2 * QUERY_ROWS), lambda i, *_: (i, 0, 0)),
            ],
            out_specs=[narrow, tall, tall],
            scratch_shapes=[
                pltpu.VMEM((total, TILE), BF16),
                pltpu.VMEM((total, TILE), F32),
                pltpu.VMEM((total, TILE), F32),
                pltpu.VMEM((TILE, 2 * QUERY_ROWS), F32),
            ],
        ),
        out_shape=[
            jax.ShapeDtypeStruct((row_count, width), F32),
            jax.ShapeDtypeStruct((total, width), BF16),
            jax.ShapeDtypeStruct((total, width), BF16),
        ],
        compiler_params=params(),
        name="attend_back",
    )(info, queries, keys, values, grads, attended, mass)


def slot_sums(first_row, info, values):
    count = values.shape[0]
    rows = first_row + lax.broadcasted_iota(jnp.int32, (8, count), 1)
    which = lax.broadcasted_iota(jnp.int32, (8, count), 0)
    picks = jnp.where(slot_of(rows, info) == which, 1.0, 0.0).astype(BF16)
    high, middle, low = thirds(values)
    return dot(picks, high) + dot(picks, middle) + dot(picks, low)


def mlp_kernel(
    info, x_ref, attended_ref, cot_ref, cond_ref, ada_ref, bias_ref, gain_ref, out_w_ref,
    fc1_ref, fc1_b_ref, fc2_ref, fc2_b_ref,
    layer_ref, g_fc1_ref, g_fc2_ref, g_fc1_b_ref, g_out_ref, g_att_ref, g_mid_ref, small_ref,
    slots_ref,
    mods_ref, second_ref, second_t_ref, grad2_ref, branch_ref, middle_ref, xh_ref, inverse_ref,
    sum2_ref, gsum_ref,
):
    step = pl.program_id(0)
    width = x_ref.shape[1]
    row_count = x_ref.shape[0]
    first_row = info[4]

    def mod(which):
        picks = slot_picks(row_count, first_row, info)
        return dot(picks, mods_ref[:, which * width : (which + 1) * width])

    @pl.when(step == 0)
    def _():
        mods = dot(cond_ref[...], ada_ref[:, 2 * width :]) + bias_ref[:, 2 * width :]
        mods_ref[:, : 4 * width] = pick_table(mods)
        mods_ref[:, 4 * width :] = pick_table(
            (1.0 + mods[:, 2 * width : 3 * width]) * gain_ref[...]
        )
        attended_low = attended_ref[...].astype(BF16)
        branch = dot(attended_low, out_w_ref[...])
        branch_ref[...] = branch
        middle = x_ref[...].astype(F32) + mod(0) * branch
        middle_ref[...] = middle
        xh, inverse = normed(middle)
        xh_ref[...] = xh
        inverse_ref[...] = jnp.broadcast_to(inverse, inverse_ref.shape)
        second = xh * mod(4) + mod(1)
        second_ref[...] = second.astype(BF16)
        second_t_ref[...] = second.T.astype(BF16)
        grad2 = (cot_ref[...].astype(F32) * mod(3)).astype(BF16)
        grad2_ref[...] = grad2
        small_ref[0:1, :] = jnp.sum(grad2.astype(F32), axis=0, keepdims=True)
        sum2_ref[...] = jnp.zeros_like(sum2_ref)
        gsum_ref[...] = jnp.zeros_like(gsum_ref)

    pre = dot(second_ref[...], fc1_ref[...]) + fc1_b_ref[...]
    root = math.sqrt(2.0 / math.pi)
    square = pre * pre
    bend = jnp.tanh(root * pre * (1.0 + 0.044715 * square))
    half = 0.5 * (1.0 + bend)
    act = (pre * half).astype(BF16)
    slope = half + 0.5 * pre * (1.0 - bend * bend) * (root * (1.0 + 0.134145 * square))
    sum2_ref[...] += dot(act, fc2_ref[...])
    grad_act = dot(grad2_ref[...], fc2_ref[...], ((1,), (1,)))
    grad_pre = (grad_act * slope).astype(BF16)
    g_fc1_b_ref[...] = jnp.sum(grad_pre.astype(F32), axis=0, keepdims=True)
    g_fc2_ref[...] = dot(act, grad2_ref[...], ((0,), (0,))).astype(BF16)
    g_fc1_ref[...] = dot(second_t_ref[...], grad_pre).astype(BF16)
    gsum_ref[...] += dot(grad_pre, fc1_ref[...], ((1,), (1,)))

    @pl.when(step == pl.num_programs(0) - 1)
    def _():
        branch2 = sum2_ref[...] + fc2_b_ref[...]
        layer_ref[...] = (middle_ref[...] + mod(3) * branch2).astype(BF16)
        upstream = cot_ref[...].astype(F32)
        slots_ref[:, 3 * width :] = slot_sums(first_row, info, upstream * branch2)
        grad = gsum_ref[...]
        xh = xh_ref[...]
        picks = slot_picks(row_count, first_row, info)
        slots_ref[:, width : 2 * width] = slot_sums(first_row, info, grad)
        moved = grad * xh
        slots_ref[:, 2 * width : 3 * width] = slot_sums(first_row, info, moved * gain_ref[...])
        small_ref[1:2, :] = jnp.sum(moved * (1.0 + mod(2)), axis=0, keepdims=True)
        h = grad * mod(4)
        inverse = inverse_ref[:, 0:1]
        g_mid = upstream + inverse * (
            h - jnp.mean(h, axis=1, keepdims=True) - xh * jnp.mean(h * xh, axis=1, keepdims=True)
        )
        g_mid_ref[...] = g_mid
        slots_ref[:, :width] = slot_sums(first_row, info, g_mid * branch_ref[...])
        g_branch = (g_mid * mod(0)).astype(BF16)
        g_out_ref[...] = dot(attended_ref[...].astype(BF16), g_branch, ((0,), (0,))).astype(BF16)
        g_att_ref[...] = dot(g_branch, out_w_ref[...], ((1,), (1,))).astype(BF16)


def mlp(info, x, attended, cot, cond, ada, bias, gain, out_w, fc1, fc1_b, fc2, fc2_b):
    row_count, width = x.shape
    hidden = fc1.shape[1]
    chunk = 512

    def whole(shape):
        return pl.BlockSpec(shape, lambda i, *_: (0,) * len(shape))

    columns = pl.BlockSpec((width, chunk), lambda i, *_: (0, i))
    lines = pl.BlockSpec((chunk, width), lambda i, *_: (i, 0))
    part = pl.BlockSpec((1, chunk), lambda i, *_: (0, i))
    rows = (row_count, width)
    return pl.pallas_call(
        mlp_kernel,
        grid_spec=pltpu.PrefetchScalarGridSpec(
            num_scalar_prefetch=1,
            grid=(hidden // chunk,),
            in_specs=[
                whole(rows), whole(rows), whole(rows), whole(cond.shape), whole(ada.shape),
                whole(bias.shape), whole(gain.shape), whole(out_w.shape), columns, part, lines,
                whole(fc2_b.shape),
            ],
            out_specs=[
                whole(rows), columns, lines, part, whole(out_w.shape), whole(rows), whole(rows),
                whole((8, width)), whole((8, 4 * width)),
            ],
            scratch_shapes=[
                pltpu.VMEM((16, 5 * width), BF16),
                pltpu.VMEM(rows, BF16),
                pltpu.VMEM((width, row_count), BF16),
                pltpu.VMEM(rows, BF16),
                pltpu.VMEM(rows, F32),
                pltpu.VMEM(rows, F32),
                pltpu.VMEM(rows, F32),
                pltpu.VMEM((row_count, TILE), F32),
                pltpu.VMEM(rows, F32),
                pltpu.VMEM(rows, F32),
            ],
        ),
        out_shape=[
            jax.ShapeDtypeStruct(rows, BF16),
            jax.ShapeDtypeStruct(fc1.shape, BF16),
            jax.ShapeDtypeStruct(fc2.shape, BF16),
            jax.ShapeDtypeStruct((1, hidden), F32),
            jax.ShapeDtypeStruct(out_w.shape, BF16),
            jax.ShapeDtypeStruct(rows, BF16),
            jax.ShapeDtypeStruct(rows, F32),
            jax.ShapeDtypeStruct((8, width), F32),
            jax.ShapeDtypeStruct((8, 4 * width), F32),
        ],
        compiler_params=params(),
        name="mlp",
    )(info, x, attended, cot, cond, ada, bias, gain, out_w, fc1, fc1_b, fc2, fc2_b)


def spread_kernel(
    info, first_ref, dk_ref, dv_ref, dq_ref, weight_ref, position_ref, coarse_ref, fine_ref,
    dx_ref, own_ref, dw_ref, sum_ref,
):
    block = pl.program_id(0)
    row_count, width = dq_ref.shape

    @pl.when(block == 0)
    def _():
        sum_ref[...] = jnp.zeros_like(sum_ref)

    @pl.when(jnp.logical_not(block_active(block, info, row_count)))
    def _():
        dx_ref[...] = jnp.zeros_like(dx_ref)

    @pl.when(block_active(block, info, row_count))
    def _():
        cosine, sine = rotary(position_ref[pl.ds(block, 1), :], coarse_ref, fine_ref)

        def back(ref):
            tiles = []
            for tile in range(width // TILE):
                cut = slice(tile * TILE, (tile + 1) * TILE)
                tiles.append(turn_back(ref[:, cut].astype(F32), cosine, sine).astype(BF16))
            return jnp.concatenate(tiles, axis=1)

        dk = back(dk_ref)
        dv = dv_ref[...]
        first = first_ref[...]
        total = dot(dk, weight_ref[:, width : 2 * width], ((1,), (1,))) + dot(
            dv, weight_ref[:, 2 * width :], ((1,), (1,))
        )
        sum_ref[:, width : 2 * width] += dot(first, dk, ((0,), (0,)))
        sum_ref[:, 2 * width :] += dot(first, dv, ((0,), (0,)))
        dx_ref[...] = total.astype(BF16)

        @pl.when(block * BLOCK == info[4])
        def _():
            dq = back(dq_ref)
            sum_ref[:, :width] += dot(first, dq, ((0,), (0,)))
            own = dot(dq, weight_ref[:, :width], ((1,), (1,)))
            dx_ref[...] = (total + own).astype(BF16)
            own_ref[...] = total + own

    @pl.when(block == pl.num_programs(0) - 1)
    def _():
        dw_ref[...] = sum_ref[...].astype(BF16)


def spread(info, first, dk, dv, dq, weight, positions, tables):
    row_count, width = dq.shape
    total = first.shape[0]
    rows = pl.BlockSpec((BLOCK, width), lambda i, *_: (i, 0))

    def whole(shape):
        return pl.BlockSpec(shape, lambda i, *_: (0,) * len(shape))

    return pl.pallas_call(
        spread_kernel,
        grid_spec=pltpu.PrefetchScalarGridSpec(
            num_scalar_prefetch=1,
            grid=(total // BLOCK,),
            in_specs=[
                rows, rows, rows, whole(dq.shape), whole(weight.shape), whole(positions.shape),
                whole(tables[0].shape), whole(tables[1].shape),
            ],
            out_specs=[rows, whole(dq.shape), whole(weight.shape)],
            scratch_shapes=[pltpu.VMEM(weight.shape, F32)],
        ),
        out_shape=[
            jax.ShapeDtypeStruct((total, width), BF16),
            jax.ShapeDtypeStruct(dq.shape, F32),
            jax.ShapeDtypeStruct(weight.shape, BF16),
        ],
        compiler_params=params(),
        name="spread",
    )(info, first, dk, dv, dq, weight, positions, *tables)


def finish_kernel(
    info, grad_ref, x_ref, g_mid_ref, cond_ref, ada_ref, bias_ref, gain_ref,
    tokens_ref, small_ref, slots_ref,
):
    width = x_ref.shape[1]
    first_row = info[4]
    mods = dot(cond_ref[...], ada_ref[...]) + bias_ref[...]
    scale = 1.0 + mods[:, width:]
    picks = slot_picks(x_ref.shape[0], first_row, info)
    grad = grad_ref[...].astype(F32)
    xh, inverse = normed(x_ref[...].astype(F32))
    slots_ref[:, :width] = slot_sums(first_row, info, grad)
    moved = grad * xh
    slots_ref[:, width:] = slot_sums(first_row, info, moved * gain_ref[...])
    small_ref[0:1, :] = jnp.sum(moved * dot(picks, pick_table(scale)), axis=0, keepdims=True)
    h = grad * dot(picks, pick_table(scale * gain_ref[...]))
    tokens_ref[...] = g_mid_ref[...] + inverse * (
        h - jnp.mean(h, axis=1, keepdims=True) - xh * jnp.mean(h * xh, axis=1, keepdims=True)
    )


def finish(info, grad, x, g_mid, cond, ada, bias, gain):
    row_count, width = x.shape

    def whole(shape):
        return pl.BlockSpec(shape, lambda i, *_: (0,) * len(shape))

    return pl.pallas_call(
        finish_kernel,
        grid_spec=pltpu.PrefetchScalarGridSpec(
            num_scalar_prefetch=1,
            grid=(1,),
            in_specs=[
                whole(grad.shape), whole(x.shape), whole(x.shape), whole(cond.shape),
                whole((ada.shape[0], 2 * width)), whole((1, 2 * width)), whole(gain.shape),
            ],
            out_specs=[whole(x.shape), whole((8, width)), whole((8, 2 * width))],
        ),
        out_shape=[
            jax.ShapeDtypeStruct(x.shape, F32),
            jax.ShapeDtypeStruct((8, width), F32),
            jax.ShapeDtypeStruct((8, 2 * width), F32),
        ],
        compiler_params=params(),
        name="finish",
    )(info, grad, x, g_mid, cond, ada, bias, gain)


MESH = pl.DeviceIdType.MESH


def piece_of(array, which):
    rows, columns = array
    if rows >= 192:
        quarter = rows // 4
        return which * quarter, quarter, 0, columns
    if rows % 32 == 0 and (columns // 2) % TILE == 0:
        return (which % 2) * (rows // 2), rows // 2, (which // 2) * (columns // 2), columns // 2
    return 0, rows, which * (columns // 4), columns // 4


class Place:
    def __init__(self):
        self.wide = lax.axis_index("wide")
        self.narrow = lax.axis_index("narrow")
        self.z = self.narrow // 2
        self.core = self.narrow % 2
        self.quarter = self.wide % 4
        self.bit1 = 1 + self.core
        self.bit2 = 2 - self.core
        self.near = self.z + 1 - 2 * (self.z % 2)
        low = self.z < 2
        self.order = (self.near, jnp.where(low, 2, 1), jnp.where(low, 3, 0))

    def flip(self, value, bit):
        return value + bit * (1 - 2 * ((value // bit) % 2))

    def partner(self, bit):
        return (self.flip(self.wide, bit), self.narrow)

    def sibling(self):
        return (self.wide, self.narrow + 1 - 2 * self.core)

    def column(self, narrow):
        return (self.wide, narrow)

    def up(self):
        return (self.wide, jnp.minimum(self.narrow + 2, 7))

    def down(self):
        return (self.wide, jnp.maximum(self.narrow - 2, 0))


def greet(place, size):
    barrier = pltpu.get_barrier_semaphore()
    for step in range(1, size):
        pl.semaphore_signal(
            barrier, inc=1, device_id=place.column((place.narrow + step) % size), device_id_type=MESH
        )
    for bit in (1, 2):
        pl.semaphore_signal(barrier, inc=1, device_id=place.partner(bit), device_id_type=MESH)
    pl.semaphore_wait(barrier, size + 1)


def gather_kernel(shapes, size, *refs):
    count = len(shapes)
    shard_refs = refs[:count]
    x_ref, position_ref, vector_ref = refs[count : count + 3]
    full_refs = refs[count + 3 : 2 * count + 3]
    x_all, position_all, vector_all = refs[2 * count + 3 : 2 * count + 6]
    (
        own_sems, own_send, own_recv, line_send, line_recv, turn_send, turn_recv, next_send,
        next_recv, back_send, back_recv, small_send, small_recv,
    ) = refs[2 * count + 6 :]
    place = Place()
    narrow, z, core = place.narrow, place.z, place.core
    greet(place, size)

    def remote(source, target, send, recv, device):
        return pltpu.make_async_remote_copy(
            src_ref=source, dst_ref=target, send_sem=send, recv_sem=recv, device_id=device,
            device_id_type=MESH,
        )

    def region(a, owner, which):
        rows, columns = shapes[a]
        first_row, row_count, first_column, column_count = piece_of(shapes[a], which)
        start = pl.multiple_of(owner * rows + first_row, 16)
        if isinstance(first_column, int):
            return full_refs[a].at[pl.ds(start, row_count), :]
        lanes = pl.ds(pl.multiple_of(first_column, TILE), column_count)
        return full_refs[a].at[pl.ds(start, row_count), lanes]

    def shard(a, owner):
        rows, _ = shapes[a]
        return full_refs[a].at[pl.ds(pl.multiple_of(owner * rows, 16), rows), :]

    def own_piece(a):
        first_row, row_count, first_column, column_count = piece_of(shapes[a], place.quarter)
        if isinstance(first_row, int) and first_row == 0:
            rows = slice(None)
        else:
            rows = pl.ds(pl.multiple_of(first_row, 16), row_count)
        if isinstance(first_column, int):
            return shard_refs[a].at[rows, :]
        return shard_refs[a].at[rows, pl.ds(pl.multiple_of(first_column, TILE), column_count)]

    block = x_ref.shape[0]

    def tokens_of(owner):
        return x_all.at[pl.ds(pl.multiple_of(owner * block, 16), block), :]

    owner_of = [zp * 2 + core for zp in place.order]
    smalls = []
    for step in range(1, size):
        device = place.column((narrow + step) % size)
        smalls.append(
            remote(vector_ref, vector_all.at[narrow], small_send.at[0, step], small_recv.at[0, step], device)
        )
        smalls.append(
            remote(position_ref, position_all.at[narrow], small_send.at[1, step], small_recv.at[1, step], device)
        )
    for copy in smalls:
        copy.start()
    local = [
        pltpu.make_async_copy(vector_ref, vector_all.at[narrow], own_sems.at[count + 1]),
        pltpu.make_async_copy(position_ref, position_all.at[narrow], own_sems.at[count + 2]),
        pltpu.make_async_copy(x_ref, tokens_of(narrow), own_sems.at[count]),
    ]
    for a in range(count):
        local.append(pltpu.make_async_copy(shard_refs[a], shard(a, narrow), own_sems.at[a]))
    for copy in local:
        copy.start()

    def line_copies(a, owner, source, target):
        return (
            remote(source, target, line_send.at[a, owner // 2, 0], line_recv.at[a, owner // 2], place.up()),
            remote(source, target, line_send.at[a, owner // 2, 1], line_recv.at[a, owner // 2], place.down()),
        )

    def line_pair(a, owner):
        if a == count:
            target = tokens_of(owner)
            source = target
        else:
            target = region(a, owner, place.quarter)
            source = target
        return line_copies(a, owner, source, target)

    def own_pair(a):
        if a == count:
            return line_copies(a, narrow, x_ref, tokens_of(narrow))
        return line_copies(a, narrow, own_piece(a), region(a, narrow, place.quarter))

    def own_to_sibling(a):
        if a == count:
            return remote(x_ref, tokens_of(narrow), own_send.at[a], own_recv.at[a], place.sibling())
        return remote(shard_refs[a], shard(a, narrow), own_send.at[a], own_recv.at[a], place.sibling())

    def start_own(a):
        up, down = own_pair(a)
        pl.when(z < 3)(up.start)
        pl.when(z > 0)(down.start)
        own_to_sibling(a).start()

    def forwards(a, index):
        zp = place.order[index]
        if a == count:
            near = jnp.logical_and(zp - z < 2, z - zp < 2)
            return (
                jnp.logical_and(jnp.logical_and(zp < z, z < 3), near),
                jnp.logical_and(jnp.logical_and(zp > z, z > 0), near),
            )
        return jnp.logical_and(zp < z, z < 3), jnp.logical_and(zp > z, z > 0)

    def arrives(index):
        zp = place.order[index]
        return jnp.logical_and(zp - z < 3, z - zp < 3)

    def quarters(bit_first):
        first = place.flip(place.quarter, place.bit1)
        return first, place.flip(place.quarter, place.bit2), place.flip(first, place.bit2)

    def turn_copy(a, index):
        target = region(a, owner_of[index], place.quarter)
        return remote(
            target, target, turn_send.at[a, index], turn_recv.at[a, index], place.partner(place.bit1)
        )

    def next_copy(a, index, which):
        quarter = place.quarter if which == 0 else place.flip(place.quarter, place.bit1)
        target = region(a, owner_of[index], quarter)
        return remote(
            target, target, next_send.at[a, index, which], next_recv.at[a, index, which],
            place.partner(place.bit2),
        )

    def back_copy(a, index):
        if a == count:
            target = tokens_of(owner_of[index])
        else:
            target = shard(a, owner_of[index])
        return remote(
            target, target, back_send.at[a, index], back_recv.at[a, index], place.sibling()
        )

    def on_line(a, index):
        up, down = line_pair(a, owner_of[index])

        def work():
            up.wait_recv()
            goes_up, goes_down = forwards(a, index)
            pl.when(goes_up)(up.start)
            pl.when(goes_down)(down.start)
            if a == count:
                back_copy(a, index).start()
            else:
                turn_copy(a, index).start()
                next_copy(a, index, 0).start()

        if a == count:
            pl.when(arrives(index))(work)
        else:
            work()

    sequence = [0, 1, count] + list(range(2, count))
    for a in sequence:
        start_own(a)
    for a in sequence:
        for index in range(3):
            on_line(a, index)
        if a != count:
            for index in range(3):
                turn_copy(a, index).wait_recv()
                next_copy(a, index, 1).start()
    for a in range(count):
        for index in range(3):
            next_copy(a, index, 0).wait_recv()
            next_copy(a, index, 1).wait_recv()
            back_copy(a, index).start()
    for a in range(count):
        for index in range(3):
            back_copy(a, index).wait_recv()
    for a in range(count + 1):
        own_to_sibling(a).wait()
        up, down = own_pair(a)
        pl.when(z < 3)(up.wait_send)
        pl.when(z > 0)(down.wait_send)
    for index in range(3):

        @pl.when(arrives(index))
        def _():
            back_copy(count, index).wait()
            goes_up, goes_down = forwards(count, index)
            up, down = line_pair(count, owner_of[index])
            pl.when(goes_up)(up.wait_send)
            pl.when(goes_down)(down.wait_send)

        for a in range(count):
            goes_up, goes_down = forwards(a, index)
            up, down = line_pair(a, owner_of[index])
            pl.when(goes_up)(up.wait_send)
            pl.when(goes_down)(down.wait_send)
            turn_copy(a, index).wait_send()
            next_copy(a, index, 0).wait_send()
            next_copy(a, index, 1).wait_send()
            back_copy(a, index).wait_send()
    for copy in local:
        copy.wait()
    for copy in smalls:
        copy.wait()


def gather_all(x, positions, vector, shards, size):
    count = len(shards)
    shapes = tuple(shard.shape for shard in shards)
    anywhere = pl.BlockSpec(memory_space=pl.ANY)
    dma = pltpu.SemaphoreType.DMA
    out_shape = [
        jax.ShapeDtypeStruct((size * shard.shape[0], shard.shape[1]), shard.dtype) for shard in shards
    ] + [
        jax.ShapeDtypeStruct((size * x.shape[0], x.shape[1]), x.dtype),
        jax.ShapeDtypeStruct((size, *positions.shape), positions.dtype),
        jax.ShapeDtypeStruct((size, *vector.shape), vector.dtype),
    ]
    return pl.pallas_call(
        functools.partial(gather_kernel, shapes, size),
        out_shape=out_shape,
        in_specs=[anywhere] * (count + 3),
        out_specs=[anywhere] * (count + 3),
        scratch_shapes=[
            dma((count + 3,)),
            dma((count + 1,)),
            dma((count + 1,)),
            dma((count + 1, 4, 2)),
            dma((count + 1, 4)),
            dma((count, 3)),
            dma((count, 3)),
            dma((count, 3, 2)),
            dma((count, 3, 2)),
            dma((count + 1, 3)),
            dma((count + 1, 3)),
            dma((2, size)),
            dma((2, size)),
        ],
        compiler_params=pltpu.CompilerParams(collective_id=1, has_side_effects=True),
        name="gather_all",
    )(*shards, x, positions, vector)


def body(
    tokens, cotangent, time_emb, seq_table, lengths, positions, norm1_gain, norm2_gain,
    ada_weight, ada_bias, qkv_weight, out_weight, fc1_weight, fc1_bias, fc2_weight, fc2_bias,
):
    row_count, width = tokens.shape
    me = lax.axis_index("narrow")
    first_row = me * row_count
    slots = lengths.shape[1]
    below = np.tril(np.ones((slots, slots), np.int32))
    seq_ends = jnp.sum(jnp.asarray(below) * lengths[0][None, :], axis=1)
    info = jnp.concatenate(
        [seq_ends, first_row[None], jnp.zeros((3,), jnp.int32)]
    ).astype(jnp.int32)
    onehot_table = (
        seq_table[:, None] == jnp.arange(time_emb.shape[0], dtype=jnp.int32)[None, :]
    ).astype(BF16)
    cond = jnp.dot(onehot_table, time_emb, preferred_element_type=F32).astype(BF16)
    cond8 = jnp.concatenate([cond, jnp.zeros_like(cond)], axis=0)
    tables = tuple(jnp.asarray(t) for t in rotary_constants())

    pieces = (norm1_gain, norm2_gain, ada_bias, fc1_bias, fc2_bias)
    cuts = np.cumsum([piece.size for piece in pieces])
    room = -cuts[-1] % (16 * TILE)
    vector = jnp.concatenate([*pieces, jnp.zeros((room,), BF16)]).reshape(16, TILE)
    ada, qkv_w, out_w, fc1, fc2, x_all, position_all, vectors = gather_all(
        tokens, positions.reshape(-1, TILE), vector,
        (ada_weight, qkv_weight, out_weight, fc1_weight, fc2_weight), lax.axis_size("narrow"),
    )
    vectors = vectors.reshape(vectors.shape[0], -1)
    position_all = position_all.reshape(position_all.shape[0], -1)
    gain1, gain2, bias, fc1_b, fc2_b = (
        piece.reshape(1, -1).astype(F32) for piece in jnp.split(vectors[:, : cuts[-1]], cuts[:-1], axis=1)
    )

    keys, values, first, queries = project(
        info, x_all, position_all, cond8, ada, bias, gain1, qkv_w, tables, row_count
    )
    attended, mass = attend(info, queries, keys, values)
    layer_out, g_fc1, g_fc2, g_fc1_b, g_out, g_att, g_mid, small2, slots2 = mlp(
        info, tokens, attended, cotangent, cond8, ada, bias, gain2, out_w, fc1, fc1_b, fc2, fc2_b
    )
    dq, dk, dv = attend_back(info, queries, keys, values, g_att, attended, mass)
    dx, own, g_qkv = spread(info, first, dk, dv, dq, qkv_w, position_all, tables)
    grad_first = lax.psum_scatter(dx, "narrow", scatter_dimension=0, tiled=True)
    grad_tokens, small1, slots1 = finish(
        info, grad_first, tokens, g_mid, cond8, ada, bias, gain1
    )
    grad_slot = jnp.concatenate([slots1[:slots], slots2[:slots]], axis=1)
    grad_ada_bias = jnp.sum(grad_slot, axis=0)
    grad_ada = jnp.einsum("sc,se->ce", cond.astype(F32), grad_slot, precision=HIGH)
    grad_cond = jnp.einsum("se,ce->sc", grad_slot, ada.astype(F32), precision=HIGH)
    grad_time = jnp.einsum("sn,sc->nc", onehot_table.astype(F32), grad_cond, precision=HIGH)
    partial = (
        grad_time, small1[0], small2[1], grad_ada, grad_ada_bias, g_qkv, g_out, g_fc1,
        g_fc1_b[0], g_fc2, small2[0],
    )
    shards = tuple(
        lax.psum_scatter(part.astype(BF16), "narrow", scatter_dimension=0, tiled=True)
        for part in partial
    )
    sums = jax.tree.map(lambda part: part.astype(F32), lax.psum(shards, "wide"))
    return (layer_out, grad_tokens) + tuple(sums)


def solution(mesh):
    both = P(("wide", "narrow"), None)
    row = P("narrow")
    table = P("narrow", None)
    return jax.shard_map(
        body,
        mesh=mesh,
        in_specs=(
            both, both, P(), P("wide"), P("wide", None), P(("wide", "narrow")), row, row,
            table, row, table, table, table, row, table, row,
        ),
        out_specs=(both, both, table, row, row, table, row, table, table, table, row, table, row),
        check_vma=False,
    )
```

```python
import functools
import math

import jax
import jax.numpy as jnp
import numpy as np
from jax import lax
from jax.experimental import pallas as pl
from jax.experimental.pallas import tpu as pltpu
from jax.sharding import PartitionSpec as P

HEADS = 12
HEAD_DIM = 64
EPSILON = 1e-05
FAR = -(2.0**100)
SAFE = 64.0
LIFT = 20.0
F32 = jnp.float32
BF16 = jnp.bfloat16
HIGH = lax.Precision.HIGHEST
VMEM_LIMIT = 56 * 2**20
REDUCE_VMEM = 63 * 2**20
TILE = 128
QUERY_ROWS = 256
KEY_ROWS = 256
BLOCK = 512
CHUNK = 768


def params(grid_dims=1):
    return pltpu.CompilerParams(
        dimension_semantics=("arbitrary",) * grid_dims, vmem_limit_bytes=VMEM_LIMIT
    )


def dot(left, right, contract=((1,), (0,)), precision=None):
    return lax.dot_general(
        left, right, (contract, ((), ())), preferred_element_type=F32, precision=precision
    )


def thirds(values):
    high = values.astype(BF16)
    rest = values - high.astype(F32)
    middle = rest.astype(BF16)
    low = (rest - middle.astype(F32)).astype(BF16)
    return high, middle, low


def slot_of(rows, info):
    zero = jnp.zeros_like(rows)
    slot = zero
    for which in range(3):
        slot = slot + jnp.where(rows >= info[which], 1, zero)
    return slot


def scalar_slot(row, info):
    slot = jnp.int32(0)
    for which in range(3):
        slot = slot + jnp.where(row >= info[which], 1, 0)
    return slot


def key_range(first, last, info):
    low_slot = scalar_slot(first, info)
    high_slot = scalar_slot(last, info)
    start = jnp.where(
        low_slot == 0, 0, jnp.where(low_slot == 1, info[0], jnp.where(low_slot == 2, info[1], info[2]))
    )
    end = jnp.where(
        high_slot == 0,
        info[0],
        jnp.where(high_slot == 1, info[1], jnp.where(high_slot == 2, info[2], info[3])),
    )
    return start, end


def active_range(info):
    start, end = key_range(info[4], info[4] + BLOCK - 1, info)
    return start // BLOCK, (end - 1) // BLOCK


def block_active(block, info):
    low, high = active_range(info)
    return jnp.logical_and(block >= low, block <= high)


def active_rows(block, info):
    low, high = active_range(info)
    return jnp.clip(block, low, high), 0


def slot_picks(row_count, first_row, info):
    rows = first_row + lax.broadcasted_iota(jnp.int32, (row_count, 16), 0)
    lane = lax.broadcasted_iota(jnp.int32, (row_count, 16), 1)
    return jnp.where(
        jnp.logical_and(slot_of(rows, info) == lane % 4, lane < 12), 1.0, 0.0
    ).astype(BF16)


def pick_table(values):
    high, middle, low = thirds(values)
    zero = jnp.zeros_like(high[:4])
    return jnp.concatenate([high[:4], middle[:4], low[:4], zero], axis=0)


def normed(values):
    center = values - jnp.mean(values, axis=1, keepdims=True)
    spread = jnp.mean(center * center, axis=1, keepdims=True)
    inverse = lax.rsqrt(spread + EPSILON)
    return center * inverse, inverse


def rotary_constants():
    half = HEAD_DIM // 2
    inverse = 10000.0 ** (-(np.arange(half, dtype=np.float64) * 2.0) / HEAD_DIM)
    inverse = inverse.astype(np.float32).astype(np.float64)
    tables = []
    for count, step in ((128, 64), (64, 1)):
        angles = (np.arange(count, dtype=np.float64) * step)[:, None] * inverse[None, :]
        full = np.concatenate(
            [np.tile(np.cos(angles), (1, 4)), np.tile(np.sin(angles), (1, 4))], axis=1
        ).astype(np.float32)
        high = full.astype(jnp.bfloat16)
        low = (full - high.astype(np.float32)).astype(jnp.bfloat16)
        tables.append(np.concatenate([high, low], axis=1))
    return tables


def rotary(positions, coarse_ref, fine_ref):
    count = positions.size
    parts = []
    for picks, table in ((positions // 64, coarse_ref), (positions % 64, fine_ref)):
        depth = table.shape[0]
        sub = lax.broadcasted_iota(jnp.int32, (depth, TILE), 0)
        onehot = jnp.concatenate(
            [(sub == picks[at : at + 1, :]).astype(F32) for at in range(positions.shape[0])], axis=1
        )
        both = dot(onehot.astype(BF16), table[...], ((0,), (0,)))
        parts.append(both[:, :256] + both[:, 256:])
    coarse, fine = parts
    cosine = coarse[:, :128] * fine[:, :128] - coarse[:, 128:] * fine[:, 128:]
    sine = coarse[:, 128:] * fine[:, :128] + coarse[:, :128] * fine[:, 128:]
    lane = lax.broadcasted_iota(jnp.int32, (count, TILE), 1)
    return cosine, jnp.where(lane % 64 < 32, -sine, sine)


def swapped(values):
    lane = lax.broadcasted_iota(jnp.int32, values.shape, 1)
    return jnp.where(
        lane % 64 < 32, pltpu.roll(values, TILE - 32, 1), pltpu.roll(values, 32, 1)
    )


def turn(values, cosine, sine):
    return values * cosine + swapped(values) * sine


def turn_back(values, cosine, sine):
    return values * cosine - swapped(values) * sine


def packed(pieces):
    starts = np.cumsum([0] + [-(-piece.size // TILE) * TILE for piece in pieces])
    whole = -(-starts[-1] // (16 * TILE)) * 16 * TILE
    rows = [
        jnp.pad(piece, (start, whole - start - piece.size)) for piece, start in zip(pieces, starts)
    ]
    return functools.reduce(jnp.add, rows).reshape(-1, TILE)


def joined(vector_ref, row, size):
    devices = vector_ref.shape[0]
    rows = -(-size // TILE)
    room = -(-(devices - 1) * size // TILE) + rows
    total = jnp.zeros((8, room * TILE), F32)
    for device in range(devices):
        block = vector_ref[device].astype(F32)
        lanes = [block[row + at : row + at + 1, :] for at in range(rows)]
        line = jnp.concatenate(lanes, axis=1)
        line = jnp.concatenate([line, jnp.zeros((1, (room - rows) * TILE), F32)], axis=1)
        line = jnp.broadcast_to(line, (8, room * TILE))
        total = total + (pltpu.roll(line, device * size, 1) if device else line)
    return total[:1, : devices * size]


def project_kernel(
    sizes, info, x_ref, position_ref, cond_ref, ada_ref, vector_ref, weight_ref, coarse_ref,
    fine_ref, keys_ref, values_ref, first_ref, query_ref, norm_ref, mods_ref, gain_ref, gain2_ref,
    bias_ref, fc1_b_ref, fc2_b_ref, table_ref,
):
    block = pl.program_id(0)
    width = x_ref.shape[1]
    row_count = query_ref.shape[0]

    @pl.when(block == 0)
    def _():
        row = 0
        for out_ref, size in zip((gain_ref, gain2_ref, bias_ref, fc1_b_ref, fc2_b_ref), sizes):
            out_ref[...] = joined(vector_ref, row, size)
            row += -(-size // TILE)
        modulation = dot(cond_ref[...], ada_ref[...]) + bias_ref[:, : 2 * width]
        mods_ref[...] = modulation
        scale = (1.0 + modulation[:, width:]) * gain_ref[...]
        table_ref[:, :width] = pick_table(scale)
        table_ref[:, width:] = pick_table(modulation[:, :width])
        norm_ref[...] = jnp.zeros_like(norm_ref)

    def most_square(values):
        row = lax.broadcasted_iota(jnp.int32, (width, TILE), 0)
        lane = lax.broadcasted_iota(jnp.int32, (width, TILE), 1)
        heads = jnp.where(row // HEAD_DIM == lane, 1.0, 0.0).astype(BF16)
        return jnp.max(dot((values * values).astype(BF16), heads), axis=0, keepdims=True)

    @pl.when(jnp.logical_not(block_active(block, info)))
    def _():
        first_ref[...] = jnp.zeros_like(first_ref)

    @pl.when(block_active(block, info))
    def _():
        x = x_ref[...].astype(F32)
        picks = slot_picks(BLOCK, block * BLOCK, info)
        mods = dot(picks, table_ref[...])
        xh, _ = normed(x)
        first = (xh * mods[:, :width] + mods[:, width:]).astype(BF16)
        first_ref[...] = first
        cosine, sine = rotary(position_ref[block], coarse_ref, fine_ref)
        keys = dot(first, weight_ref[:, width : 2 * width])
        norm_ref[0:1, :] = jnp.maximum(norm_ref[0:1, :], most_square(keys) * 1.02)
        for tile in range(width // TILE):
            cut = slice(tile * TILE, (tile + 1) * TILE)
            keys_ref[:, cut] = turn(keys[:, cut], cosine, sine).astype(BF16)
        values_ref[...] = dot(first, weight_ref[:, 2 * width :]).astype(BF16)

        @pl.when(block * BLOCK == info[4])
        def _():
            queries = dot(first, weight_ref[:, :width])
            for tile in range(width // TILE):
                cut = slice(tile * TILE, (tile + 1) * TILE)
                turned = turn(queries[:, cut], cosine, sine).astype(BF16)
                query_ref[:, cut] = (turned.astype(F32) * HEAD_DIM**-0.5).astype(BF16)


def project(info, x_all, positions, cond, ada, vectors, sizes, weight, tables, row_count):
    total, width = x_all.shape
    rows = pl.BlockSpec((BLOCK, width), active_rows)

    def whole(array):
        return pl.BlockSpec(array.shape, lambda i, *_: (0,) * array.ndim)

    shape = jax.ShapeDtypeStruct((total, width), BF16)
    lengths = [vectors.shape[0] * size for size in sizes]
    return pl.pallas_call(
        functools.partial(project_kernel, sizes),
        grid_spec=pltpu.PrefetchScalarGridSpec(
            num_scalar_prefetch=1,
            grid=(total // BLOCK,),
            in_specs=[
                rows,
                whole(positions),
                whole(cond),
                pl.BlockSpec((ada.shape[0], 2 * width), lambda i, *_: (0, 0)),
                whole(vectors),
                whole(weight),
                whole(tables[0]),
                whole(tables[1]),
            ],
            out_specs=[
                rows,
                rows,
                pl.BlockSpec((BLOCK, width), lambda i, *_: (i, 0)),
                pl.BlockSpec((row_count, width), lambda i, *_: (0, 0)),
                pl.BlockSpec((8, TILE), lambda i, *_: (0, 0)),
                pl.BlockSpec((8, 2 * width), lambda i, *_: (0, 0)),
            ]
            + [pl.BlockSpec((1, count), lambda i, *_: (0, 0)) for count in lengths],
            scratch_shapes=[pltpu.VMEM((16, 2 * width), BF16)],
        ),
        out_shape=[
            shape, shape, shape, jax.ShapeDtypeStruct((row_count, width), BF16),
            jax.ShapeDtypeStruct((8, TILE), F32),
            jax.ShapeDtypeStruct((8, 2 * width), F32),
        ]
        + [jax.ShapeDtypeStruct((1, count), F32) for count in lengths],
        compiler_params=params(),
        name="project",
    )(info, x_all, positions, cond, ada, vectors, weight, *tables)


def fill_key_features(feature_ref, info):
    total = feature_ref.shape[0]

    @pl.loop(0, total // KEY_ROWS)
    def _(chunk):
        start = pl.multiple_of(chunk * KEY_ROWS, KEY_ROWS)
        rows = start + lax.broadcasted_iota(jnp.int32, (KEY_ROWS, TILE), 0)
        lane = lax.broadcasted_iota(jnp.int32, (KEY_ROWS, TILE), 1)
        slot = slot_of(rows, info)
        masked = jnp.where(slot == lane, 0.0, FAR)
        ones = jnp.where(lane < 8, 1.0, 0.0)
        feature_ref[pl.ds(start, KEY_ROWS), :] = jnp.where(lane < 4, masked, ones).astype(BF16)


def stacked_heads(flipped):
    sub = lax.broadcasted_iota(jnp.int32, flipped.shape, 0)
    zero = jnp.zeros_like(flipped)
    return jnp.concatenate(
        [jnp.where(sub < HEAD_DIM, flipped, zero), jnp.where(sub < HEAD_DIM, zero, flipped)],
        axis=1,
    )


def slot_rows(first, count, info):
    sub = lax.broadcasted_iota(jnp.int32, (TILE, 2 * count), 0)
    lane = lax.broadcasted_iota(jnp.int32, (TILE, 2 * count), 1)
    return jnp.where(slot_of(first + lane % count, info) == sub, 1.0, 0.0), sub


def spans(low, count, step, carried, most):
    span = most
    while span:
        times = count // span
        carried = lax.fori_loop(0, times, functools.partial(step, span, low), carried)
        low = low + times * span
        count = count - times * span
        span //= 2
    return carried


def chunk_rows(chunk):
    return pl.ds(pl.multiple_of(chunk * KEY_ROWS, KEY_ROWS), KEY_ROWS)


def with_parts(base, sub, row):
    for place, piece in enumerate(thirds(row)):
        base = jnp.where(sub == 4 + place, piece.astype(F32), base)
    return base


def attend_kernel(
    info, q_ref, k_ref, v_ref, norm_ref, out_ref, mass_ref, feature_ref, sum_ref, row_ref
):
    pair = pl.program_id(0)

    @pl.when(pair == 0)
    def _():
        fill_key_features(feature_ref, info)

    row_count = q_ref.shape[0]
    wide = 2 * QUERY_ROWS
    head = lax.broadcasted_iota(jnp.int32, (1, TILE), 1)
    longest = [
        jnp.sqrt(jnp.max(jnp.where(head == 2 * pair + which, norm_ref[0:1, :], 0.0), axis=1, keepdims=True))
        for which in range(2)
    ]
    for part in range(row_count // QUERY_ROWS):
        first = info[4] + part * QUERY_ROWS
        cut = pl.ds(part * QUERY_ROWS, QUERY_ROWS)
        flipped = q_ref[cut, :].astype(F32).T
        onehot, sub = slot_rows(first, QUERY_ROWS, info)
        stack = stacked_heads(flipped)
        start, end = key_range(first, first + QUERY_ROWS - 1, info)
        low = start // KEY_ROWS
        count = (end + KEY_ROWS - 1) // KEY_ROWS - low
        sum_ref[...] = jnp.zeros_like(sum_ref)

        def scores_of(rows, queries):
            return dot(jnp.concatenate([k_ref[rows, :], feature_ref[rows, :]], axis=1), queries)

        own_rows = chunk_rows(first // KEY_ROWS)
        near = jnp.max(
            scores_of(own_rows, jnp.concatenate([stack, onehot], axis=0).astype(BF16)),
            axis=0, keepdims=True,
        )
        square = flipped * flipped
        bound = jnp.concatenate(
            [
                jnp.sqrt(jnp.sum(square[:HEAD_DIM], axis=0, keepdims=True)) * longest[0],
                jnp.sqrt(jnp.sum(square[HEAD_DIM:], axis=0, keepdims=True)) * longest[1],
            ],
            axis=1,
        )
        shift = near + LIFT
        narrow_range = jnp.max(bound - shift) < SAFE
        queries = jnp.concatenate([stack, with_parts(onehot, sub, -shift)], axis=0).astype(BF16)

        @pl.when(narrow_range)
        def _():
            def step(span, base, index, mass):
                weights, values = [], []
                for inner in range(span):
                    rows = chunk_rows(base + index * span + inner)
                    part_weights = jnp.exp(scores_of(rows, queries))
                    mass = mass + jnp.sum(part_weights, axis=0, keepdims=True)
                    weights.append(part_weights.astype(BF16))
                    values.append(v_ref[rows, :])
                sum_ref[...] += dot(
                    jnp.concatenate(values, axis=0), jnp.concatenate(weights, axis=0), ((0,), (0,))
                )
                return mass

            row_ref[0:1, :] = shift
            row_ref[1:2, :] = spans(low, count, step, jnp.zeros((1, wide), F32), 8)

        @pl.when(jnp.logical_not(narrow_range))
        def _():
            def step(span, base, index, carried):
                most, mass = carried
                scores, values = [], []
                new_most = most
                for inner in range(span):
                    rows = chunk_rows(base + index * span + inner)
                    some = scores_of(rows, queries)
                    new_most = jnp.maximum(new_most, jnp.max(some, axis=0, keepdims=True))
                    scores.append(some)
                    values.append(v_ref[rows, :])
                shrink = jnp.exp(most - new_most)
                mass = mass * shrink
                weights = []
                for some in scores:
                    part_weights = jnp.exp(some - new_most)
                    mass = mass + jnp.sum(part_weights, axis=0, keepdims=True)
                    weights.append(part_weights.astype(BF16))
                sum_ref[...] = sum_ref[...] * shrink + dot(
                    jnp.concatenate(values, axis=0), jnp.concatenate(weights, axis=0), ((0,), (0,))
                )
                return new_most, mass

            most, mass = spans(
                low, count, step, (jnp.full((1, wide), FAR * 2, F32), jnp.zeros((1, wide), F32)), 4
            )
            row_ref[0:1, :] = most + shift
            row_ref[1:2, :] = mass

        mass = row_ref[1:2, :]
        result = sum_ref[...] / mass
        joined = jnp.concatenate(
            [result[:HEAD_DIM, :QUERY_ROWS], result[HEAD_DIM:, QUERY_ROWS:]], axis=0
        )
        out_ref[cut, :] = joined.T
        mass_ref[0, pl.ds(part, 1), :] = row_ref[0:1, :] + jnp.log(mass)


def attend(info, queries, keys, values, norms):
    row_count, width = queries.shape
    total = keys.shape[0]
    pairs = width // TILE
    parts = row_count // QUERY_ROWS
    narrow = pl.BlockSpec((row_count, TILE), lambda i, *_: (0, i))
    tall = pl.BlockSpec((total, TILE), lambda i, *_: (0, i))
    return pl.pallas_call(
        attend_kernel,
        grid_spec=pltpu.PrefetchScalarGridSpec(
            num_scalar_prefetch=1,
            grid=(pairs,),
            in_specs=[narrow, tall, tall, pl.BlockSpec(norms.shape, lambda i, *_: (0, 0))],
            out_specs=[
                narrow,
                pl.BlockSpec((1, parts, 2 * QUERY_ROWS), lambda i, *_: (i, 0, 0)),
            ],
            scratch_shapes=[
                pltpu.VMEM((total, TILE), BF16),
                pltpu.VMEM((TILE, 2 * QUERY_ROWS), F32),
                pltpu.VMEM((8, 2 * QUERY_ROWS), F32),
            ],
        ),
        out_shape=[
            jax.ShapeDtypeStruct((row_count, width), F32),
            jax.ShapeDtypeStruct((pairs, parts, 2 * QUERY_ROWS), F32),
        ],
        compiler_params=params(),
        name="attend",
    )(info, queries, keys, values, norms)


def attend_back_kernel(
    info, q_ref, k_ref, v_ref, grad_ref, out_ref, mass_ref, dq_ref, dk_ref, dv_ref,
    feature_ref, dk_sum, dv_sum, dq_sum,
):
    @pl.when(pl.program_id(0) == 0)
    def _():
        fill_key_features(feature_ref, info)

    row_count = q_ref.shape[0]
    total = k_ref.shape[0]
    low_block, high_block = active_range(info)
    for block in range(total // BLOCK):

        @pl.when(jnp.logical_and(block >= low_block, block <= high_block))
        def _():
            rows = pl.ds(block * BLOCK, BLOCK)
            dk_sum[rows, :] = jnp.zeros((BLOCK, TILE), F32)
            dv_sum[rows, :] = jnp.zeros((BLOCK, TILE), F32)

    for part in range(row_count // QUERY_ROWS):
        first = info[4] + part * QUERY_ROWS
        cut = pl.ds(part * QUERY_ROWS, QUERY_ROWS)
        q_rows = q_ref[cut, :].astype(F32)
        g_rows = grad_ref[cut, :].astype(F32)
        q_flip = q_rows.T
        g_flip = g_rows.T
        product = g_flip * out_ref[cut, :].T
        delta = jnp.concatenate(
            [
                jnp.sum(product[:HEAD_DIM], axis=0, keepdims=True),
                jnp.sum(product[HEAD_DIM:], axis=0, keepdims=True),
            ],
            axis=1,
        )
        onehot, sub = slot_rows(first, QUERY_ROWS, info)

        queries = jnp.concatenate(
            [stacked_heads(q_flip), with_parts(onehot, sub, -mass_ref[0, pl.ds(part, 1), :])], axis=0
        ).astype(BF16)
        grads = jnp.concatenate(
            [stacked_heads(g_flip), with_parts(jnp.zeros_like(onehot), sub, -delta)], axis=0
        ).astype(BF16)
        lane = lax.broadcasted_iota(jnp.int32, (QUERY_ROWS, TILE), 1)

        def stacked(rows):
            zero = jnp.zeros_like(rows)
            return jnp.concatenate(
                [jnp.where(lane < HEAD_DIM, rows, zero), jnp.where(lane < HEAD_DIM, zero, rows)],
                axis=0,
            ).astype(BF16)

        q_stack = stacked(q_rows)
        g_stack = stacked(g_rows)
        start, end = key_range(first, first + QUERY_ROWS - 1, info)
        dq_sum[...] = jnp.zeros_like(dq_sum)

        def step(span, base, index, carried):
            all_keys, all_grads = [], []
            for inner in range(span):
                rows = chunk_rows(base + index * span + inner)
                keys = k_ref[rows, :]
                features = feature_ref[rows, :]
                probs = jnp.exp(dot(jnp.concatenate([keys, features], axis=1), queries))
                change = dot(jnp.concatenate([v_ref[rows, :], features], axis=1), grads)
                grad_scores = (probs * change).astype(BF16)
                dv_sum[rows, :] += dot(probs.astype(BF16), g_stack)
                dk_sum[rows, :] += dot(grad_scores, q_stack)
                all_keys.append(keys)
                all_grads.append(grad_scores)
            dq_sum[...] += dot(
                jnp.concatenate(all_keys, axis=0), jnp.concatenate(all_grads, axis=0), ((0,), (0,))
            )
            return carried

        low = start // KEY_ROWS
        spans(low, (end + KEY_ROWS - 1) // KEY_ROWS - low, step, 0, 8)
        result = dq_sum[...]
        joined = jnp.concatenate(
            [result[:HEAD_DIM, :QUERY_ROWS], result[HEAD_DIM:, QUERY_ROWS:]], axis=0
        )
        dq_ref[cut, :] = joined.T * HEAD_DIM**-0.5

    for block in range(total // BLOCK):

        @pl.when(jnp.logical_and(block >= low_block, block <= high_block))
        def _():
            rows = pl.ds(block * BLOCK, BLOCK)
            dk_ref[rows, :] = dk_sum[rows, :].astype(BF16)
            dv_ref[rows, :] = dv_sum[rows, :].astype(BF16)

        @pl.when(jnp.logical_or(block < low_block, block > high_block))
        def _():
            rows = pl.ds(block * BLOCK, BLOCK)
            dk_ref[rows, :] = jnp.zeros((BLOCK, TILE), BF16)
            dv_ref[rows, :] = jnp.zeros((BLOCK, TILE), BF16)


def attend_back(info, queries, keys, values, grads, attended, mass):
    row_count, width = queries.shape
    total = keys.shape[0]
    pairs = width // TILE
    parts = row_count // QUERY_ROWS
    narrow = pl.BlockSpec((row_count, TILE), lambda i, *_: (0, i))
    tall = pl.BlockSpec((total, TILE), lambda i, *_: (0, i))
    return pl.pallas_call(
        attend_back_kernel,
        grid_spec=pltpu.PrefetchScalarGridSpec(
            num_scalar_prefetch=1,
            grid=(pairs,),
            in_specs=[
                narrow,
                tall,
                tall,
                narrow,
                narrow,
                pl.BlockSpec((1, parts, 2 * QUERY_ROWS), lambda i, *_: (i, 0, 0)),
            ],
            out_specs=[narrow, tall, tall],
            scratch_shapes=[
                pltpu.VMEM((total, TILE), BF16),
                pltpu.VMEM((total, TILE), F32),
                pltpu.VMEM((total, TILE), F32),
                pltpu.VMEM((TILE, 2 * QUERY_ROWS), F32),
            ],
        ),
        out_shape=[
            jax.ShapeDtypeStruct((row_count, width), F32),
            jax.ShapeDtypeStruct((total, width), BF16),
            jax.ShapeDtypeStruct((total, width), BF16),
        ],
        compiler_params=params(),
        name="attend_back",
    )(info, queries, keys, values, grads, attended, mass)


def slot_sums(first_row, info, values):
    count = values.shape[0]
    rows = first_row + lax.broadcasted_iota(jnp.int32, (8, count), 1)
    which = lax.broadcasted_iota(jnp.int32, (8, count), 0)
    picks = jnp.where(slot_of(rows, info) == which, 1.0, 0.0).astype(BF16)
    high, middle, low = thirds(values)
    return dot(picks, high) + dot(picks, middle) + dot(picks, low)


def mlp_kernel(
    info, x_ref, attended_ref, cot_ref, cond_ref, ada_ref, bias_ref, gain_ref, out_w_ref,
    fc1_ref, fc1_b_ref, fc2_ref, fc2_b_ref,
    layer_ref, g_fc1_ref, g_fc2_ref, g_out_ref, g_att_ref, g_mid_ref, early_ref,
    pack_ref, mods_ref, second_ref, second_t_ref, grad2_ref, branch_ref, middle_ref, xh_ref, inverse_ref,
    sum2_ref, gsum_ref,
):
    step = pl.program_id(0)
    width = x_ref.shape[1]
    row_count = x_ref.shape[0]
    first_row = info[4]

    def mod(which):
        picks = slot_picks(row_count, first_row, info)
        return dot(picks, mods_ref[:, which * width : (which + 1) * width])

    @pl.when(step == 0)
    def _():
        mods = dot(cond_ref[...], ada_ref[:, 2 * width :]) + bias_ref[:, 2 * width :]
        mods_ref[:, : 4 * width] = pick_table(mods)
        mods_ref[:, 4 * width :] = pick_table(
            (1.0 + mods[:, 2 * width : 3 * width]) * gain_ref[...]
        )
        attended_low = attended_ref[...].astype(BF16)
        branch = dot(attended_low, out_w_ref[...])
        branch_ref[...] = branch
        middle = x_ref[...].astype(F32) + mod(0) * branch
        middle_ref[...] = middle
        xh, inverse = normed(middle)
        xh_ref[...] = xh
        inverse_ref[...] = jnp.broadcast_to(inverse, inverse_ref.shape)
        second = xh * mod(4) + mod(1)
        second_ref[...] = second.astype(BF16)
        second_t_ref[...] = second.T.astype(BF16)
        grad2 = (cot_ref[...].astype(F32) * mod(3)).astype(BF16)
        grad2_ref[...] = grad2
        pack_ref[...] = jnp.zeros_like(pack_ref)
        pack_ref[17:18, :] = jnp.sum(grad2.astype(F32), axis=0, keepdims=True)
        lane = lax.broadcasted_iota(jnp.int32, (1, width), 1)
        table = jnp.zeros((1, width), F32)
        for slot in range(4):
            table = jnp.where(lane == slot, info[8 + slot].astype(F32), table)
        pack_ref[22:23, :] = table
        sum2_ref[...] = jnp.zeros_like(sum2_ref)
        gsum_ref[...] = jnp.zeros_like(gsum_ref)

    pre = dot(second_ref[...], fc1_ref[...]) + fc1_b_ref[...]
    root = math.sqrt(2.0 / math.pi)
    square = pre * pre
    bend = jnp.tanh(root * pre * (1.0 + 0.044715 * square))
    half = 0.5 * (1.0 + bend)
    act = (pre * half).astype(BF16)
    slope = half + 0.5 * pre * (1.0 - bend * bend) * (root * (1.0 + 0.134145 * square))
    sum2_ref[...] += dot(act, fc2_ref[...])
    grad_act = dot(grad2_ref[...], fc2_ref[...], ((1,), (1,)))
    grad_pre = (grad_act * slope).astype(BF16)
    pack_ref[pl.ds(18 + step, 1), :] = jnp.sum(grad_pre.astype(F32), axis=0, keepdims=True)
    g_fc2_ref[...] = dot(act, grad2_ref[...], ((0,), (0,))).astype(BF16)
    g_fc1_ref[...] = dot(second_t_ref[...], grad_pre).astype(BF16)
    gsum_ref[...] += dot(grad_pre, fc1_ref[...], ((1,), (1,)))

    @pl.when(step == pl.num_programs(0) - 1)
    def _():
        branch2 = sum2_ref[...] + fc2_b_ref[...]
        layer_ref[...] = (middle_ref[...] + mod(3) * branch2).astype(BF16)
        upstream = cot_ref[...].astype(F32)
        pack_ref[12:16, :] = slot_sums(first_row, info, upstream * branch2)[:4]
        grad = gsum_ref[...]
        xh = xh_ref[...]
        picks = slot_picks(row_count, first_row, info)
        pack_ref[4:8, :] = slot_sums(first_row, info, grad)[:4]
        moved = grad * xh
        pack_ref[8:12, :] = slot_sums(first_row, info, moved * gain_ref[...])[:4]
        pack_ref[16:17, :] = jnp.sum(moved * (1.0 + mod(2)), axis=0, keepdims=True)
        h = grad * mod(4)
        inverse = inverse_ref[:, 0:1]
        g_mid = upstream + inverse * (
            h - jnp.mean(h, axis=1, keepdims=True) - xh * jnp.mean(h * xh, axis=1, keepdims=True)
        )
        g_mid_ref[...] = g_mid
        pack_ref[0:4, :] = slot_sums(first_row, info, g_mid * branch_ref[...])[:4]
        early_ref[...] = pack_ref[...].astype(BF16)
        g_branch = (g_mid * mod(0)).astype(BF16)
        g_out_ref[...] = dot(attended_ref[...].astype(BF16), g_branch, ((0,), (0,))).astype(BF16)
        g_att_ref[...] = dot(g_branch, out_w_ref[...], ((1,), (1,))).astype(BF16)


def mlp(info, x, attended, cot, cond, ada, bias, gain, out_w, fc1, fc1_b, fc2, fc2_b):
    row_count, width = x.shape
    hidden = fc1.shape[1]
    chunk = CHUNK

    def whole(shape):
        return pl.BlockSpec(shape, lambda i, *_: (0,) * len(shape))

    columns = pl.BlockSpec((width, chunk), lambda i, *_: (0, i))
    lines = pl.BlockSpec((chunk, width), lambda i, *_: (i, 0))
    part = pl.BlockSpec((1, chunk), lambda i, *_: (0, i))
    rows = (row_count, width)
    return pl.pallas_call(
        mlp_kernel,
        grid_spec=pltpu.PrefetchScalarGridSpec(
            num_scalar_prefetch=1,
            grid=(hidden // chunk,),
            in_specs=[
                whole(rows), whole(rows), whole(rows), whole(cond.shape), whole(ada.shape),
                whole(bias.shape), whole(gain.shape), whole(out_w.shape), columns, part, lines,
                whole(fc2_b.shape),
            ],
            out_specs=[
                whole(rows), columns, lines, whole(out_w.shape), whole(rows), whole(rows),
                whole((32, width)),
            ],
            scratch_shapes=[
                pltpu.VMEM((32, width), F32),
                pltpu.VMEM((16, 5 * width), BF16),
                pltpu.VMEM(rows, BF16),
                pltpu.VMEM((width, row_count), BF16),
                pltpu.VMEM(rows, BF16),
                pltpu.VMEM(rows, F32),
                pltpu.VMEM(rows, F32),
                pltpu.VMEM(rows, F32),
                pltpu.VMEM((row_count, TILE), F32),
                pltpu.VMEM(rows, F32),
                pltpu.VMEM(rows, F32),
            ],
        ),
        out_shape=[
            jax.ShapeDtypeStruct(rows, BF16),
            jax.ShapeDtypeStruct(fc1.shape, BF16),
            jax.ShapeDtypeStruct(fc2.shape, BF16),
            jax.ShapeDtypeStruct(out_w.shape, BF16),
            jax.ShapeDtypeStruct(rows, BF16),
            jax.ShapeDtypeStruct(rows, F32),
            jax.ShapeDtypeStruct((32, width), BF16),
        ],
        compiler_params=params(),
        name="mlp",
    )(info, x, attended, cot, cond, ada, bias, gain, out_w, fc1, fc1_b, fc2, fc2_b)


MESH = pl.DeviceIdType.MESH


def piece_of(array, which):
    rows, columns = array
    if rows % 32 == 0 and (columns // 2) % TILE == 0:
        return (which % 2) * (rows // 2), rows // 2, (which // 2) * (columns // 2), columns // 2
    return 0, rows, which * (columns // 4), columns // 4


def cut_of(start, size, whole, unit):
    if size == whole:
        return slice(None)
    return pl.ds(pl.multiple_of(start, unit), size)


class Place:
    def __init__(self):
        self.wide = lax.axis_index("wide")
        self.narrow = lax.axis_index("narrow")
        self.z = self.narrow // 2
        self.core = self.narrow % 2
        self.quarter = self.wide % 4
        self.bit1 = 1 + self.core
        self.bit2 = 2 - self.core
        self.near = self.z + 1 - 2 * (self.z % 2)
        low = self.z < 2
        self.order = (self.near, jnp.where(low, 2, 1), jnp.where(low, 3, 0))

    def flip(self, value, bit):
        return value + bit * (1 - 2 * ((value // bit) % 2))

    def partner(self, bit):
        return (self.flip(self.wide, bit), self.narrow)

    def sibling(self):
        return (self.wide, self.narrow + 1 - 2 * self.core)

    def column(self, narrow):
        return (self.wide, narrow)

    def up(self):
        return (self.wide, jnp.minimum(self.narrow + 2, 7))

    def down(self):
        return (self.wide, jnp.maximum(self.narrow - 2, 0))


def greet(place, size):
    barrier = pltpu.get_barrier_semaphore()
    for step in range(1, size):
        pl.semaphore_signal(
            barrier, inc=1, device_id=place.column((place.narrow + step) % size), device_id_type=MESH
        )
    for bit in (1, 2):
        pl.semaphore_signal(barrier, inc=1, device_id=place.partner(bit), device_id_type=MESH)
    pl.semaphore_wait(barrier, size + 1)


def gather_kernel(shapes, size, *refs):
    count = len(shapes)
    shard_refs = refs[:count]
    x_ref, position_ref, vector_ref = refs[count : count + 3]
    full_refs = refs[count + 3 : 2 * count + 3]
    x_all, position_all, vector_all = refs[2 * count + 3 : 2 * count + 6]
    (
        own_sems, own_send, own_recv, line_send, line_recv, turn_send, turn_recv, next_send,
        next_recv, back_send, back_recv, small_send, small_recv,
    ) = refs[2 * count + 6 :]
    place = Place()
    narrow, z, core = place.narrow, place.z, place.core
    greet(place, size)

    def remote(source, target, send, recv, device):
        return pltpu.make_async_remote_copy(
            src_ref=source, dst_ref=target, send_sem=send, recv_sem=recv, device_id=device,
            device_id_type=MESH,
        )

    def region(a, owner, which):
        rows, columns = shapes[a]
        first_row, row_count, first_column, column_count = piece_of(shapes[a], which)
        start = pl.multiple_of(owner * rows + first_row, 16)
        if isinstance(first_column, int):
            return full_refs[a].at[pl.ds(start, row_count), :]
        lanes = pl.ds(pl.multiple_of(first_column, TILE), column_count)
        return full_refs[a].at[pl.ds(start, row_count), lanes]

    def shard(a, owner):
        rows, _ = shapes[a]
        return full_refs[a].at[pl.ds(pl.multiple_of(owner * rows, 16), rows), :]

    def own_piece(a):
        first_row, row_count, first_column, column_count = piece_of(shapes[a], place.quarter)
        if isinstance(first_row, int) and first_row == 0:
            rows = slice(None)
        else:
            rows = pl.ds(pl.multiple_of(first_row, 16), row_count)
        if isinstance(first_column, int):
            return shard_refs[a].at[rows, :]
        return shard_refs[a].at[rows, pl.ds(pl.multiple_of(first_column, TILE), column_count)]

    block = x_ref.shape[0]

    def tokens_of(owner):
        return x_all.at[pl.ds(pl.multiple_of(owner * block, 16), block), :]

    owner_of = [zp * 2 + core for zp in place.order]
    smalls = []
    for step in range(1, size):
        device = place.column((narrow + step) % size)
        smalls.append(
            remote(vector_ref, vector_all.at[narrow], small_send.at[0, step], small_recv.at[0, step], device)
        )
        smalls.append(
            remote(position_ref, position_all.at[narrow], small_send.at[1, step], small_recv.at[1, step], device)
        )
    for copy in smalls:
        copy.start()
    local = [
        pltpu.make_async_copy(vector_ref, vector_all.at[narrow], own_sems.at[count + 1]),
        pltpu.make_async_copy(position_ref, position_all.at[narrow], own_sems.at[count + 2]),
        pltpu.make_async_copy(x_ref, tokens_of(narrow), own_sems.at[count]),
    ]
    for a in range(count):
        local.append(pltpu.make_async_copy(shard_refs[a], shard(a, narrow), own_sems.at[a]))
    for copy in local:
        copy.start()

    def line_copies(a, owner, source, target):
        return (
            remote(source, target, line_send.at[a, owner // 2, 0], line_recv.at[a, owner // 2], place.up()),
            remote(source, target, line_send.at[a, owner // 2, 1], line_recv.at[a, owner // 2], place.down()),
        )

    def line_pair(a, owner):
        if a == count:
            target = tokens_of(owner)
            source = target
        else:
            target = region(a, owner, place.quarter)
            source = target
        return line_copies(a, owner, source, target)

    def own_pair(a):
        if a == count:
            return line_copies(a, narrow, x_ref, tokens_of(narrow))
        return line_copies(a, narrow, own_piece(a), region(a, narrow, place.quarter))

    def own_to_sibling(a):
        if a == count:
            return remote(x_ref, tokens_of(narrow), own_send.at[a], own_recv.at[a], place.sibling())
        return remote(shard_refs[a], shard(a, narrow), own_send.at[a], own_recv.at[a], place.sibling())

    def start_own(a):
        up, down = own_pair(a)
        pl.when(z < 3)(up.start)
        pl.when(z > 0)(down.start)
        own_to_sibling(a).start()

    def forwards(a, index):
        zp = place.order[index]
        if a == count:
            near = jnp.logical_and(zp - z < 2, z - zp < 2)
            return (
                jnp.logical_and(jnp.logical_and(zp < z, z < 3), near),
                jnp.logical_and(jnp.logical_and(zp > z, z > 0), near),
            )
        return jnp.logical_and(zp < z, z < 3), jnp.logical_and(zp > z, z > 0)

    def arrives(index):
        zp = place.order[index]
        return jnp.logical_and(zp - z < 3, z - zp < 3)

    def quarters(bit_first):
        first = place.flip(place.quarter, place.bit1)
        return first, place.flip(place.quarter, place.bit2), place.flip(first, place.bit2)

    def turn_copy(a, index):
        target = region(a, owner_of[index], place.quarter)
        return remote(
            target, target, turn_send.at[a, index], turn_recv.at[a, index], place.partner(place.bit1)
        )

    def next_copy(a, index, which):
        quarter = place.quarter if which == 0 else place.flip(place.quarter, place.bit1)
        target = region(a, owner_of[index], quarter)
        return remote(
            target, target, next_send.at[a, index, which], next_recv.at[a, index, which],
            place.partner(place.bit2),
        )

    def back_copy(a, index):
        if a == count:
            target = tokens_of(owner_of[index])
        else:
            target = shard(a, owner_of[index])
        return remote(
            target, target, back_send.at[a, index], back_recv.at[a, index], place.sibling()
        )

    def on_line(a, index):
        up, down = line_pair(a, owner_of[index])

        def work():
            up.wait_recv()
            goes_up, goes_down = forwards(a, index)
            pl.when(goes_up)(up.start)
            pl.when(goes_down)(down.start)
            if a == count:
                back_copy(a, index).start()
            else:
                turn_copy(a, index).start()
                next_copy(a, index, 0).start()

        if a == count:
            pl.when(arrives(index))(work)
        else:
            work()

    def turned(index):
        for a in range(count):
            turn_copy(a, index).wait_recv()
            next_copy(a, index, 1).start()

    def on_lines(index):
        for a in range(count):
            on_line(a, index)

    token_up, token_down = own_pair(count)
    for a in range(count):
        start_own(a)
    own_to_sibling(count).start()
    pl.when(z == 0)(token_up.start)
    pl.when(z == 3)(token_down.start)
    on_lines(0)
    pl.when(z == 1)(token_up.start)
    pl.when(z == 2)(token_down.start)
    on_lines(1)
    turned(0)
    on_lines(2)
    pl.when(z == 2)(token_up.start)
    pl.when(z == 1)(token_down.start)
    turned(1)
    turned(2)
    for index in range(3):
        on_line(count, index)
    for index in range(3):
        for a in range(count):
            next_copy(a, index, 0).wait_recv()
            next_copy(a, index, 1).wait_recv()
            back_copy(a, index).start()
    for a in range(count):
        for index in range(3):
            back_copy(a, index).wait_recv()
    for a in range(count + 1):
        own_to_sibling(a).wait()
        up, down = own_pair(a)
        pl.when(z < 3)(up.wait_send)
        pl.when(z > 0)(down.wait_send)
    for index in range(3):

        @pl.when(arrives(index))
        def _():
            back_copy(count, index).wait()
            goes_up, goes_down = forwards(count, index)
            up, down = line_pair(count, owner_of[index])
            pl.when(goes_up)(up.wait_send)
            pl.when(goes_down)(down.wait_send)

        for a in range(count):
            goes_up, goes_down = forwards(a, index)
            up, down = line_pair(a, owner_of[index])
            pl.when(goes_up)(up.wait_send)
            pl.when(goes_down)(down.wait_send)
            turn_copy(a, index).wait_send()
            next_copy(a, index, 0).wait_send()
            next_copy(a, index, 1).wait_send()
            back_copy(a, index).wait_send()
    for copy in local:
        copy.wait()
    for copy in smalls:
        copy.wait()


def gather_all(x, positions, vector, shards, size):
    count = len(shards)
    shapes = tuple(shard.shape for shard in shards)
    anywhere = pl.BlockSpec(memory_space=pl.ANY)
    dma = pltpu.SemaphoreType.DMA
    out_shape = [
        jax.ShapeDtypeStruct((size * shard.shape[0], shard.shape[1]), shard.dtype) for shard in shards
    ] + [
        jax.ShapeDtypeStruct((size * x.shape[0], x.shape[1]), x.dtype),
        jax.ShapeDtypeStruct((size, *positions.shape), positions.dtype),
        jax.ShapeDtypeStruct((size, *vector.shape), vector.dtype),
    ]
    return pl.pallas_call(
        functools.partial(gather_kernel, shapes, size),
        out_shape=out_shape,
        in_specs=[anywhere] * (count + 3),
        out_specs=[anywhere] * (count + 3),
        scratch_shapes=[
            dma((count + 3,)),
            dma((count + 1,)),
            dma((count + 1,)),
            dma((count + 1, 4, 2)),
            dma((count + 1, 4)),
            dma((count, 3)),
            dma((count, 3)),
            dma((count, 3, 2)),
            dma((count, 3, 2)),
            dma((count + 1, 3)),
            dma((count + 1, 3)),
            dma((2, size)),
            dma((2, size)),
        ],
        compiler_params=pltpu.CompilerParams(collective_id=1, has_side_effects=True),
        name="gather_all",
    )(*shards, x, positions, vector)


def add_into(target, source):
    rows = target.shape[-2]
    step = 32 if rows % 32 == 0 else 16
    lead = target.shape[:-2]

    @pl.loop(0, rows // step)
    def _(turn_index):
        cut = pl.ds(pl.multiple_of(turn_index * step, 16), step)
        for index in np.ndindex(*lead):
            at = (*index, cut, slice(None))
            target[at] = target[at] + source[at]


def finish_rows(info, grad, x, g_mid, mods, gain):
    width = x.shape[1]
    first_row = info[4]
    scale = 1.0 + mods[:, width:]
    picks = slot_picks(x.shape[0], first_row, info)
    xh, inverse = normed(x.astype(F32))
    moved = grad * xh
    sums = jnp.concatenate(
        [slot_sums(first_row, info, grad), slot_sums(first_row, info, moved * gain)], axis=1
    )
    g_gain = jnp.sum(moved * dot(picks, pick_table(scale)), axis=0, keepdims=True)
    h = grad * dot(picks, pick_table(scale * gain))
    tokens = g_mid + inverse * (
        h - jnp.mean(h, axis=1, keepdims=True) - xh * jnp.mean(h * xh, axis=1, keepdims=True)
    )
    return tokens, sums, g_gain


def folded(values, columns):
    return jnp.concatenate(
        [values[:, at : at + columns] for at in range(0, values.shape[1], columns)], axis=0
    )


def reduce_kernel(shapes, summed, size, groups, info, *refs):
    count, made = len(shapes), summed - 1
    refs = list(refs)
    grad_refs = [refs.pop(0) for _ in range(count - 1)]
    grad_refs.insert(made, None)
    (
        first_ref, dk_ref, dv_ref, early_ref, dq_ref, weight_ref, position_ref, coarse_ref, fine_ref,
        x_ref, g_mid_ref, mods_ref, gain_ref,
    ) = (refs.pop(0) for _ in range(13))
    out_refs = [refs.pop(0) for _ in range(count)]
    tokens_ref, early_all, late_all = (refs.pop(0) for _ in range(3))
    rest = refs
    own, turned, nexted, far = ([rest.pop(0) for _ in range(count)] for _ in range(4))
    side, upward, downward = ([rest.pop(0) for _ in range(summed)] for _ in range(3))
    (
        first_in, dk_in, dv_in, dw_sum, made_out, dx_out,
        dx_own, dx_side, dx_up, dx_down, late_ref, early_in, late_in, early_sum, late_sum,
        own_sem, side_send, side_recv, turn_send, turn_recv, next_send, next_recv, line_send,
        line_recv, far_send, far_recv, share_send, share_recv, final_sem,
        block_sem, dx_side_send, dx_side_recv, dx_send, dx_recv,
        pack_send, pack_recv, wide_send, wide_recv, pack_own,
    ) = rest
    place = Place()
    z, core, narrow = place.z, place.core, place.narrow
    barrier = pltpu.get_barrier_semaphore()
    for step in range(1, size):
        pl.semaphore_signal(
            barrier, inc=1, device_id=place.column((narrow + step) % size), device_id_type=MESH
        )
    for step in range(1, groups):
        pl.semaphore_signal(
            barrier, inc=1, device_id=((place.wide + step) % groups, narrow), device_id_type=MESH
        )
    pl.semaphore_wait(barrier, size + groups - 2)

    def remote(source, target, send, recv, device):
        return pltpu.make_async_remote_copy(
            src_ref=source, dst_ref=target, send_sem=send, recv_sem=recv, device_id=device,
            device_id_type=MESH,
        )

    def piece(ref, a, which, lead):
        rows, columns = shapes[a]
        first_row, row_count, first_column, column_count = piece_of(shapes[a], which)
        return ref.at[
            (*lead, cut_of(first_row, row_count, rows, 16), cut_of(first_column, column_count, columns, TILE))
        ]

    quarter = place.quarter
    other1 = place.flip(quarter, place.bit1)
    other2 = place.flip(quarter, place.bit2)
    every = (slice(None),)

    def pack_copies(which, source, target):
        return [
            remote(
                source, target.at[narrow], pack_send.at[which, step], pack_recv.at[which, step],
                place.column((narrow + step) % size),
            )
            for step in range(1, size)
        ]

    def wide_copies(which, source, target):
        return [
            remote(
                source, target.at[place.wide], wide_send.at[which, step], wide_recv.at[which, step],
                ((place.wide + step) % groups, narrow),
            )
            for step in range(1, groups)
        ]

    early_copies = pack_copies(0, early_ref, early_in)
    early_own = pltpu.make_async_copy(early_ref, early_in.at[narrow], pack_own.at[0])
    early_own.start()

    side_copy, own_copy = [], []
    for a in range(count):
        if a == made:
            side_copy.append(
                remote(made_out, side[a], side_send.at[a], side_recv.at[a], place.sibling())
            )
            own_copy.append(None)
            continue
        if a < summed:
            side_copy.append(
                remote(grad_refs[a].at[:, 1 - core], side[a], side_send.at[a], side_recv.at[a], place.sibling())
            )
            own_copy.append(pltpu.make_async_copy(grad_refs[a].at[:, core], own[a], own_sem.at[a]))
            side_copy[a].start()
        else:
            own_copy.append(pltpu.make_async_copy(grad_refs[a], own[a].at[0], own_sem.at[a]))
        own_copy[a].start()

    def dx_copy(upwards, slot):
        zp = jnp.clip(z + 1 + slot if upwards else z - 1 - slot, 0, 3)
        way = 0 if upwards else 1
        landing = dx_up if upwards else dx_down
        return remote(
            dx_own.at[zp], landing.at[slot], dx_send.at[way, slot], dx_recv.at[way, slot],
            place.up() if upwards else place.down(),
        )

    def dx_middle():
        @pl.when(z < 3)
        def _():
            @pl.when(z > 0)
            def _():
                dx_copy(True, 1).wait_recv()
                add_into(dx_own.at[jnp.minimum(z + 1, 3)], dx_up.at[1])

            dx_copy(True, 0).start()

        @pl.when(z > 0)
        def _():
            @pl.when(z < 3)
            def _():
                dx_copy(False, 1).wait_recv()
                add_into(dx_own.at[jnp.maximum(z - 1, 0)], dx_down.at[1])

            dx_copy(False, 0).start()

    def dx_end():
        @pl.when(z > 0)
        def _():
            dx_copy(True, 0).wait_recv()
            add_into(dx_own.at[z], dx_up.at[0])

        @pl.when(z < 3)
        def _():
            dx_copy(False, 0).wait_recv()
            add_into(dx_own.at[z], dx_down.at[0])

        pl.when(z < 3)(dx_copy(True, 0).wait_send)
        pl.when(z < 2)(dx_copy(True, 1).wait_send)
        pl.when(z > 0)(dx_copy(False, 0).wait_send)
        pl.when(z > 1)(dx_copy(False, 1).wait_send)

    def turn_copy(a):
        rows, columns = shapes[a]
        out = []
        for bit in (1, 2):
            if bit == 1:
                there = (slice(None), pl.ds(pl.multiple_of((1 - quarter % 2) * (rows // 2), 16), rows // 2), slice(None))
                landing = turned[a].at[:, pl.ds(0, rows // 2), :]
            else:
                there = (slice(None), slice(None), pl.ds(pl.multiple_of((1 - quarter // 2) * (columns // 2), TILE), columns // 2))
                landing = turned[a].at[:, :, pl.ds(0, columns // 2)]
            out.append(
                remote(own[a].at[there], landing, turn_send.at[a], turn_recv.at[a], place.partner(bit))
            )
        return out

    def by_core(copies, what):
        pl.when(core == 0)(getattr(copies[0], what))
        pl.when(core == 1)(getattr(copies[1], what))

    def join(a):
        if a != made:
            own_copy[a].wait()
        if a < summed:
            side_copy[a].wait_recv()
            add_into(own[a], side[a])

    def start_turn(a):
        by_core(turn_copy(a), "start")

    def next_copy(a):
        return remote(
            piece(own[a], a, other2, every), nexted[a], next_send.at[a], next_recv.at[a],
            place.partner(place.bit2),
        )

    def start_next(a):
        rows, columns = shapes[a]
        by_core(turn_copy(a), "wait_recv")

        @pl.when(core == 0)
        def _():
            add_into(
                own[a].at[:, pl.ds(pl.multiple_of((quarter % 2) * (rows // 2), 16), rows // 2), :],
                turned[a].at[:, pl.ds(0, rows // 2), :],
            )

        @pl.when(core == 1)
        def _():
            add_into(
                own[a].at[:, :, pl.ds(pl.multiple_of((quarter // 2) * (columns // 2), TILE), columns // 2)],
                turned[a].at[:, :, pl.ds(0, columns // 2)],
            )

        next_copy(a).start()

    def line_copy(a, zp, upwards, source):
        if upwards:
            return remote(source, upward[a].at[zp], line_send.at[a, zp, 0], line_recv.at[a, zp, 0], place.up())
        return remote(source, downward[a].at[zp], line_send.at[a, zp, 1], line_recv.at[a, zp, 1], place.down())

    def start_line(a):
        next_copy(a).wait_recv()
        add_into(piece(own[a], a, quarter, every), nexted[a])
        if a >= summed:
            return
        for zp in (3, 2, 1):
            pl.when(z == 0)(line_copy(a, zp, True, piece(own[a], a, quarter, (zp,))).start)
            low = 3 - zp
            pl.when(z == 3)(line_copy(a, low, False, piece(own[a], a, quarter, (low,))).start)

    def middle_line(a):
        if a >= summed:
            return
        for zp in (3, 2, 1):

            @pl.when(jnp.logical_and(z > 0, z < zp))
            def _():
                copy = line_copy(a, zp, True, upward[a].at[zp])
                copy.wait_recv()
                add_into(upward[a].at[zp], piece(own[a], a, quarter, (zp,)))
                copy.start()

            low = 3 - zp

            @pl.when(jnp.logical_and(z < 3, z > low))
            def _():
                copy = line_copy(a, low, False, downward[a].at[low])
                copy.wait_recv()
                add_into(downward[a].at[low], piece(own[a], a, quarter, (low,)))
                copy.start()

    def share_copy(a, which, bit_place, slot):
        source = piece(out_refs[a], a, which, ())
        return remote(source, source, share_send.at[a, slot], share_recv.at[a, slot], place.partner(bit_place))

    def kept(a):
        return piece(own[a], a, quarter, (z,) if a < summed else (0,))

    def final_copy(a):
        return pltpu.make_async_copy(
            kept(a), piece(out_refs[a], a, quarter, ()), final_sem.at[a]
        )

    def far_copy(a, which, bit):
        return remote(
            kept(a), far[a].at[which], far_send.at[a, which],
            far_recv.at[a, which], (place.flip(place.wide, bit), narrow),
        )

    def end_line(a):
        mine = kept(a)
        if a < summed:

            @pl.when(z > 0)
            def _():
                line_copy(a, z, True, mine).wait_recv()
                add_into(mine, upward[a].at[z])

            @pl.when(z < 3)
            def _():
                line_copy(a, z, False, mine).wait_recv()
                add_into(mine, downward[a].at[z])

        bit, which = 4, 0
        while bit < groups:
            copy = far_copy(a, which, bit)
            copy.start()
            copy.wait()
            add_into(mine, far[a].at[which])
            bit, which = bit * 2, which + 1
        final_copy(a).start()

    def start_share(a):
        final_copy(a).wait()
        share_copy(a, quarter, place.bit1, 0).start()
        share_copy(a, quarter, place.bit2, 1).start()

    def pass_share(a):
        share_copy(a, quarter, place.bit1, 0).wait_recv()
        share_copy(a, other1, place.bit2, 2).start()

    def close(a):
        share_copy(a, quarter, place.bit2, 1).wait_recv()
        share_copy(a, other1, place.bit2, 2).wait_recv()
        share_copy(a, quarter, place.bit1, 0).wait_send()
        share_copy(a, quarter, place.bit2, 1).wait_send()
        share_copy(a, other1, place.bit2, 2).wait_send()
        by_core(turn_copy(a), "wait_send")
        next_copy(a).wait_send()
        if a >= summed:
            return
        side_copy[a].wait_send()
        for zp in range(4):
            mine = piece(own[a], a, quarter, (zp,))
            pl.when(z < zp)(line_copy(a, zp, True, mine).wait_send)
            pl.when(z > zp)(line_copy(a, zp, False, mine).wait_send)

    def column_total(landed):
        total = landed[0].astype(F32)
        for step in range(1, size):
            total = total + landed[step].astype(F32)
        return total.astype(BF16)

    width = x_ref.shape[1]
    block_rows = x_ref.shape[0]

    def zp_of(step):
        near = place.near
        return jnp.where(
            step == 0, (z + 2) % 4, jnp.where(step == 1, near, jnp.where(step == 2, (near + 2) % 4, z))
        )

    def needed(step):
        zp = zp_of(step)
        return jnp.logical_and(zp - z < 3, z - zp < 3)

    def fetch(turn_index):
        parity = turn_index % 2
        owner = zp_of(turn_index // 2) * 2 + jnp.where(parity == 0, 1 - core, core)
        rows = pl.ds(pl.multiple_of(owner * block_rows, block_rows), block_rows)
        return [
            pltpu.make_async_copy(ref.at[rows, :], landing.at[parity], block_sem.at[which, parity])
            for which, (ref, landing) in enumerate(((first_ref, first_in), (dk_ref, dk_in), (dv_ref, dv_in)))
        ]

    def dx_side_copy(step):
        return remote(
            dx_out.at[step % 2], dx_side.at[zp_of(step)], dx_side_send.at[step], dx_side_recv.at[step],
            place.sibling(),
        )

    def turned_back(values, cosine, sine):
        tiles = []
        for tile in range(width // TILE):
            cut = slice(tile * TILE, (tile + 1) * TILE)
            tiles.append(turn_back(values[:, cut].astype(F32), cosine, sine).astype(BF16))
        return jnp.concatenate(tiles, axis=1)

    dw_sum[...] = jnp.zeros_like(dw_sum)
    for copy in fetch(0):
        copy.start()

    @pl.loop(0, 8)
    def _(turn_index):
        step = turn_index // 2
        parity = turn_index % 2
        zp = zp_of(step)
        owner = zp * 2 + jnp.where(parity == 0, 1 - core, core)

        @pl.when(turn_index < 7)
        def _():
            for copy in fetch(turn_index + 1):
                copy.start()

        for copy in fetch(turn_index):
            copy.wait()

        @pl.when(needed(step))
        def _():
            cosine, sine = rotary(position_ref[owner], coarse_ref, fine_ref)
            dk = turned_back(dk_in[parity], cosine, sine)
            dv = dv_in[parity]
            first = first_in[parity]
            dw_sum[:, width : 2 * width] += dot(first, dk, ((0,), (0,)))
            dw_sum[:, 2 * width :] += dot(first, dv, ((0,), (0,)))
            total = (
                dot(dk, weight_ref[:, width : 2 * width], ((1,), (1,)))
                + dot(dv, weight_ref[:, 2 * width :], ((1,), (1,)))
            ).astype(BF16)

            @pl.when(parity == 0)
            def _():
                @pl.when(jnp.logical_and(step > 1, needed(step - 2)))
                def _():
                    dx_side_copy(step - 2).wait_send()

                dx_out[step % 2] = total
                dx_side_copy(step).start()

            @pl.when(parity == 1)
            def _():
                dx_own[zp] = total
                dx_side_copy(step).wait_recv()
                add_into(dx_own.at[zp], dx_side.at[zp])

        @pl.when(turn_index == 1)
        def _():
            pl.when(z < 2)(dx_copy(True, 1).start)
            pl.when(z > 1)(dx_copy(False, 1).start)
            join(0)
            start_turn(0)

        @pl.when(turn_index == 3)
        def _():
            for a in range(1, count):
                if a != made:
                    join(a)
                    start_turn(a)

    cosine, sine = rotary(position_ref[narrow], coarse_ref, fine_ref)
    dq = turned_back(dq_ref[...], cosine, sine)
    dw_sum[:, :width] = dot(first_in[1], dq, ((0,), (0,)))
    dx_own[z] = (
        dx_own[z].astype(F32) + dot(dq, weight_ref[:, :width], ((1,), (1,)))
    ).astype(BF16)
    shard_rows = shapes[made][0]

    @pl.loop(0, 4)
    def _(zp):
        mine = pl.ds(pl.multiple_of((2 * zp + core) * shard_rows, 16), shard_rows)
        other = pl.ds(pl.multiple_of((2 * zp + 1 - core) * shard_rows, 16), shard_rows)
        own[made][zp] = dw_sum[mine, :].astype(BF16)
        made_out[zp] = dw_sum[other, :].astype(BF16)

    side_copy[made].start()
    dx_middle()
    for a in range(count):
        if a != made:
            start_next(a)
    join(made)
    start_turn(made)
    for copy in early_copies:
        copy.start()
    for a in range(made):
        start_line(a)
    for a in range(summed, count):
        start_line(a)
        end_line(a)
        start_share(a)
    for a in range(made):
        middle_line(a)
    start_next(made)
    dx_end()
    for a in range(made):
        end_line(a)
        start_share(a)
    start_line(made)
    tokens, sums, g_gain = finish_rows(
        info, dx_own[z].astype(F32), x_ref[...], g_mid_ref[...], mods_ref[...], gain_ref[...]
    )
    tokens_ref[...] = tokens
    quarter_width = sums.shape[1] // 4
    late_ref[...] = jnp.concatenate(
        [
            folded(sums[:4], quarter_width),
            folded(g_gain, quarter_width),
            jnp.zeros((14, quarter_width), F32),
        ],
        axis=0,
    ).astype(BF16)
    late_copies = pack_copies(1, late_ref, late_in)
    for copy in late_copies:
        copy.start()
    late_own = pltpu.make_async_copy(late_ref, late_in.at[narrow], pack_own.at[1])
    late_own.start()
    middle_line(made)
    for a in range(count):
        if a != made:
            pass_share(a)
    end_line(made)
    start_share(made)
    for copy in early_copies:
        copy.wait_recv()
    early_own.wait()
    early_sum[...] = column_total(early_in)
    early_wide = wide_copies(0, early_sum, early_all)
    for copy in early_wide:
        copy.start()
    early_final = pltpu.make_async_copy(early_sum, early_all.at[place.wide], pack_own.at[2])
    early_final.start()
    for copy in late_copies:
        copy.wait_recv()
    late_own.wait()
    late_sum[...] = column_total(late_in)
    late_wide = wide_copies(1, late_sum, late_all)
    for copy in late_wide:
        copy.start()
    late_final = pltpu.make_async_copy(late_sum, late_all.at[place.wide], pack_own.at[3])
    late_final.start()
    pass_share(made)
    for a in range(count):
        close(a)
    for step in (2, 3):
        pl.when(needed(step))(dx_side_copy(step).wait_send)
    pl.when(jnp.logical_and(needed(0), jnp.logical_not(needed(2))))(dx_side_copy(0).wait_send)
    pl.when(jnp.logical_and(needed(1), jnp.logical_not(needed(3))))(dx_side_copy(1).wait_send)
    early_final.wait()
    late_final.wait()
    for copy in early_copies + late_copies:
        copy.wait_send()
    for copy in early_wide + late_wide:
        copy.wait()


def reduce_all(
    info, grads, summed, first, dk, dv, early, dq, weight, positions, tables, x, g_mid, mods, gain,
    size, groups,
):
    shapes = tuple((grad.shape[0] // size, grad.shape[1]) for grad in (*grads, weight)) + tuple(
        shard.shape for shard in summed
    )
    count, full = len(shapes), len(grads) + 1
    row_count, width = x.shape
    anywhere = pl.BlockSpec(memory_space=pl.ANY)
    vmem = pl.BlockSpec(memory_space=pltpu.VMEM)
    dma = pltpu.SemaphoreType.DMA

    def scratch(*shape):
        return pltpu.VMEM(shape, BF16)

    pieces = [(piece_of(shape, 0)[1], piece_of(shape, 0)[3]) for shape in shapes]
    leads = [4] * full + [1] * len(summed)
    late = (32, 2 * width // 4)
    turns = max(1, int(math.log2(groups)) - 2)
    scratch_shapes = (
        [scratch(lead, *shape) for lead, shape in zip(leads, shapes)]
        + [scratch(lead, *shape) for lead, shape in zip(leads, shapes)]
        + [scratch(lead, *piece) for lead, piece in zip(leads, pieces)]
        + [scratch(turns, *piece) for piece in pieces]
        + [scratch(4, *shape) for shape in shapes[:full]]
        + [scratch(4, *piece) for piece in pieces[:full]] * 2
        + [
            scratch(2, row_count, width), scratch(2, row_count, width),
            scratch(2, row_count, width), pltpu.VMEM(weight.shape, F32),
            scratch(4, *shapes[full - 1]), scratch(2, row_count, width),
            scratch(4, row_count, width), scratch(4, row_count, width),
            scratch(2, row_count, width), scratch(2, row_count, width),
            scratch(*late), scratch(size, *early.shape), scratch(size, *late),
            scratch(*early.shape), scratch(*late),
            dma((count,)), dma((count,)), dma((count,)), dma((count,)), dma((count,)),
            dma((count,)), dma((count,)), dma((count, 4, 2)), dma((count, 4, 2)),
            dma((count, turns)), dma((count, turns)), dma((count, 3)), dma((count, 3)),
            dma((count,)), dma((3, 2)), dma((4,)), dma((4,)), dma((2, 2)), dma((2, 2)),
            dma((2, size)), dma((2, size)), dma((2, groups)), dma((2, groups)), dma((4,)),
        ]
    )
    views = [grad.reshape(4, 2, *shape) for grad, shape in zip(grads, shapes)]
    return pl.pallas_call(
        functools.partial(reduce_kernel, shapes, full, size, groups),
        out_shape=[jax.ShapeDtypeStruct(shape, BF16) for shape in shapes]
        + [
            jax.ShapeDtypeStruct(x.shape, F32),
            jax.ShapeDtypeStruct((groups, *early.shape), BF16),
            jax.ShapeDtypeStruct((groups, *late), BF16),
        ],
        in_specs=[pl.BlockSpec(memory_space=pltpu.SMEM)]
        + [anywhere] * (count + 3)
        + [vmem] * 9,
        out_specs=[anywhere] * count + [vmem, anywhere, anywhere],
        scratch_shapes=scratch_shapes,
        compiler_params=pltpu.CompilerParams(
            collective_id=2, has_side_effects=True, vmem_limit_bytes=REDUCE_VMEM
        ),
        name="reduce_all",
        )(
        info, *views, *summed, first, dk, dv, early, dq, weight, positions, *tables, x, g_mid, mods, gain,
    )


def tail_kernel(
    g0_ref, g1_ref, g2_ref, g3_ref, early_ref, late_ref, time_ref, ada_ref,
    o0_ref, o1_ref, o2_ref, o3_ref, g_ada_ref, g_bias_ref, g_time_ref, norm1_ref, norm2_ref, fc1_b_ref,
    fc2_b_ref, mod_ref, cond_ref, turned_ref, full_ref,
):
    for source, target in ((g0_ref, o0_ref), (g1_ref, o1_ref), (g2_ref, o2_ref), (g3_ref, o3_ref)):
        target[...] = source[...].astype(F32)
    me = lax.axis_index("narrow")
    groups, _, width = early_ref.shape
    seqs = time_ref.shape[0]
    vectors = jnp.zeros((16, width), F32)
    norm1 = jnp.zeros((2, width // 2), F32)
    picks = []
    for group in range(groups):
        early = early_ref[group].astype(F32)
        late = late_ref[group].astype(F32)
        vectors = vectors + early[16:32]
        norm1 = norm1 + late[16:18]
        rows = jnp.concatenate(
            [late[4 * at : 4 * at + 4] for at in range(4)] + [early[4 * at : 4 * at + 4] for at in range(4)],
            axis=1,
        )
        mod_ref[4 * group : 4 * group + 4, :] = rows
        sub = lax.broadcasted_iota(jnp.int32, (seqs, TILE), 0).astype(F32)
        lane = lax.broadcasted_iota(jnp.int32, (seqs, TILE), 1)
        pick = jnp.where(jnp.logical_and(sub == early[22:23, :TILE], lane < 4), 1.0, 0.0)
        picks.append(pick)
        cond_ref[4 * group : 4 * group + 4, :] = dot(
            pick.astype(BF16), time_ref[...], ((0,), (0,))
        )[:4]
    g_mod = mod_ref[...]

    def mine(row, size):
        lanes = row.shape[1]
        block = jnp.broadcast_to(row, (8, lanes))
        return pltpu.roll(block, lax.rem(lanes - me * size, lanes), 1)[:1, :size]

    g_bias_ref[...] = mine(jnp.sum(g_mod, axis=0, keepdims=True), g_bias_ref.shape[1])
    norm1_ref[...] = mine(jnp.concatenate([norm1[0:1], norm1[1:2]], axis=1), norm1_ref.shape[1])
    norm2_ref[...] = mine(vectors[0:1], norm2_ref.shape[1])
    fc2_b_ref[...] = mine(vectors[1:2], fc2_b_ref.shape[1])
    fc1_b_ref[...] = mine(
        jnp.concatenate([vectors[2 + at : 3 + at] for at in range(4)], axis=1), fc1_b_ref.shape[1]
    )
    turned_ref[...] = cond_ref[...].T
    own_rows = g_ada_ref.shape[0]
    g_ada_ref[...] = dot(
        turned_ref[pl.ds(pl.multiple_of(me * own_rows, 8), own_rows), :], g_mod, precision=HIGH
    )
    g_cond = dot(g_mod, ada_ref[...].astype(F32), ((1,), (1,)), precision=HIGH)
    total = jnp.zeros((seqs, TILE), F32)
    for group in range(groups):
        part = jnp.concatenate([g_cond[4 * group : 4 * group + 4], jnp.zeros((TILE - 4, TILE), F32)], axis=0)
        total = total + dot(picks[group], part, precision=HIGH)
    full_ref[...] = total
    own_seqs = g_time_ref.shape[0]
    g_time_ref[...] = full_ref[pl.ds(me * own_seqs, own_seqs), :]


def tail(grads, early, late, time_emb, ada, sizes):
    vmem = pl.BlockSpec(memory_space=pltpu.VMEM)
    groups = early.shape[0]
    devices = ada.shape[1] // sizes[2]
    return pl.pallas_call(
        tail_kernel,
        out_shape=[jax.ShapeDtypeStruct(grad.shape, F32) for grad in grads]
        + [
            jax.ShapeDtypeStruct((ada.shape[0] // devices, ada.shape[1]), F32),
            jax.ShapeDtypeStruct((1, sizes[2]), F32),
            jax.ShapeDtypeStruct((time_emb.shape[0] // devices, time_emb.shape[1]), F32),
        ]
        + [jax.ShapeDtypeStruct((1, sizes[which]), F32) for which in (0, 1, 3, 4)],
        in_specs=[vmem] * (len(grads) + 4),
        out_specs=[vmem] * (len(grads) + 7),
        scratch_shapes=[
            pltpu.VMEM((4 * groups, ada.shape[1]), F32),
            pltpu.VMEM((4 * groups, ada.shape[0]), F32),
            pltpu.VMEM((ada.shape[0], 4 * groups), F32),
            pltpu.VMEM(time_emb.shape, F32),
        ],
        compiler_params=pltpu.CompilerParams(vmem_limit_bytes=VMEM_LIMIT),
        name="tail",
    )(*grads, early, late, time_emb, ada)


def body(
    tokens, cotangent, time_emb, seq_table, lengths, positions, norm1_gain, norm2_gain,
    ada_weight, ada_bias, qkv_weight, out_weight, fc1_weight, fc1_bias, fc2_weight, fc2_bias,
):
    row_count, width = tokens.shape
    me = lax.axis_index("narrow")
    size, groups = lax.axis_size("narrow"), lax.axis_size("wide")
    slots = lengths.shape[1]
    below = np.zeros((16, slots), np.int32)
    below[:slots] = np.tril(np.ones((slots, slots), np.int32))
    table = np.zeros((16, slots), np.int32)
    table[8 : 8 + slots] = np.eye(slots, dtype=np.int32)
    info = (
        jnp.sum(
            jnp.asarray(below) * lengths[0][None, :]
            + jnp.asarray(table) * jnp.where(me == 0, seq_table, 0)[None, :],
            axis=1,
        )
        + (jnp.arange(16) == 4) * (me * row_count)
    ).astype(jnp.int32)
    seqs = jnp.pad(seq_table, (0, 8 - slots), constant_values=-1)
    onehot_table = (
        seqs[:, None] == jnp.arange(time_emb.shape[0], dtype=jnp.int32)[None, :]
    ).astype(BF16)
    cond8 = jnp.dot(onehot_table, time_emb, preferred_element_type=F32).astype(BF16)
    tables = tuple(jnp.asarray(t) for t in rotary_constants())
    pieces = (norm1_gain, norm2_gain, ada_bias, fc1_bias, fc2_bias)
    sizes = tuple(piece.size for piece in pieces)

    def spread_gather(shard):
        part = shard.shape[0] // groups
        mine = lax.dynamic_slice_in_dim(shard, lax.axis_index("wide") * part, part, 0)
        return lax.all_gather(mine, ("narrow", "wide"), axis=0, tiled=True)

    out_w, fc1 = (spread_gather(shard) for shard in (out_weight, fc1_weight))
    ada, qkv_w, fc2, x_all, position_all, vectors = gather_all(
        tokens, positions.reshape(-1, TILE), packed(pieces), (ada_weight, qkv_weight, fc2_weight), size
    )
    keys, values, first, queries, norms, mods1, gain1, gain2, bias, fc1_b, fc2_b = project(
        info, x_all, position_all, cond8, ada, vectors, sizes, qkv_w, tables, row_count
    )
    attended, mass = attend(info, queries, keys, values, norms)
    layer_out, g_fc1, g_fc2, g_out, g_att, g_mid, early = mlp(
        info, tokens, attended, cotangent, cond8, ada, bias, gain2, out_w, fc1, fc1_b, fc2, fc2_b
    )
    dq, dk, dv = attend_back(info, queries, keys, values, g_att, attended, mass)
    g_fc1 = lax.psum_scatter(g_fc1, "narrow", scatter_dimension=0, tiled=True)
    g_fc2, g_out, g_qkv, g_fc1, grad_tokens, early_all, late_all = reduce_all(
        info, (g_fc2, g_out), (g_fc1,), first, dk, dv, early, dq, qkv_w, position_all, tables, tokens,
        g_mid, mods1, gain1, size, groups,
    )
    g_fc2, g_out, g_qkv, g_fc1, g_ada, g_ada_bias, g_time, g_norm1, g_norm2, g_fc1_b, g_fc2_b = tail(
        (g_fc2, g_out, g_qkv, g_fc1), early_all, late_all, time_emb, ada, sizes
    )
    return (
        layer_out, grad_tokens, g_time, g_norm1[0], g_norm2[0], g_ada, g_ada_bias[0], g_qkv, g_out,
        g_fc1, g_fc1_b[0], g_fc2, g_fc2_b[0],
    )


def solution(mesh):
    both = P(("wide", "narrow"), None)
    row = P("narrow")
    table = P("narrow", None)
    return jax.shard_map(
        body,
        mesh=mesh,
        in_specs=(
            both, both, P(), P("wide"), P("wide", None), P(("wide", "narrow")), row, row,
            table, row, table, table, table, row, table, row,
        ),
        out_specs=(both, both, table, row, row, table, row, table, table, table, row, table, row),
        check_vma=False,
    )
```

```python
import functools
import math

import jax
import jax.numpy as jnp
import numpy as np
from jax import lax
from jax.experimental import pallas as pl
from jax.experimental.pallas import tpu as pltpu
from jax.sharding import PartitionSpec as P

HEADS = 12
HEAD_DIM = 64
EPSILON = 1e-05
FAR = -(2.0**100)
SAFE = 64.0
LIFT = 20.0
F32 = jnp.float32
BF16 = jnp.bfloat16
HIGH = lax.Precision.HIGHEST
VMEM_LIMIT = 56 * 2**20
REDUCE_VMEM = 63 * 2**20
TILE = 128
QUERY_ROWS = 256
KEY_ROWS = 256
BLOCK = 512
CHUNK = 768


def params(grid_dims=1):
    return pltpu.CompilerParams(
        dimension_semantics=("arbitrary",) * grid_dims, vmem_limit_bytes=VMEM_LIMIT
    )


def dot(left, right, contract=((1,), (0,)), precision=None):
    return lax.dot_general(
        left, right, (contract, ((), ())), preferred_element_type=F32, precision=precision
    )


def thirds(values):
    high = values.astype(BF16)
    rest = values - high.astype(F32)
    middle = rest.astype(BF16)
    low = (rest - middle.astype(F32)).astype(BF16)
    return high, middle, low


def slot_of(rows, info):
    zero = jnp.zeros_like(rows)
    slot = zero
    for which in range(3):
        slot = slot + jnp.where(rows >= info[which], 1, zero)
    return slot


def scalar_slot(row, info):
    slot = jnp.int32(0)
    for which in range(3):
        slot = slot + jnp.where(row >= info[which], 1, 0)
    return slot


def key_range(first, last, info):
    low_slot = scalar_slot(first, info)
    high_slot = scalar_slot(last, info)
    start = jnp.where(
        low_slot == 0, 0, jnp.where(low_slot == 1, info[0], jnp.where(low_slot == 2, info[1], info[2]))
    )
    end = jnp.where(
        high_slot == 0,
        info[0],
        jnp.where(high_slot == 1, info[1], jnp.where(high_slot == 2, info[2], info[3])),
    )
    return start, end


def active_range(info):
    start, end = key_range(info[4], info[4] + BLOCK - 1, info)
    return start // BLOCK, (end - 1) // BLOCK


def block_active(block, info):
    low, high = active_range(info)
    return jnp.logical_and(block >= low, block <= high)


def active_rows(block, info):
    low, high = active_range(info)
    return jnp.clip(block, low, high), 0


def slot_picks(row_count, first_row, info):
    rows = first_row + lax.broadcasted_iota(jnp.int32, (row_count, 16), 0)
    lane = lax.broadcasted_iota(jnp.int32, (row_count, 16), 1)
    return jnp.where(
        jnp.logical_and(slot_of(rows, info) == lane % 4, lane < 12), 1.0, 0.0
    ).astype(BF16)


def pick_table(values):
    high, middle, low = thirds(values)
    zero = jnp.zeros_like(high[:4])
    return jnp.concatenate([high[:4], middle[:4], low[:4], zero], axis=0)


def normed(values):
    center = values - jnp.mean(values, axis=1, keepdims=True)
    spread = jnp.mean(center * center, axis=1, keepdims=True)
    inverse = lax.rsqrt(spread + EPSILON)
    return center * inverse, inverse


def rotary_constants():
    half = HEAD_DIM // 2
    inverse = 10000.0 ** (-(np.arange(half, dtype=np.float64) * 2.0) / HEAD_DIM)
    inverse = inverse.astype(np.float32).astype(np.float64)
    tables = []
    for count, step in ((128, 64), (64, 1)):
        angles = (np.arange(count, dtype=np.float64) * step)[:, None] * inverse[None, :]
        full = np.concatenate(
            [np.tile(np.cos(angles), (1, 4)), np.tile(np.sin(angles), (1, 4))], axis=1
        ).astype(np.float32)
        high = full.astype(jnp.bfloat16)
        low = (full - high.astype(np.float32)).astype(jnp.bfloat16)
        tables.append(np.concatenate([high, low], axis=1))
    return tables


def rotary(positions, coarse_ref, fine_ref):
    count = positions.size
    parts = []
    for picks, table in ((positions // 64, coarse_ref), (positions % 64, fine_ref)):
        depth = table.shape[0]
        sub = lax.broadcasted_iota(jnp.int32, (depth, TILE), 0)
        onehot = jnp.concatenate(
            [(sub == picks[at : at + 1, :]).astype(F32) for at in range(positions.shape[0])], axis=1
        )
        both = dot(onehot.astype(BF16), table[...], ((0,), (0,)))
        parts.append(both[:, :256] + both[:, 256:])
    coarse, fine = parts
    cosine = coarse[:, :128] * fine[:, :128] - coarse[:, 128:] * fine[:, 128:]
    sine = coarse[:, 128:] * fine[:, :128] + coarse[:, :128] * fine[:, 128:]
    lane = lax.broadcasted_iota(jnp.int32, (count, TILE), 1)
    return cosine, jnp.where(lane % 64 < 32, -sine, sine)


def swapped(values):
    lane = lax.broadcasted_iota(jnp.int32, values.shape, 1)
    return jnp.where(
        lane % 64 < 32, pltpu.roll(values, TILE - 32, 1), pltpu.roll(values, 32, 1)
    )


def turn(values, cosine, sine):
    return values * cosine + swapped(values) * sine


def turn_back(values, cosine, sine):
    return values * cosine - swapped(values) * sine


def packed(pieces):
    starts = np.cumsum([0] + [-(-piece.size // TILE) * TILE for piece in pieces])
    whole = -(-starts[-1] // (16 * TILE)) * 16 * TILE
    rows = [
        jnp.pad(piece, (start, whole - start - piece.size)) for piece, start in zip(pieces, starts)
    ]
    return functools.reduce(jnp.add, rows).reshape(-1, TILE)


def joined(vector_ref, row, size):
    devices = vector_ref.shape[0]
    rows = -(-size // TILE)
    room = -(-(devices - 1) * size // TILE) + rows
    total = jnp.zeros((8, room * TILE), F32)
    for device in range(devices):
        block = vector_ref[device].astype(F32)
        lanes = [block[row + at : row + at + 1, :] for at in range(rows)]
        line = jnp.concatenate(lanes, axis=1)
        line = jnp.concatenate([line, jnp.zeros((1, (room - rows) * TILE), F32)], axis=1)
        line = jnp.broadcast_to(line, (8, room * TILE))
        total = total + (pltpu.roll(line, device * size, 1) if device else line)
    return total[:1, : devices * size]


def project_kernel(
    sizes, info, x_ref, position_ref, cond_ref, ada_ref, vector_ref, weight_ref, coarse_ref,
    fine_ref, keys_ref, values_ref, first_ref, query_ref, norm_ref, mods_ref, gain_ref, gain2_ref,
    bias_ref, fc1_b_ref, fc2_b_ref, table_ref,
):
    block = pl.program_id(0)
    width = x_ref.shape[1]
    row_count = query_ref.shape[0]

    @pl.when(block == 0)
    def _():
        row = 0
        for out_ref, size in zip((gain_ref, gain2_ref, bias_ref, fc1_b_ref, fc2_b_ref), sizes):
            out_ref[...] = joined(vector_ref, row, size)
            row += -(-size // TILE)
        modulation = dot(cond_ref[...], ada_ref[...]) + bias_ref[:, : 2 * width]
        mods_ref[...] = modulation
        scale = (1.0 + modulation[:, width:]) * gain_ref[...]
        table_ref[:, :width] = pick_table(scale)
        table_ref[:, width:] = pick_table(modulation[:, :width])
        norm_ref[...] = jnp.zeros_like(norm_ref)

    def most_square(values):
        row = lax.broadcasted_iota(jnp.int32, (width, TILE), 0)
        lane = lax.broadcasted_iota(jnp.int32, (width, TILE), 1)
        heads = jnp.where(row // HEAD_DIM == lane, 1.0, 0.0).astype(BF16)
        return jnp.max(dot((values * values).astype(BF16), heads), axis=0, keepdims=True)

    @pl.when(jnp.logical_not(block_active(block, info)))
    def _():
        first_ref[...] = jnp.zeros_like(first_ref)

    @pl.when(block_active(block, info))
    def _():
        x = x_ref[...].astype(F32)
        picks = slot_picks(BLOCK, block * BLOCK, info)
        mods = dot(picks, table_ref[...])
        xh, _ = normed(x)
        first = (xh * mods[:, :width] + mods[:, width:]).astype(BF16)
        first_ref[...] = first
        cosine, sine = rotary(position_ref[block], coarse_ref, fine_ref)
        keys = dot(first, weight_ref[:, width : 2 * width])
        norm_ref[0:1, :] = jnp.maximum(norm_ref[0:1, :], most_square(keys) * 1.02)
        for tile in range(width // TILE):
            cut = slice(tile * TILE, (tile + 1) * TILE)
            keys_ref[:, cut] = turn(keys[:, cut], cosine, sine).astype(BF16)
        values_ref[...] = dot(first, weight_ref[:, 2 * width :]).astype(BF16)

        @pl.when(block * BLOCK == info[4])
        def _():
            queries = dot(first, weight_ref[:, :width])
            for tile in range(width // TILE):
                cut = slice(tile * TILE, (tile + 1) * TILE)
                turned = turn(queries[:, cut], cosine, sine).astype(BF16)
                query_ref[:, cut] = (turned.astype(F32) * HEAD_DIM**-0.5).astype(BF16)


def project(info, x_all, positions, cond, ada, vectors, sizes, weight, tables, row_count):
    total, width = x_all.shape
    rows = pl.BlockSpec((BLOCK, width), active_rows)

    def whole(array):
        return pl.BlockSpec(array.shape, lambda i, *_: (0,) * array.ndim)

    shape = jax.ShapeDtypeStruct((total, width), BF16)
    lengths = [vectors.shape[0] * size for size in sizes]
    return pl.pallas_call(
        functools.partial(project_kernel, sizes),
        grid_spec=pltpu.PrefetchScalarGridSpec(
            num_scalar_prefetch=1,
            grid=(total // BLOCK,),
            in_specs=[
                rows,
                whole(positions),
                whole(cond),
                pl.BlockSpec((ada.shape[0], 2 * width), lambda i, *_: (0, 0)),
                whole(vectors),
                whole(weight),
                whole(tables[0]),
                whole(tables[1]),
            ],
            out_specs=[
                rows,
                rows,
                pl.BlockSpec((BLOCK, width), lambda i, *_: (i, 0)),
                pl.BlockSpec((row_count, width), lambda i, *_: (0, 0)),
                pl.BlockSpec((8, TILE), lambda i, *_: (0, 0)),
                pl.BlockSpec((8, 2 * width), lambda i, *_: (0, 0)),
            ]
            + [pl.BlockSpec((1, count), lambda i, *_: (0, 0)) for count in lengths],
            scratch_shapes=[pltpu.VMEM((16, 2 * width), BF16)],
        ),
        out_shape=[
            shape, shape, shape, jax.ShapeDtypeStruct((row_count, width), BF16),
            jax.ShapeDtypeStruct((8, TILE), F32),
            jax.ShapeDtypeStruct((8, 2 * width), F32),
        ]
        + [jax.ShapeDtypeStruct((1, count), F32) for count in lengths],
        compiler_params=params(),
        name="project",
    )(info, x_all, positions, cond, ada, vectors, weight, *tables)


def fill_key_features(feature_ref, info):
    total = feature_ref.shape[0]

    @pl.loop(0, total // KEY_ROWS)
    def _(chunk):
        start = pl.multiple_of(chunk * KEY_ROWS, KEY_ROWS)
        rows = start + lax.broadcasted_iota(jnp.int32, (KEY_ROWS, TILE), 0)
        lane = lax.broadcasted_iota(jnp.int32, (KEY_ROWS, TILE), 1)
        slot = slot_of(rows, info)
        masked = jnp.where(slot == lane, 0.0, FAR)
        ones = jnp.where(lane < 8, 1.0, 0.0)
        feature_ref[pl.ds(start, KEY_ROWS), :] = jnp.where(lane < 4, masked, ones).astype(BF16)


def stacked_heads(flipped):
    sub = lax.broadcasted_iota(jnp.int32, flipped.shape, 0)
    zero = jnp.zeros_like(flipped)
    return jnp.concatenate(
        [jnp.where(sub < HEAD_DIM, flipped, zero), jnp.where(sub < HEAD_DIM, zero, flipped)],
        axis=1,
    )


def slot_rows(first, count, info):
    sub = lax.broadcasted_iota(jnp.int32, (TILE, 2 * count), 0)
    lane = lax.broadcasted_iota(jnp.int32, (TILE, 2 * count), 1)
    return jnp.where(slot_of(first + lane % count, info) == sub, 1.0, 0.0), sub


def spans(low, count, step, carried, most):
    span = most
    while span:
        times = count // span
        carried = lax.fori_loop(0, times, functools.partial(step, span, low), carried)
        low = low + times * span
        count = count - times * span
        span //= 2
    return carried


def chunk_rows(chunk):
    return pl.ds(pl.multiple_of(chunk * KEY_ROWS, KEY_ROWS), KEY_ROWS)


def with_parts(base, sub, row):
    for place, piece in enumerate(thirds(row)):
        base = jnp.where(sub == 4 + place, piece.astype(F32), base)
    return base


def attend_kernel(
    info, q_ref, k_ref, v_ref, norm_ref, out_ref, mass_ref, feature_ref, sum_ref, row_ref
):
    pair = pl.program_id(0)

    @pl.when(pair == 0)
    def _():
        fill_key_features(feature_ref, info)

    row_count = q_ref.shape[0]
    wide = 2 * QUERY_ROWS
    head = lax.broadcasted_iota(jnp.int32, (1, TILE), 1)
    longest = [
        jnp.sqrt(jnp.max(jnp.where(head == 2 * pair + which, norm_ref[0:1, :], 0.0), axis=1, keepdims=True))
        for which in range(2)
    ]
    for part in range(row_count // QUERY_ROWS):
        first = info[4] + part * QUERY_ROWS
        cut = pl.ds(part * QUERY_ROWS, QUERY_ROWS)
        flipped = q_ref[cut, :].astype(F32).T
        onehot, sub = slot_rows(first, QUERY_ROWS, info)
        stack = stacked_heads(flipped)
        start, end = key_range(first, first + QUERY_ROWS - 1, info)
        low = start // KEY_ROWS
        count = (end + KEY_ROWS - 1) // KEY_ROWS - low
        sum_ref[...] = jnp.zeros_like(sum_ref)

        def scores_of(rows, queries):
            return dot(jnp.concatenate([k_ref[rows, :], feature_ref[rows, :]], axis=1), queries)

        own_rows = chunk_rows(first // KEY_ROWS)
        near = jnp.max(
            scores_of(own_rows, jnp.concatenate([stack, onehot], axis=0).astype(BF16)),
            axis=0, keepdims=True,
        )
        square = flipped * flipped
        bound = jnp.concatenate(
            [
                jnp.sqrt(jnp.sum(square[:HEAD_DIM], axis=0, keepdims=True)) * longest[0],
                jnp.sqrt(jnp.sum(square[HEAD_DIM:], axis=0, keepdims=True)) * longest[1],
            ],
            axis=1,
        )
        shift = near + LIFT
        narrow_range = jnp.max(bound - shift) < SAFE
        queries = jnp.concatenate([stack, with_parts(onehot, sub, -shift)], axis=0).astype(BF16)

        @pl.when(narrow_range)
        def _():
            def step(span, base, index, mass):
                weights, values = [], []
                for inner in range(span):
                    rows = chunk_rows(base + index * span + inner)
                    part_weights = jnp.exp(scores_of(rows, queries))
                    mass = mass + jnp.sum(part_weights, axis=0, keepdims=True)
                    weights.append(part_weights.astype(BF16))
                    values.append(v_ref[rows, :])
                sum_ref[...] += dot(
                    jnp.concatenate(values, axis=0), jnp.concatenate(weights, axis=0), ((0,), (0,))
                )
                return mass

            row_ref[0:1, :] = shift
            row_ref[1:2, :] = spans(low, count, step, jnp.zeros((1, wide), F32), 8)

        @pl.when(jnp.logical_not(narrow_range))
        def _():
            def step(span, base, index, carried):
                most, mass = carried
                scores, values = [], []
                new_most = most
                for inner in range(span):
                    rows = chunk_rows(base + index * span + inner)
                    some = scores_of(rows, queries)
                    new_most = jnp.maximum(new_most, jnp.max(some, axis=0, keepdims=True))
                    scores.append(some)
                    values.append(v_ref[rows, :])
                shrink = jnp.exp(most - new_most)
                mass = mass * shrink
                weights = []
                for some in scores:
                    part_weights = jnp.exp(some - new_most)
                    mass = mass + jnp.sum(part_weights, axis=0, keepdims=True)
                    weights.append(part_weights.astype(BF16))
                sum_ref[...] = sum_ref[...] * shrink + dot(
                    jnp.concatenate(values, axis=0), jnp.concatenate(weights, axis=0), ((0,), (0,))
                )
                return new_most, mass

            most, mass = spans(
                low, count, step, (jnp.full((1, wide), FAR * 2, F32), jnp.zeros((1, wide), F32)), 4
            )
            row_ref[0:1, :] = most + shift
            row_ref[1:2, :] = mass

        mass = row_ref[1:2, :]
        result = sum_ref[...] / mass
        joined = jnp.concatenate(
            [result[:HEAD_DIM, :QUERY_ROWS], result[HEAD_DIM:, QUERY_ROWS:]], axis=0
        )
        out_ref[cut, :] = joined.T
        mass_ref[0, pl.ds(part, 1), :] = row_ref[0:1, :] + jnp.log(mass)


def attend(info, queries, keys, values, norms):
    row_count, width = queries.shape
    total = keys.shape[0]
    pairs = width // TILE
    parts = row_count // QUERY_ROWS
    narrow = pl.BlockSpec((row_count, TILE), lambda i, *_: (0, i))
    tall = pl.BlockSpec((total, TILE), lambda i, *_: (0, i))
    return pl.pallas_call(
        attend_kernel,
        grid_spec=pltpu.PrefetchScalarGridSpec(
            num_scalar_prefetch=1,
            grid=(pairs,),
            in_specs=[narrow, tall, tall, pl.BlockSpec(norms.shape, lambda i, *_: (0, 0))],
            out_specs=[
                narrow,
                pl.BlockSpec((1, parts, 2 * QUERY_ROWS), lambda i, *_: (i, 0, 0)),
            ],
            scratch_shapes=[
                pltpu.VMEM((total, TILE), BF16),
                pltpu.VMEM((TILE, 2 * QUERY_ROWS), F32),
                pltpu.VMEM((8, 2 * QUERY_ROWS), F32),
            ],
        ),
        out_shape=[
            jax.ShapeDtypeStruct((row_count, width), F32),
            jax.ShapeDtypeStruct((pairs, parts, 2 * QUERY_ROWS), F32),
        ],
        compiler_params=params(),
        name="attend",
    )(info, queries, keys, values, norms)


def attend_back_kernel(
    info, q_ref, k_ref, v_ref, grad_ref, out_ref, mass_ref, dq_ref, dk_ref, dv_ref,
    feature_ref, dk_sum, dv_sum, dq_sum,
):
    @pl.when(pl.program_id(0) == 0)
    def _():
        fill_key_features(feature_ref, info)

    row_count = q_ref.shape[0]
    total = k_ref.shape[0]
    low_block, high_block = active_range(info)
    for block in range(total // BLOCK):

        @pl.when(jnp.logical_and(block >= low_block, block <= high_block))
        def _():
            rows = pl.ds(block * BLOCK, BLOCK)
            dk_sum[rows, :] = jnp.zeros((BLOCK, TILE), F32)
            dv_sum[rows, :] = jnp.zeros((BLOCK, TILE), F32)

    for part in range(row_count // QUERY_ROWS):
        first = info[4] + part * QUERY_ROWS
        cut = pl.ds(part * QUERY_ROWS, QUERY_ROWS)
        q_rows = q_ref[cut, :].astype(F32)
        g_rows = grad_ref[cut, :].astype(F32)
        q_flip = q_rows.T
        g_flip = g_rows.T
        product = g_flip * out_ref[cut, :].T
        delta = jnp.concatenate(
            [
                jnp.sum(product[:HEAD_DIM], axis=0, keepdims=True),
                jnp.sum(product[HEAD_DIM:], axis=0, keepdims=True),
            ],
            axis=1,
        )
        onehot, sub = slot_rows(first, QUERY_ROWS, info)

        queries = jnp.concatenate(
            [stacked_heads(q_flip), with_parts(onehot, sub, -mass_ref[0, pl.ds(part, 1), :])], axis=0
        ).astype(BF16)
        grads = jnp.concatenate(
            [stacked_heads(g_flip), with_parts(jnp.zeros_like(onehot), sub, -delta)], axis=0
        ).astype(BF16)
        lane = lax.broadcasted_iota(jnp.int32, (QUERY_ROWS, TILE), 1)

        def stacked(rows):
            zero = jnp.zeros_like(rows)
            return jnp.concatenate(
                [jnp.where(lane < HEAD_DIM, rows, zero), jnp.where(lane < HEAD_DIM, zero, rows)],
                axis=0,
            ).astype(BF16)

        q_stack = stacked(q_rows)
        g_stack = stacked(g_rows)
        start, end = key_range(first, first + QUERY_ROWS - 1, info)
        dq_sum[...] = jnp.zeros_like(dq_sum)

        def step(span, base, index, carried):
            all_keys, all_grads = [], []
            for inner in range(span):
                rows = chunk_rows(base + index * span + inner)
                keys = k_ref[rows, :]
                features = feature_ref[rows, :]
                probs = jnp.exp(dot(jnp.concatenate([keys, features], axis=1), queries))
                change = dot(jnp.concatenate([v_ref[rows, :], features], axis=1), grads)
                grad_scores = (probs * change).astype(BF16)
                dv_sum[rows, :] += dot(probs.astype(BF16), g_stack)
                dk_sum[rows, :] += dot(grad_scores, q_stack)
                all_keys.append(keys)
                all_grads.append(grad_scores)
            dq_sum[...] += dot(
                jnp.concatenate(all_keys, axis=0), jnp.concatenate(all_grads, axis=0), ((0,), (0,))
            )
            return carried

        low = start // KEY_ROWS
        spans(low, (end + KEY_ROWS - 1) // KEY_ROWS - low, step, 0, 8)
        result = dq_sum[...]
        joined = jnp.concatenate(
            [result[:HEAD_DIM, :QUERY_ROWS], result[HEAD_DIM:, QUERY_ROWS:]], axis=0
        )
        dq_ref[cut, :] = joined.T * HEAD_DIM**-0.5

    for block in range(total // BLOCK):

        @pl.when(jnp.logical_and(block >= low_block, block <= high_block))
        def _():
            rows = pl.ds(block * BLOCK, BLOCK)
            dk_ref[rows, :] = dk_sum[rows, :].astype(BF16)
            dv_ref[rows, :] = dv_sum[rows, :].astype(BF16)

        @pl.when(jnp.logical_or(block < low_block, block > high_block))
        def _():
            rows = pl.ds(block * BLOCK, BLOCK)
            dk_ref[rows, :] = jnp.zeros((BLOCK, TILE), BF16)
            dv_ref[rows, :] = jnp.zeros((BLOCK, TILE), BF16)


def attend_back(info, queries, keys, values, grads, attended, mass):
    row_count, width = queries.shape
    total = keys.shape[0]
    pairs = width // TILE
    parts = row_count // QUERY_ROWS
    narrow = pl.BlockSpec((row_count, TILE), lambda i, *_: (0, i))
    tall = pl.BlockSpec((total, TILE), lambda i, *_: (0, i))
    return pl.pallas_call(
        attend_back_kernel,
        grid_spec=pltpu.PrefetchScalarGridSpec(
            num_scalar_prefetch=1,
            grid=(pairs,),
            in_specs=[
                narrow,
                tall,
                tall,
                narrow,
                narrow,
                pl.BlockSpec((1, parts, 2 * QUERY_ROWS), lambda i, *_: (i, 0, 0)),
            ],
            out_specs=[narrow, tall, tall],
            scratch_shapes=[
                pltpu.VMEM((total, TILE), BF16),
                pltpu.VMEM((total, TILE), F32),
                pltpu.VMEM((total, TILE), F32),
                pltpu.VMEM((TILE, 2 * QUERY_ROWS), F32),
            ],
        ),
        out_shape=[
            jax.ShapeDtypeStruct((row_count, width), F32),
            jax.ShapeDtypeStruct((total, width), BF16),
            jax.ShapeDtypeStruct((total, width), BF16),
        ],
        compiler_params=params(),
        name="attend_back",
    )(info, queries, keys, values, grads, attended, mass)


def slot_sums(first_row, info, values):
    count, width = values.shape
    slot = slot_of(first_row + lax.broadcasted_iota(jnp.int32, (count, TILE), 0), info)
    sums = []
    for which in range(4):
        mask = jnp.where(slot == which, 1.0, 0.0)
        wide_mask = jnp.concatenate([mask] * (width // TILE), axis=1)
        sums.append(jnp.sum(values * wide_mask, axis=0, keepdims=True))
    return jnp.concatenate(sums + [jnp.zeros((4, width), F32)], axis=0)


def mlp_kernel(
    info, x_ref, attended_ref, cot_ref, cond_ref, ada_ref, bias_ref, gain_ref, out_w_ref,
    fc1_ref, fc1_b_ref, fc2_ref, fc2_b_ref,
    layer_ref, g_fc1_ref, g_fc2_ref, g_out_ref, g_att_ref, g_mid_ref, early_ref,
    pack_ref, mods_ref, second_ref, second_t_ref, grad2_ref, branch_ref, middle_ref, xh_ref, inverse_ref,
    sum2_ref, gsum_ref,
):
    step = pl.program_id(0)
    width = x_ref.shape[1]
    row_count = x_ref.shape[0]
    first_row = info[4]

    def mod(which):
        picks = slot_picks(row_count, first_row, info)
        return dot(picks, mods_ref[:, which * width : (which + 1) * width])

    @pl.when(step == 0)
    def _():
        mods = dot(cond_ref[...], ada_ref[:, 2 * width :]) + bias_ref[:, 2 * width :]
        mods_ref[:, : 4 * width] = pick_table(mods)
        mods_ref[:, 4 * width :] = pick_table(
            (1.0 + mods[:, 2 * width : 3 * width]) * gain_ref[...]
        )
        attended_low = attended_ref[...].astype(BF16)
        branch = dot(attended_low, out_w_ref[...])
        branch_ref[...] = branch
        middle = x_ref[...].astype(F32) + mod(0) * branch
        middle_ref[...] = middle
        xh, inverse = normed(middle)
        xh_ref[...] = xh
        inverse_ref[...] = jnp.broadcast_to(inverse, inverse_ref.shape)
        second = xh * mod(4) + mod(1)
        second_ref[...] = second.astype(BF16)
        second_t_ref[...] = second.T.astype(BF16)
        grad2 = (cot_ref[...].astype(F32) * mod(3)).astype(BF16)
        grad2_ref[...] = grad2
        pack_ref[...] = jnp.zeros_like(pack_ref)
        pack_ref[17:18, :] = jnp.sum(grad2.astype(F32), axis=0, keepdims=True)
        lane = lax.broadcasted_iota(jnp.int32, (1, width), 1)
        table = jnp.zeros((1, width), F32)
        for slot in range(4):
            table = jnp.where(lane == slot, info[8 + slot].astype(F32), table)
        pack_ref[22:23, :] = table
        sum2_ref[...] = jnp.zeros_like(sum2_ref)
        gsum_ref[...] = jnp.zeros_like(gsum_ref)

    pre = dot(second_ref[...], fc1_ref[...]) + fc1_b_ref[...]
    root = math.sqrt(2.0 / math.pi)
    square = pre * pre
    bend = jnp.tanh(root * pre * (1.0 + 0.044715 * square))
    half = 0.5 * (1.0 + bend)
    act = (pre * half).astype(BF16)
    slope = half + 0.5 * pre * (1.0 - bend * bend) * (root * (1.0 + 0.134145 * square))
    sum2_ref[...] += dot(act, fc2_ref[...])
    grad_act = dot(grad2_ref[...], fc2_ref[...], ((1,), (1,)))
    grad_pre = (grad_act * slope).astype(BF16)
    pack_ref[pl.ds(18 + step, 1), :] = jnp.sum(grad_pre.astype(F32), axis=0, keepdims=True)
    g_fc2_ref[...] = dot(act, grad2_ref[...], ((0,), (0,))).astype(BF16)
    g_fc1_ref[...] = dot(second_t_ref[...], grad_pre).astype(BF16)
    gsum_ref[...] += dot(grad_pre, fc1_ref[...], ((1,), (1,)))

    @pl.when(step == pl.num_programs(0) - 1)
    def _():
        branch2 = sum2_ref[...] + fc2_b_ref[...]
        layer_ref[...] = (middle_ref[...] + mod(3) * branch2).astype(BF16)
        upstream = cot_ref[...].astype(F32)
        pack_ref[12:16, :] = slot_sums(first_row, info, upstream * branch2)[:4]
        grad = gsum_ref[...]
        xh = xh_ref[...]
        picks = slot_picks(row_count, first_row, info)
        pack_ref[4:8, :] = slot_sums(first_row, info, grad)[:4]
        moved = grad * xh
        pack_ref[8:12, :] = slot_sums(first_row, info, moved * gain_ref[...])[:4]
        pack_ref[16:17, :] = jnp.sum(moved * (1.0 + mod(2)), axis=0, keepdims=True)
        h = grad * mod(4)
        inverse = inverse_ref[:, 0:1]
        g_mid = upstream + inverse * (
            h - jnp.mean(h, axis=1, keepdims=True) - xh * jnp.mean(h * xh, axis=1, keepdims=True)
        )
        g_mid_ref[...] = g_mid
        pack_ref[0:4, :] = slot_sums(first_row, info, g_mid * branch_ref[...])[:4]
        early_ref[...] = pack_ref[...].astype(BF16)
        g_branch = (g_mid * mod(0)).astype(BF16)
        g_out_ref[...] = dot(attended_ref[...].astype(BF16), g_branch, ((0,), (0,))).astype(BF16)
        g_att_ref[...] = dot(g_branch, out_w_ref[...], ((1,), (1,))).astype(BF16)


def mlp(info, x, attended, cot, cond, ada, bias, gain, out_w, fc1, fc1_b, fc2, fc2_b):
    row_count, width = x.shape
    hidden = fc1.shape[1]
    chunk = CHUNK

    def whole(shape):
        return pl.BlockSpec(shape, lambda i, *_: (0,) * len(shape))

    columns = pl.BlockSpec((width, chunk), lambda i, *_: (0, i))
    lines = pl.BlockSpec((chunk, width), lambda i, *_: (i, 0))
    part = pl.BlockSpec((1, chunk), lambda i, *_: (0, i))
    rows = (row_count, width)
    return pl.pallas_call(
        mlp_kernel,
        grid_spec=pltpu.PrefetchScalarGridSpec(
            num_scalar_prefetch=1,
            grid=(hidden // chunk,),
            in_specs=[
                whole(rows), whole(rows), whole(rows), whole(cond.shape), whole(ada.shape),
                whole(bias.shape), whole(gain.shape), whole(out_w.shape), columns, part, lines,
                whole(fc2_b.shape),
            ],
            out_specs=[
                whole(rows), columns, lines, whole(out_w.shape), whole(rows), whole(rows),
                whole((32, width)),
            ],
            scratch_shapes=[
                pltpu.VMEM((32, width), F32),
                pltpu.VMEM((16, 5 * width), BF16),
                pltpu.VMEM(rows, BF16),
                pltpu.VMEM((width, row_count), BF16),
                pltpu.VMEM(rows, BF16),
                pltpu.VMEM(rows, F32),
                pltpu.VMEM(rows, F32),
                pltpu.VMEM(rows, F32),
                pltpu.VMEM((row_count, TILE), F32),
                pltpu.VMEM(rows, F32),
                pltpu.VMEM(rows, F32),
            ],
        ),
        out_shape=[
            jax.ShapeDtypeStruct(rows, BF16),
            jax.ShapeDtypeStruct(fc1.shape, BF16),
            jax.ShapeDtypeStruct(fc2.shape, BF16),
            jax.ShapeDtypeStruct(out_w.shape, BF16),
            jax.ShapeDtypeStruct(rows, BF16),
            jax.ShapeDtypeStruct(rows, F32),
            jax.ShapeDtypeStruct((32, width), BF16),
        ],
        compiler_params=params(),
        name="mlp",
    )(info, x, attended, cot, cond, ada, bias, gain, out_w, fc1, fc1_b, fc2, fc2_b)


MESH = pl.DeviceIdType.MESH


def piece_of(array, which):
    rows, columns = array
    if rows % 32 == 0 and (columns // 2) % TILE == 0:
        return (which % 2) * (rows // 2), rows // 2, (which // 2) * (columns // 2), columns // 2
    return 0, rows, which * (columns // 4), columns // 4


def cut_of(start, size, whole, unit):
    if size == whole:
        return slice(None)
    return pl.ds(pl.multiple_of(start, unit), size)


class Place:
    def __init__(self):
        self.wide = lax.axis_index("wide")
        self.narrow = lax.axis_index("narrow")
        self.z = self.narrow // 2
        self.core = self.narrow % 2
        self.quarter = self.wide % 4
        self.bit1 = 1 + self.core
        self.bit2 = 2 - self.core
        self.near = self.z + 1 - 2 * (self.z % 2)
        low = self.z < 2
        self.order = (self.near, jnp.where(low, 2, 1), jnp.where(low, 3, 0))

    def flip(self, value, bit):
        return value + bit * (1 - 2 * ((value // bit) % 2))

    def partner(self, bit):
        return (self.flip(self.wide, bit), self.narrow)

    def sibling(self):
        return (self.wide, self.narrow + 1 - 2 * self.core)

    def column(self, narrow):
        return (self.wide, narrow)

    def up(self):
        return (self.wide, jnp.minimum(self.narrow + 2, 7))

    def down(self):
        return (self.wide, jnp.maximum(self.narrow - 2, 0))


def greet(place, size):
    barrier = pltpu.get_barrier_semaphore()
    for step in range(1, size):
        pl.semaphore_signal(
            barrier, inc=1, device_id=place.column((place.narrow + step) % size), device_id_type=MESH
        )
    for bit in (1, 2):
        pl.semaphore_signal(barrier, inc=1, device_id=place.partner(bit), device_id_type=MESH)
    pl.semaphore_wait(barrier, size + 1)


def gather_kernel(shapes, size, *refs):
    count = len(shapes)
    shard_refs = refs[:count]
    x_ref, position_ref, vector_ref = refs[count : count + 3]
    full_refs = refs[count + 3 : 2 * count + 3]
    x_all, position_all, vector_all = refs[2 * count + 3 : 2 * count + 6]
    (
        own_sems, own_send, own_recv, line_send, line_recv, turn_send, turn_recv, next_send,
        next_recv, back_send, back_recv, small_send, small_recv,
    ) = refs[2 * count + 6 :]
    place = Place()
    narrow, z, core = place.narrow, place.z, place.core
    greet(place, size)

    def remote(source, target, send, recv, device):
        return pltpu.make_async_remote_copy(
            src_ref=source, dst_ref=target, send_sem=send, recv_sem=recv, device_id=device,
            device_id_type=MESH,
        )

    def region(a, owner, which):
        rows, columns = shapes[a]
        first_row, row_count, first_column, column_count = piece_of(shapes[a], which)
        start = pl.multiple_of(owner * rows + first_row, 16)
        if isinstance(first_column, int):
            return full_refs[a].at[pl.ds(start, row_count), :]
        lanes = pl.ds(pl.multiple_of(first_column, TILE), column_count)
        return full_refs[a].at[pl.ds(start, row_count), lanes]

    def shard(a, owner):
        rows, _ = shapes[a]
        return full_refs[a].at[pl.ds(pl.multiple_of(owner * rows, 16), rows), :]

    def own_piece(a):
        first_row, row_count, first_column, column_count = piece_of(shapes[a], place.quarter)
        if isinstance(first_row, int) and first_row == 0:
            rows = slice(None)
        else:
            rows = pl.ds(pl.multiple_of(first_row, 16), row_count)
        if isinstance(first_column, int):
            return shard_refs[a].at[rows, :]
        return shard_refs[a].at[rows, pl.ds(pl.multiple_of(first_column, TILE), column_count)]

    block = x_ref.shape[0]

    def tokens_of(owner):
        return x_all.at[pl.ds(pl.multiple_of(owner * block, 16), block), :]

    owner_of = [zp * 2 + core for zp in place.order]
    smalls = []
    for step in range(1, size):
        device = place.column((narrow + step) % size)
        smalls.append(
            remote(vector_ref, vector_all.at[narrow], small_send.at[0, step], small_recv.at[0, step], device)
        )
        smalls.append(
            remote(position_ref, position_all.at[narrow], small_send.at[1, step], small_recv.at[1, step], device)
        )
    for copy in smalls:
        copy.start()
    local = [
        pltpu.make_async_copy(vector_ref, vector_all.at[narrow], own_sems.at[count + 1]),
        pltpu.make_async_copy(position_ref, position_all.at[narrow], own_sems.at[count + 2]),
        pltpu.make_async_copy(x_ref, tokens_of(narrow), own_sems.at[count]),
    ]
    for a in range(count):
        local.append(pltpu.make_async_copy(shard_refs[a], shard(a, narrow), own_sems.at[a]))
    for copy in local:
        copy.start()

    def line_copies(a, owner, source, target):
        return (
            remote(source, target, line_send.at[a, owner // 2, 0], line_recv.at[a, owner // 2], place.up()),
            remote(source, target, line_send.at[a, owner // 2, 1], line_recv.at[a, owner // 2], place.down()),
        )

    def line_pair(a, owner):
        if a == count:
            target = tokens_of(owner)
            source = target
        else:
            target = region(a, owner, place.quarter)
            source = target
        return line_copies(a, owner, source, target)

    def own_pair(a):
        if a == count:
            return line_copies(a, narrow, x_ref, tokens_of(narrow))
        return line_copies(a, narrow, own_piece(a), region(a, narrow, place.quarter))

    def own_to_sibling(a):
        if a == count:
            return remote(x_ref, tokens_of(narrow), own_send.at[a], own_recv.at[a], place.sibling())
        return remote(shard_refs[a], shard(a, narrow), own_send.at[a], own_recv.at[a], place.sibling())

    def start_own(a):
        up, down = own_pair(a)
        pl.when(z < 3)(up.start)
        pl.when(z > 0)(down.start)
        own_to_sibling(a).start()

    def forwards(a, index):
        zp = place.order[index]
        if a == count:
            near = jnp.logical_and(zp - z < 2, z - zp < 2)
            return (
                jnp.logical_and(jnp.logical_and(zp < z, z < 3), near),
                jnp.logical_and(jnp.logical_and(zp > z, z > 0), near),
            )
        return jnp.logical_and(zp < z, z < 3), jnp.logical_and(zp > z, z > 0)

    def arrives(index):
        zp = place.order[index]
        return jnp.logical_and(zp - z < 3, z - zp < 3)

    def quarters(bit_first):
        first = place.flip(place.quarter, place.bit1)
        return first, place.flip(place.quarter, place.bit2), place.flip(first, place.bit2)

    def turn_copy(a, index):
        target = region(a, owner_of[index], place.quarter)
        return remote(
            target, target, turn_send.at[a, index], turn_recv.at[a, index], place.partner(place.bit1)
        )

    def next_copy(a, index, which):
        quarter = place.quarter if which == 0 else place.flip(place.quarter, place.bit1)
        target = region(a, owner_of[index], quarter)
        return remote(
            target, target, next_send.at[a, index, which], next_recv.at[a, index, which],
            place.partner(place.bit2),
        )

    def back_copy(a, index):
        if a == count:
            target = tokens_of(owner_of[index])
        else:
            target = shard(a, owner_of[index])
        return remote(
            target, target, back_send.at[a, index], back_recv.at[a, index], place.sibling()
        )

    def on_line(a, index):
        up, down = line_pair(a, owner_of[index])

        def work():
            up.wait_recv()
            goes_up, goes_down = forwards(a, index)
            pl.when(goes_up)(up.start)
            pl.when(goes_down)(down.start)
            if a == count:
                back_copy(a, index).start()
            else:
                turn_copy(a, index).start()
                next_copy(a, index, 0).start()

        if a == count:
            pl.when(arrives(index))(work)
        else:
            work()

    def turned(index):
        for a in range(count):
            turn_copy(a, index).wait_recv()
            next_copy(a, index, 1).start()

    def on_lines(index):
        for a in range(count):
            on_line(a, index)

    token_up, token_down = own_pair(count)
    for a in range(count):
        start_own(a)
    own_to_sibling(count).start()
    pl.when(z == 0)(token_up.start)
    pl.when(z == 3)(token_down.start)
    on_lines(0)
    pl.when(z == 1)(token_up.start)
    pl.when(z == 2)(token_down.start)
    on_lines(1)
    turned(0)
    on_lines(2)
    pl.when(z == 2)(token_up.start)
    pl.when(z == 1)(token_down.start)
    turned(1)
    turned(2)
    for index in range(3):
        on_line(count, index)
    for index in range(3):
        for a in range(count):
            next_copy(a, index, 0).wait_recv()
            next_copy(a, index, 1).wait_recv()
            back_copy(a, index).start()
    for a in range(count):
        for index in range(3):
            back_copy(a, index).wait_recv()
    for a in range(count + 1):
        own_to_sibling(a).wait()
        up, down = own_pair(a)
        pl.when(z < 3)(up.wait_send)
        pl.when(z > 0)(down.wait_send)
    for index in range(3):

        @pl.when(arrives(index))
        def _():
            back_copy(count, index).wait()
            goes_up, goes_down = forwards(count, index)
            up, down = line_pair(count, owner_of[index])
            pl.when(goes_up)(up.wait_send)
            pl.when(goes_down)(down.wait_send)

        for a in range(count):
            goes_up, goes_down = forwards(a, index)
            up, down = line_pair(a, owner_of[index])
            pl.when(goes_up)(up.wait_send)
            pl.when(goes_down)(down.wait_send)
            turn_copy(a, index).wait_send()
            next_copy(a, index, 0).wait_send()
            next_copy(a, index, 1).wait_send()
            back_copy(a, index).wait_send()
    for copy in local:
        copy.wait()
    for copy in smalls:
        copy.wait()


def gather_all(x, positions, vector, shards, size):
    count = len(shards)
    shapes = tuple(shard.shape for shard in shards)
    anywhere = pl.BlockSpec(memory_space=pl.ANY)
    dma = pltpu.SemaphoreType.DMA
    out_shape = [
        jax.ShapeDtypeStruct((size * shard.shape[0], shard.shape[1]), shard.dtype) for shard in shards
    ] + [
        jax.ShapeDtypeStruct((size * x.shape[0], x.shape[1]), x.dtype),
        jax.ShapeDtypeStruct((size, *positions.shape), positions.dtype),
        jax.ShapeDtypeStruct((size, *vector.shape), vector.dtype),
    ]
    return pl.pallas_call(
        functools.partial(gather_kernel, shapes, size),
        out_shape=out_shape,
        in_specs=[anywhere] * (count + 3),
        out_specs=[anywhere] * (count + 3),
        scratch_shapes=[
            dma((count + 3,)),
            dma((count + 1,)),
            dma((count + 1,)),
            dma((count + 1, 4, 2)),
            dma((count + 1, 4)),
            dma((count, 3)),
            dma((count, 3)),
            dma((count, 3, 2)),
            dma((count, 3, 2)),
            dma((count + 1, 3)),
            dma((count + 1, 3)),
            dma((2, size)),
            dma((2, size)),
        ],
        compiler_params=pltpu.CompilerParams(collective_id=1, has_side_effects=True),
        name="gather_all",
    )(*shards, x, positions, vector)


def add_into(target, source):
    rows = target.shape[-2]
    step = 32 if rows % 32 == 0 else 16
    lead = target.shape[:-2]

    @pl.loop(0, rows // step)
    def _(turn_index):
        cut = pl.ds(pl.multiple_of(turn_index * step, 16), step)
        for index in np.ndindex(*lead):
            at = (*index, cut, slice(None))
            target[at] = target[at] + source[at]


def finish_rows(info, grad, x, g_mid, mods, gain):
    width = x.shape[1]
    first_row = info[4]
    scale = 1.0 + mods[:, width:]
    picks = slot_picks(x.shape[0], first_row, info)
    xh, inverse = normed(x.astype(F32))
    moved = grad * xh
    sums = jnp.concatenate(
        [slot_sums(first_row, info, grad), slot_sums(first_row, info, moved * gain)], axis=1
    )
    g_gain = jnp.sum(moved * dot(picks, pick_table(scale)), axis=0, keepdims=True)
    h = grad * dot(picks, pick_table(scale * gain))
    tokens = g_mid + inverse * (
        h - jnp.mean(h, axis=1, keepdims=True) - xh * jnp.mean(h * xh, axis=1, keepdims=True)
    )
    return tokens, sums, g_gain


def folded(values, columns):
    return jnp.concatenate(
        [values[:, at : at + columns] for at in range(0, values.shape[1], columns)], axis=0
    )


def reduce_kernel(shapes, summed, size, groups, info, *refs):
    count, made = len(shapes), summed - 1
    refs = list(refs)
    grad_refs = [refs.pop(0) for _ in range(count - 1)]
    grad_refs.insert(made, None)
    (
        first_ref, dk_ref, dv_ref, early_ref, dq_ref, weight_ref, position_ref, coarse_ref, fine_ref,
        x_ref, g_mid_ref, mods_ref, gain_ref,
    ) = (refs.pop(0) for _ in range(13))
    out_refs = [refs.pop(0) for _ in range(count)]
    tokens_ref, early_all, late_all = (refs.pop(0) for _ in range(3))
    rest = refs
    own, turned, nexted, far = ([rest.pop(0) for _ in range(count)] for _ in range(4))
    side, upward, downward = ([rest.pop(0) for _ in range(summed)] for _ in range(3))
    (
        first_in, dk_in, dv_in, dw_sum, made_out, dx_out,
        dx_own, dx_side, dx_up, dx_down, late_ref, early_in, late_in, early_sum, late_sum,
        own_sem, side_send, side_recv, turn_send, turn_recv, next_send, next_recv, line_send,
        line_recv, far_send, far_recv, share_send, share_recv, final_sem,
        block_sem, dx_side_send, dx_side_recv, dx_send, dx_recv,
        pack_send, pack_recv, wide_send, wide_recv, pack_own,
    ) = rest
    place = Place()
    z, core, narrow = place.z, place.core, place.narrow
    barrier = pltpu.get_barrier_semaphore()
    for step in range(1, size):
        pl.semaphore_signal(
            barrier, inc=1, device_id=place.column((narrow + step) % size), device_id_type=MESH
        )
    for step in range(1, groups):
        pl.semaphore_signal(
            barrier, inc=1, device_id=((place.wide + step) % groups, narrow), device_id_type=MESH
        )
    pl.semaphore_wait(barrier, size + groups - 2)

    def remote(source, target, send, recv, device):
        return pltpu.make_async_remote_copy(
            src_ref=source, dst_ref=target, send_sem=send, recv_sem=recv, device_id=device,
            device_id_type=MESH,
        )

    def piece(ref, a, which, lead):
        rows, columns = shapes[a]
        first_row, row_count, first_column, column_count = piece_of(shapes[a], which)
        return ref.at[
            (*lead, cut_of(first_row, row_count, rows, 16), cut_of(first_column, column_count, columns, TILE))
        ]

    quarter = place.quarter
    other1 = place.flip(quarter, place.bit1)
    other2 = place.flip(quarter, place.bit2)
    every = (slice(None),)

    def pack_copies(which, source, target):
        return [
            remote(
                source, target.at[narrow], pack_send.at[which, step], pack_recv.at[which, step],
                place.column((narrow + step) % size),
            )
            for step in range(1, size)
        ]

    def wide_copies(which, source, target):
        return [
            remote(
                source, target.at[place.wide], wide_send.at[which, step], wide_recv.at[which, step],
                ((place.wide + step) % groups, narrow),
            )
            for step in range(1, groups)
        ]

    early_copies = pack_copies(0, early_ref, early_in)
    early_own = pltpu.make_async_copy(early_ref, early_in.at[narrow], pack_own.at[0])
    early_own.start()

    side_copy, own_copy = [], []
    for a in range(count):
        if a == made:
            side_copy.append(
                remote(made_out, side[a], side_send.at[a], side_recv.at[a], place.sibling())
            )
            own_copy.append(None)
            continue
        if a < summed:
            side_copy.append(
                remote(grad_refs[a].at[:, 1 - core], side[a], side_send.at[a], side_recv.at[a], place.sibling())
            )
            own_copy.append(pltpu.make_async_copy(grad_refs[a].at[:, core], own[a], own_sem.at[a]))
            side_copy[a].start()
        else:
            own_copy.append(pltpu.make_async_copy(grad_refs[a], own[a].at[0], own_sem.at[a]))
        own_copy[a].start()

    def dx_copy(upwards, slot):
        zp = jnp.clip(z + 1 + slot if upwards else z - 1 - slot, 0, 3)
        way = 0 if upwards else 1
        landing = dx_up if upwards else dx_down
        return remote(
            dx_own.at[zp], landing.at[slot], dx_send.at[way, slot], dx_recv.at[way, slot],
            place.up() if upwards else place.down(),
        )

    def dx_middle():
        @pl.when(z < 3)
        def _():
            @pl.when(z > 0)
            def _():
                dx_copy(True, 1).wait_recv()
                add_into(dx_own.at[jnp.minimum(z + 1, 3)], dx_up.at[1])

            dx_copy(True, 0).start()

        @pl.when(z > 0)
        def _():
            @pl.when(z < 3)
            def _():
                dx_copy(False, 1).wait_recv()
                add_into(dx_own.at[jnp.maximum(z - 1, 0)], dx_down.at[1])

            dx_copy(False, 0).start()

    def dx_end():
        @pl.when(z > 0)
        def _():
            dx_copy(True, 0).wait_recv()
            add_into(dx_own.at[z], dx_up.at[0])

        @pl.when(z < 3)
        def _():
            dx_copy(False, 0).wait_recv()
            add_into(dx_own.at[z], dx_down.at[0])

        pl.when(z < 3)(dx_copy(True, 0).wait_send)
        pl.when(z < 2)(dx_copy(True, 1).wait_send)
        pl.when(z > 0)(dx_copy(False, 0).wait_send)
        pl.when(z > 1)(dx_copy(False, 1).wait_send)

    def turn_copy(a):
        rows, columns = shapes[a]
        out = []
        for bit in (1, 2):
            if bit == 1:
                there = (slice(None), pl.ds(pl.multiple_of((1 - quarter % 2) * (rows // 2), 16), rows // 2), slice(None))
                landing = turned[a].at[:, pl.ds(0, rows // 2), :]
            else:
                there = (slice(None), slice(None), pl.ds(pl.multiple_of((1 - quarter // 2) * (columns // 2), TILE), columns // 2))
                landing = turned[a].at[:, :, pl.ds(0, columns // 2)]
            out.append(
                remote(own[a].at[there], landing, turn_send.at[a], turn_recv.at[a], place.partner(bit))
            )
        return out

    def by_core(copies, what):
        pl.when(core == 0)(getattr(copies[0], what))
        pl.when(core == 1)(getattr(copies[1], what))

    def join(a):
        if a != made:
            own_copy[a].wait()
        if a < summed:
            side_copy[a].wait_recv()
            add_into(own[a], side[a])

    def start_turn(a):
        by_core(turn_copy(a), "start")

    def next_copy(a):
        return remote(
            piece(own[a], a, other2, every), nexted[a], next_send.at[a], next_recv.at[a],
            place.partner(place.bit2),
        )

    def start_next(a):
        rows, columns = shapes[a]
        by_core(turn_copy(a), "wait_recv")

        @pl.when(core == 0)
        def _():
            add_into(
                own[a].at[:, pl.ds(pl.multiple_of((quarter % 2) * (rows // 2), 16), rows // 2), :],
                turned[a].at[:, pl.ds(0, rows // 2), :],
            )

        @pl.when(core == 1)
        def _():
            add_into(
                own[a].at[:, :, pl.ds(pl.multiple_of((quarter // 2) * (columns // 2), TILE), columns // 2)],
                turned[a].at[:, :, pl.ds(0, columns // 2)],
            )

        next_copy(a).start()

    def line_copy(a, zp, upwards, source):
        if upwards:
            return remote(source, upward[a].at[zp], line_send.at[a, zp, 0], line_recv.at[a, zp, 0], place.up())
        return remote(source, downward[a].at[zp], line_send.at[a, zp, 1], line_recv.at[a, zp, 1], place.down())

    def start_line(a):
        next_copy(a).wait_recv()
        add_into(piece(own[a], a, quarter, every), nexted[a])
        if a >= summed:
            return
        for zp in (3, 2, 1):
            pl.when(z == 0)(line_copy(a, zp, True, piece(own[a], a, quarter, (zp,))).start)
            low = 3 - zp
            pl.when(z == 3)(line_copy(a, low, False, piece(own[a], a, quarter, (low,))).start)

    def middle_line(a):
        if a >= summed:
            return
        for zp in (3, 2, 1):

            @pl.when(jnp.logical_and(z > 0, z < zp))
            def _():
                copy = line_copy(a, zp, True, upward[a].at[zp])
                copy.wait_recv()
                add_into(upward[a].at[zp], piece(own[a], a, quarter, (zp,)))
                copy.start()

            low = 3 - zp

            @pl.when(jnp.logical_and(z < 3, z > low))
            def _():
                copy = line_copy(a, low, False, downward[a].at[low])
                copy.wait_recv()
                add_into(downward[a].at[low], piece(own[a], a, quarter, (low,)))
                copy.start()

    def share_copy(a, which, bit_place, slot):
        source = piece(out_refs[a], a, which, ())
        return remote(source, source, share_send.at[a, slot], share_recv.at[a, slot], place.partner(bit_place))

    def kept(a):
        return piece(own[a], a, quarter, (z,) if a < summed else (0,))

    def final_copy(a):
        return pltpu.make_async_copy(
            kept(a), piece(out_refs[a], a, quarter, ()), final_sem.at[a]
        )

    def far_copy(a, which, bit):
        return remote(
            kept(a), far[a].at[which], far_send.at[a, which],
            far_recv.at[a, which], (place.flip(place.wide, bit), narrow),
        )

    def end_line(a):
        mine = kept(a)
        if a < summed:

            @pl.when(z > 0)
            def _():
                line_copy(a, z, True, mine).wait_recv()
                add_into(mine, upward[a].at[z])

            @pl.when(z < 3)
            def _():
                line_copy(a, z, False, mine).wait_recv()
                add_into(mine, downward[a].at[z])

        bit, which = 4, 0
        while bit < groups:
            copy = far_copy(a, which, bit)
            copy.start()
            copy.wait()
            add_into(mine, far[a].at[which])
            bit, which = bit * 2, which + 1
        final_copy(a).start()

    def start_share(a):
        final_copy(a).wait()
        share_copy(a, quarter, place.bit1, 0).start()
        share_copy(a, quarter, place.bit2, 1).start()

    def pass_share(a):
        share_copy(a, quarter, place.bit1, 0).wait_recv()
        share_copy(a, other1, place.bit2, 2).start()

    def close(a):
        share_copy(a, quarter, place.bit2, 1).wait_recv()
        share_copy(a, other1, place.bit2, 2).wait_recv()
        share_copy(a, quarter, place.bit1, 0).wait_send()
        share_copy(a, quarter, place.bit2, 1).wait_send()
        share_copy(a, other1, place.bit2, 2).wait_send()
        by_core(turn_copy(a), "wait_send")
        next_copy(a).wait_send()
        if a >= summed:
            return
        side_copy[a].wait_send()
        for zp in range(4):
            mine = piece(own[a], a, quarter, (zp,))
            pl.when(z < zp)(line_copy(a, zp, True, mine).wait_send)
            pl.when(z > zp)(line_copy(a, zp, False, mine).wait_send)

    def column_total(landed):
        total = landed[0].astype(F32)
        for step in range(1, size):
            total = total + landed[step].astype(F32)
        return total.astype(BF16)

    width = x_ref.shape[1]
    block_rows = x_ref.shape[0]

    def zp_of(step):
        near = place.near
        return jnp.where(
            step == 0, (z + 2) % 4, jnp.where(step == 1, near, jnp.where(step == 2, (near + 2) % 4, z))
        )

    def needed(step):
        zp = zp_of(step)
        return jnp.logical_and(zp - z < 3, z - zp < 3)

    def fetch(turn_index):
        parity = turn_index % 2
        owner = zp_of(turn_index // 2) * 2 + jnp.where(parity == 0, 1 - core, core)
        rows = pl.ds(pl.multiple_of(owner * block_rows, block_rows), block_rows)
        return [
            pltpu.make_async_copy(ref.at[rows, :], landing.at[parity], block_sem.at[which, parity])
            for which, (ref, landing) in enumerate(((first_ref, first_in), (dk_ref, dk_in), (dv_ref, dv_in)))
        ]

    def dx_side_copy(step):
        return remote(
            dx_out.at[step % 2], dx_side.at[zp_of(step)], dx_side_send.at[step], dx_side_recv.at[step],
            place.sibling(),
        )

    def turned_back(values, cosine, sine):
        tiles = []
        for tile in range(width // TILE):
            cut = slice(tile * TILE, (tile + 1) * TILE)
            tiles.append(turn_back(values[:, cut].astype(F32), cosine, sine).astype(BF16))
        return jnp.concatenate(tiles, axis=1)

    dw_sum[...] = jnp.zeros_like(dw_sum)
    for copy in fetch(0):
        copy.start()

    @pl.loop(0, 8)
    def _(turn_index):
        step = turn_index // 2
        parity = turn_index % 2
        zp = zp_of(step)
        owner = zp * 2 + jnp.where(parity == 0, 1 - core, core)

        @pl.when(turn_index < 7)
        def _():
            for copy in fetch(turn_index + 1):
                copy.start()

        for copy in fetch(turn_index):
            copy.wait()

        @pl.when(needed(step))
        def _():
            cosine, sine = rotary(position_ref[owner], coarse_ref, fine_ref)
            dk = turned_back(dk_in[parity], cosine, sine)
            dv = dv_in[parity]
            first = first_in[parity]
            dw_sum[:, width : 2 * width] += dot(first, dk, ((0,), (0,)))
            dw_sum[:, 2 * width :] += dot(first, dv, ((0,), (0,)))
            total = (
                dot(dk, weight_ref[:, width : 2 * width], ((1,), (1,)))
                + dot(dv, weight_ref[:, 2 * width :], ((1,), (1,)))
            ).astype(BF16)

            @pl.when(parity == 0)
            def _():
                @pl.when(jnp.logical_and(step > 1, needed(step - 2)))
                def _():
                    dx_side_copy(step - 2).wait_send()

                dx_out[step % 2] = total
                dx_side_copy(step).start()

            @pl.when(parity == 1)
            def _():
                dx_own[zp] = total
                dx_side_copy(step).wait_recv()
                add_into(dx_own.at[zp], dx_side.at[zp])

        @pl.when(turn_index == 1)
        def _():
            pl.when(z < 2)(dx_copy(True, 1).start)
            pl.when(z > 1)(dx_copy(False, 1).start)
            join(0)
            start_turn(0)

        @pl.when(turn_index == 3)
        def _():
            for a in range(1, count):
                if a != made:
                    join(a)
                    start_turn(a)

    cosine, sine = rotary(position_ref[narrow], coarse_ref, fine_ref)
    dq = turned_back(dq_ref[...], cosine, sine)
    dw_sum[:, :width] = dot(first_in[1], dq, ((0,), (0,)))
    dx_own[z] = (
        dx_own[z].astype(F32) + dot(dq, weight_ref[:, :width], ((1,), (1,)))
    ).astype(BF16)
    shard_rows = shapes[made][0]

    @pl.loop(0, 4)
    def _(zp):
        mine = pl.ds(pl.multiple_of((2 * zp + core) * shard_rows, 16), shard_rows)
        other = pl.ds(pl.multiple_of((2 * zp + 1 - core) * shard_rows, 16), shard_rows)
        own[made][zp] = dw_sum[mine, :].astype(BF16)
        made_out[zp] = dw_sum[other, :].astype(BF16)

    side_copy[made].start()
    dx_middle()
    for a in range(count):
        if a != made:
            start_next(a)
    join(made)
    start_turn(made)
    for copy in early_copies:
        copy.start()
    for a in range(made):
        start_line(a)
    for a in range(summed, count):
        start_line(a)
        end_line(a)
        start_share(a)
    start_next(made)
    for a in range(made):
        middle_line(a)
    dx_end()
    for a in range(made):
        end_line(a)
        start_share(a)
    start_line(made)
    tokens, sums, g_gain = finish_rows(
        info, dx_own[z].astype(F32), x_ref[...], g_mid_ref[...], mods_ref[...], gain_ref[...]
    )
    tokens_ref[...] = tokens
    quarter_width = sums.shape[1] // 4
    late_ref[...] = jnp.concatenate(
        [
            folded(sums[:4], quarter_width),
            folded(g_gain, quarter_width),
            jnp.zeros((14, quarter_width), F32),
        ],
        axis=0,
    ).astype(BF16)
    late_copies = pack_copies(1, late_ref, late_in)
    for copy in late_copies:
        copy.start()
    late_own = pltpu.make_async_copy(late_ref, late_in.at[narrow], pack_own.at[1])
    late_own.start()
    middle_line(made)
    for a in range(count):
        if a != made:
            pass_share(a)
    end_line(made)
    start_share(made)
    for copy in early_copies:
        copy.wait_recv()
    early_own.wait()
    early_sum[...] = column_total(early_in)
    early_wide = wide_copies(0, early_sum, early_all)
    for copy in early_wide:
        copy.start()
    early_final = pltpu.make_async_copy(early_sum, early_all.at[place.wide], pack_own.at[2])
    early_final.start()
    for copy in late_copies:
        copy.wait_recv()
    late_own.wait()
    late_sum[...] = column_total(late_in)
    late_wide = wide_copies(1, late_sum, late_all)
    for copy in late_wide:
        copy.start()
    late_final = pltpu.make_async_copy(late_sum, late_all.at[place.wide], pack_own.at[3])
    late_final.start()
    pass_share(made)
    for a in range(count):
        close(a)
    for step in (2, 3):
        pl.when(needed(step))(dx_side_copy(step).wait_send)
    pl.when(jnp.logical_and(needed(0), jnp.logical_not(needed(2))))(dx_side_copy(0).wait_send)
    pl.when(jnp.logical_and(needed(1), jnp.logical_not(needed(3))))(dx_side_copy(1).wait_send)
    early_final.wait()
    late_final.wait()
    for copy in early_copies + late_copies:
        copy.wait_send()
    for copy in early_wide + late_wide:
        copy.wait()


def reduce_all(
    info, grads, summed, first, dk, dv, early, dq, weight, positions, tables, x, g_mid, mods, gain,
    size, groups,
):
    shapes = tuple((grad.shape[0] // size, grad.shape[1]) for grad in (*grads, weight)) + tuple(
        shard.shape for shard in summed
    )
    count, full = len(shapes), len(grads) + 1
    row_count, width = x.shape
    anywhere = pl.BlockSpec(memory_space=pl.ANY)
    vmem = pl.BlockSpec(memory_space=pltpu.VMEM)
    dma = pltpu.SemaphoreType.DMA

    def scratch(*shape):
        return pltpu.VMEM(shape, BF16)

    pieces = [(piece_of(shape, 0)[1], piece_of(shape, 0)[3]) for shape in shapes]
    leads = [4] * full + [1] * len(summed)
    late = (32, 2 * width // 4)
    turns = max(1, int(math.log2(groups)) - 2)
    scratch_shapes = (
        [scratch(lead, *shape) for lead, shape in zip(leads, shapes)]
        + [scratch(lead, *shape) for lead, shape in zip(leads, shapes)]
        + [scratch(lead, *piece) for lead, piece in zip(leads, pieces)]
        + [scratch(turns, *piece) for piece in pieces]
        + [scratch(4, *shape) for shape in shapes[:full]]
        + [scratch(4, *piece) for piece in pieces[:full]] * 2
        + [
            scratch(2, row_count, width), scratch(2, row_count, width),
            scratch(2, row_count, width), pltpu.VMEM(weight.shape, F32),
            scratch(4, *shapes[full - 1]), scratch(2, row_count, width),
            scratch(4, row_count, width), scratch(4, row_count, width),
            scratch(2, row_count, width), scratch(2, row_count, width),
            scratch(*late), scratch(size, *early.shape), scratch(size, *late),
            scratch(*early.shape), scratch(*late),
            dma((count,)), dma((count,)), dma((count,)), dma((count,)), dma((count,)),
            dma((count,)), dma((count,)), dma((count, 4, 2)), dma((count, 4, 2)),
            dma((count, turns)), dma((count, turns)), dma((count, 3)), dma((count, 3)),
            dma((count,)), dma((3, 2)), dma((4,)), dma((4,)), dma((2, 2)), dma((2, 2)),
            dma((2, size)), dma((2, size)), dma((2, groups)), dma((2, groups)), dma((4,)),
        ]
    )
    views = [grad.reshape(4, 2, *shape) for grad, shape in zip(grads, shapes)]
    return pl.pallas_call(
        functools.partial(reduce_kernel, shapes, full, size, groups),
        out_shape=[jax.ShapeDtypeStruct(shape, BF16) for shape in shapes]
        + [
            jax.ShapeDtypeStruct(x.shape, F32),
            jax.ShapeDtypeStruct((groups, *early.shape), BF16),
            jax.ShapeDtypeStruct((groups, *late), BF16),
        ],
        in_specs=[pl.BlockSpec(memory_space=pltpu.SMEM)]
        + [anywhere] * (count + 3)
        + [vmem] * 9,
        out_specs=[anywhere] * count + [vmem, anywhere, anywhere],
        scratch_shapes=scratch_shapes,
        compiler_params=pltpu.CompilerParams(
            collective_id=2, has_side_effects=True, vmem_limit_bytes=REDUCE_VMEM
        ),
        name="reduce_all",
        )(
        info, *views, *summed, first, dk, dv, early, dq, weight, positions, *tables, x, g_mid, mods, gain,
    )


def tail_kernel(
    g0_ref, g1_ref, g2_ref, g3_ref, early_ref, late_ref, time_ref, ada_ref,
    o0_ref, o1_ref, o2_ref, o3_ref, g_ada_ref, g_bias_ref, g_time_ref, norm1_ref, norm2_ref, fc1_b_ref,
    fc2_b_ref, mod_ref, cond_ref, turned_ref, full_ref,
):
    for source, target in ((g0_ref, o0_ref), (g1_ref, o1_ref), (g2_ref, o2_ref), (g3_ref, o3_ref)):
        target[...] = source[...].astype(F32)
    me = lax.axis_index("narrow")
    groups, _, width = early_ref.shape
    seqs = time_ref.shape[0]
    vectors = jnp.zeros((16, width), F32)
    norm1 = jnp.zeros((2, width // 2), F32)
    picks = []
    for group in range(groups):
        early = early_ref[group].astype(F32)
        late = late_ref[group].astype(F32)
        vectors = vectors + early[16:32]
        norm1 = norm1 + late[16:18]
        rows = jnp.concatenate(
            [late[4 * at : 4 * at + 4] for at in range(4)] + [early[4 * at : 4 * at + 4] for at in range(4)],
            axis=1,
        )
        mod_ref[4 * group : 4 * group + 4, :] = rows
        sub = lax.broadcasted_iota(jnp.int32, (seqs, TILE), 0).astype(F32)
        lane = lax.broadcasted_iota(jnp.int32, (seqs, TILE), 1)
        pick = jnp.where(jnp.logical_and(sub == early[22:23, :TILE], lane < 4), 1.0, 0.0)
        picks.append(pick)
        cond_ref[4 * group : 4 * group + 4, :] = dot(
            pick.astype(BF16), time_ref[...], ((0,), (0,))
        )[:4]
    g_mod = mod_ref[...]

    def mine(row, size):
        lanes = row.shape[1]
        block = jnp.broadcast_to(row, (8, lanes))
        return pltpu.roll(block, lax.rem(lanes - me * size, lanes), 1)[:1, :size]

    g_bias_ref[...] = mine(jnp.sum(g_mod, axis=0, keepdims=True), g_bias_ref.shape[1])
    norm1_ref[...] = mine(jnp.concatenate([norm1[0:1], norm1[1:2]], axis=1), norm1_ref.shape[1])
    norm2_ref[...] = mine(vectors[0:1], norm2_ref.shape[1])
    fc2_b_ref[...] = mine(vectors[1:2], fc2_b_ref.shape[1])
    fc1_b_ref[...] = mine(
        jnp.concatenate([vectors[2 + at : 3 + at] for at in range(4)], axis=1), fc1_b_ref.shape[1]
    )
    turned_ref[...] = cond_ref[...].T
    own_rows = g_ada_ref.shape[0]
    parts = jnp.concatenate(thirds(g_mod), axis=0)
    own_cond = turned_ref[pl.ds(pl.multiple_of(me * own_rows, 8), own_rows), :].astype(BF16)
    g_ada_ref[...] = dot(jnp.concatenate([own_cond] * 3, axis=1), parts)
    g_cond = dot(parts, ada_ref[...], ((1,), (1,)))
    count = 4 * groups
    g_cond = g_cond[:count] + g_cond[count : 2 * count] + g_cond[2 * count :]
    total = jnp.zeros((seqs, TILE), F32)
    for group in range(groups):
        part = jnp.concatenate([g_cond[4 * group : 4 * group + 4], jnp.zeros((TILE - 4, TILE), F32)], axis=0)
        total = total + dot(picks[group], part, precision=HIGH)
    full_ref[...] = total
    own_seqs = g_time_ref.shape[0]
    g_time_ref[...] = full_ref[pl.ds(me * own_seqs, own_seqs), :]


def tail(grads, early, late, time_emb, ada, sizes):
    vmem = pl.BlockSpec(memory_space=pltpu.VMEM)
    groups = early.shape[0]
    devices = ada.shape[1] // sizes[2]
    return pl.pallas_call(
        tail_kernel,
        out_shape=[jax.ShapeDtypeStruct(grad.shape, F32) for grad in grads]
        + [
            jax.ShapeDtypeStruct((ada.shape[0] // devices, ada.shape[1]), F32),
            jax.ShapeDtypeStruct((1, sizes[2]), F32),
            jax.ShapeDtypeStruct((time_emb.shape[0] // devices, time_emb.shape[1]), F32),
        ]
        + [jax.ShapeDtypeStruct((1, sizes[which]), F32) for which in (0, 1, 3, 4)],
        in_specs=[vmem] * (len(grads) + 4),
        out_specs=[vmem] * (len(grads) + 7),
        scratch_shapes=[
            pltpu.VMEM((4 * groups, ada.shape[1]), F32),
            pltpu.VMEM((4 * groups, ada.shape[0]), F32),
            pltpu.VMEM((ada.shape[0], 4 * groups), F32),
            pltpu.VMEM(time_emb.shape, F32),
        ],
        compiler_params=pltpu.CompilerParams(vmem_limit_bytes=VMEM_LIMIT),
        name="tail",
    )(*grads, early, late, time_emb, ada)


def body(
    tokens, cotangent, time_emb, seq_table, lengths, positions, norm1_gain, norm2_gain,
    ada_weight, ada_bias, qkv_weight, out_weight, fc1_weight, fc1_bias, fc2_weight, fc2_bias,
):
    row_count, width = tokens.shape
    me = lax.axis_index("narrow")
    size, groups = lax.axis_size("narrow"), lax.axis_size("wide")
    slots = lengths.shape[1]
    below = np.zeros((16, slots), np.int32)
    below[:slots] = np.tril(np.ones((slots, slots), np.int32))
    table = np.zeros((16, slots), np.int32)
    table[8 : 8 + slots] = np.eye(slots, dtype=np.int32)
    info = (
        jnp.sum(
            jnp.asarray(below) * lengths[0][None, :]
            + jnp.asarray(table) * jnp.where(me == 0, seq_table, 0)[None, :],
            axis=1,
        )
        + (jnp.arange(16) == 4) * (me * row_count)
    ).astype(jnp.int32)
    seqs = jnp.pad(seq_table, (0, 8 - slots), constant_values=-1)
    onehot_table = (
        seqs[:, None] == jnp.arange(time_emb.shape[0], dtype=jnp.int32)[None, :]
    ).astype(BF16)
    cond8 = jnp.dot(onehot_table, time_emb, preferred_element_type=F32).astype(BF16)
    tables = tuple(jnp.asarray(t) for t in rotary_constants())
    pieces = (norm1_gain, norm2_gain, ada_bias, fc1_bias, fc2_bias)
    sizes = tuple(piece.size for piece in pieces)

    def spread_gather(shard):
        part = shard.shape[0] // groups
        mine = lax.dynamic_slice_in_dim(shard, lax.axis_index("wide") * part, part, 0)
        return lax.all_gather(mine, ("narrow", "wide"), axis=0, tiled=True)

    out_w, fc1 = (spread_gather(shard) for shard in (out_weight, fc1_weight))
    ada, qkv_w, fc2, x_all, position_all, vectors = gather_all(
        tokens, positions.reshape(-1, TILE), packed(pieces), (ada_weight, qkv_weight, fc2_weight), size
    )
    keys, values, first, queries, norms, mods1, gain1, gain2, bias, fc1_b, fc2_b = project(
        info, x_all, position_all, cond8, ada, vectors, sizes, qkv_w, tables, row_count
    )
    attended, mass = attend(info, queries, keys, values, norms)
    layer_out, g_fc1, g_fc2, g_out, g_att, g_mid, early = mlp(
        info, tokens, attended, cotangent, cond8, ada, bias, gain2, out_w, fc1, fc1_b, fc2, fc2_b
    )
    dq, dk, dv = attend_back(info, queries, keys, values, g_att, attended, mass)
    g_fc1 = lax.psum_scatter(g_fc1, "narrow", scatter_dimension=0, tiled=True)
    g_fc2, g_out, g_qkv, g_fc1, grad_tokens, early_all, late_all = reduce_all(
        info, (g_fc2, g_out), (g_fc1,), first, dk, dv, early, dq, qkv_w, position_all, tables, tokens,
        g_mid, mods1, gain1, size, groups,
    )
    g_fc2, g_out, g_qkv, g_fc1, g_ada, g_ada_bias, g_time, g_norm1, g_norm2, g_fc1_b, g_fc2_b = tail(
        (g_fc2, g_out, g_qkv, g_fc1), early_all, late_all, time_emb, ada, sizes
    )
    return (
        layer_out, grad_tokens, g_time, g_norm1.reshape(-1), g_norm2.reshape(-1), g_ada,
        g_ada_bias.reshape(-1), g_qkv, g_out, g_fc1, g_fc1_b.reshape(-1), g_fc2, g_fc2_b.reshape(-1),
    )


def solution(mesh):
    both = P(("wide", "narrow"), None)
    row = P("narrow")
    table = P("narrow", None)
    return jax.shard_map(
        body,
        mesh=mesh,
        in_specs=(
            both, both, P(), P("wide"), P("wide", None), P(("wide", "narrow")), row, row,
            table, row, table, table, table, row, table, row,
        ),
        out_specs=(both, both, table, row, row, table, row, table, table, table, row, table, row),
        check_vma=False,
    )
```

```python
import functools
import math

import jax
import jax.numpy as jnp
import numpy as np
from jax import lax
from jax.experimental import pallas as pl
from jax.experimental.pallas import tpu as pltpu
from jax.sharding import PartitionSpec as P

HEADS = 12
HEAD_DIM = 64
EPSILON = 1e-05
FAR = -(2.0**100)
SAFE = 64.0
LIFT = 20.0
F32 = jnp.float32
BF16 = jnp.bfloat16
HIGH = lax.Precision.HIGHEST
VMEM_LIMIT = 56 * 2**20
REDUCE_VMEM = 63 * 2**20
TILE = 128
QUERY_ROWS = 256
KEY_ROWS = 256
BLOCK = 512
CHUNK = 768


def params(grid_dims=1):
    return pltpu.CompilerParams(
        dimension_semantics=("arbitrary",) * grid_dims, vmem_limit_bytes=VMEM_LIMIT
    )


def dot(left, right, contract=((1,), (0,)), precision=None):
    return lax.dot_general(
        left, right, (contract, ((), ())), preferred_element_type=F32, precision=precision
    )


def thirds(values):
    high = values.astype(BF16)
    rest = values - high.astype(F32)
    middle = rest.astype(BF16)
    low = (rest - middle.astype(F32)).astype(BF16)
    return high, middle, low


def slot_of(rows, info):
    zero = jnp.zeros_like(rows)
    slot = zero
    for which in range(3):
        slot = slot + jnp.where(rows >= info[which], 1, zero)
    return slot


def scalar_slot(row, info):
    slot = jnp.int32(0)
    for which in range(3):
        slot = slot + jnp.where(row >= info[which], 1, 0)
    return slot


def key_range(first, last, info):
    low_slot = scalar_slot(first, info)
    high_slot = scalar_slot(last, info)
    start = jnp.where(
        low_slot == 0, 0, jnp.where(low_slot == 1, info[0], jnp.where(low_slot == 2, info[1], info[2]))
    )
    end = jnp.where(
        high_slot == 0,
        info[0],
        jnp.where(high_slot == 1, info[1], jnp.where(high_slot == 2, info[2], info[3])),
    )
    return start, end


def active_range(info):
    start, end = key_range(info[4], info[4] + BLOCK - 1, info)
    return start // BLOCK, (end - 1) // BLOCK


def block_active(block, info):
    low, high = active_range(info)
    return jnp.logical_and(block >= low, block <= high)


def active_rows(block, info):
    low, high = active_range(info)
    return jnp.clip(block, low, high), 0


def slot_picks(row_count, first_row, info):
    rows = first_row + lax.broadcasted_iota(jnp.int32, (row_count, 16), 0)
    lane = lax.broadcasted_iota(jnp.int32, (row_count, 16), 1)
    return jnp.where(
        jnp.logical_and(slot_of(rows, info) == lane % 4, lane < 12), 1.0, 0.0
    ).astype(BF16)


def pick_table(values):
    high, middle, low = thirds(values)
    zero = jnp.zeros_like(high[:4])
    return jnp.concatenate([high[:4], middle[:4], low[:4], zero], axis=0)


def normed(values):
    center = values - jnp.mean(values, axis=1, keepdims=True)
    spread = jnp.mean(center * center, axis=1, keepdims=True)
    inverse = lax.rsqrt(spread + EPSILON)
    return center * inverse, inverse


def rotary_constants():
    half = HEAD_DIM // 2
    inverse = 10000.0 ** (-(np.arange(half, dtype=np.float64) * 2.0) / HEAD_DIM)
    inverse = inverse.astype(np.float32).astype(np.float64)
    tables = []
    for count, step in ((128, 64), (64, 1)):
        angles = (np.arange(count, dtype=np.float64) * step)[:, None] * inverse[None, :]
        full = np.concatenate(
            [np.tile(np.cos(angles), (1, 4)), np.tile(np.sin(angles), (1, 4))], axis=1
        ).astype(np.float32)
        high = full.astype(jnp.bfloat16)
        low = (full - high.astype(np.float32)).astype(jnp.bfloat16)
        tables.append(np.concatenate([high, low], axis=1))
    return tables


def rotary(positions, coarse_ref, fine_ref):
    count = positions.size
    parts = []
    for picks, table in ((positions // 64, coarse_ref), (positions % 64, fine_ref)):
        depth = table.shape[0]
        sub = lax.broadcasted_iota(jnp.int32, (depth, TILE), 0)
        onehot = jnp.concatenate(
            [(sub == picks[at : at + 1, :]).astype(F32) for at in range(positions.shape[0])], axis=1
        )
        both = dot(onehot.astype(BF16), table[...], ((0,), (0,)))
        parts.append(both[:, :256] + both[:, 256:])
    coarse, fine = parts
    cosine = coarse[:, :128] * fine[:, :128] - coarse[:, 128:] * fine[:, 128:]
    sine = coarse[:, 128:] * fine[:, :128] + coarse[:, :128] * fine[:, 128:]
    lane = lax.broadcasted_iota(jnp.int32, (count, TILE), 1)
    return cosine, jnp.where(lane % 64 < 32, -sine, sine)


def swapped(values):
    lane = lax.broadcasted_iota(jnp.int32, values.shape, 1)
    return jnp.where(
        lane % 64 < 32, pltpu.roll(values, TILE - 32, 1), pltpu.roll(values, 32, 1)
    )


def turn(values, cosine, sine):
    return values * cosine + swapped(values) * sine


def turn_back(values, cosine, sine):
    return values * cosine - swapped(values) * sine


def packed(pieces):
    starts = np.cumsum([0] + [-(-piece.size // TILE) * TILE for piece in pieces])
    whole = -(-starts[-1] // (16 * TILE)) * 16 * TILE
    rows = [
        jnp.pad(piece, (start, whole - start - piece.size)) for piece, start in zip(pieces, starts)
    ]
    return functools.reduce(jnp.add, rows).reshape(-1, TILE)


def joined(vector_ref, row, size):
    devices = vector_ref.shape[0]
    rows = -(-size // TILE)
    room = -(-(devices - 1) * size // TILE) + rows
    total = jnp.zeros((8, room * TILE), F32)
    for device in range(devices):
        block = vector_ref[device].astype(F32)
        lanes = [block[row + at : row + at + 1, :] for at in range(rows)]
        line = jnp.concatenate(lanes, axis=1)
        line = jnp.concatenate([line, jnp.zeros((1, (room - rows) * TILE), F32)], axis=1)
        line = jnp.broadcast_to(line, (8, room * TILE))
        total = total + (pltpu.roll(line, device * size, 1) if device else line)
    return total[:1, : devices * size]


def project_kernel(
    sizes, info, x_ref, position_ref, cond_ref, ada_ref, vector_ref, weight_ref, coarse_ref,
    fine_ref, keys_ref, values_ref, first_ref, query_ref, norm_ref, mods_ref, gain_ref, gain2_ref,
    bias_ref, fc1_b_ref, fc2_b_ref, table_ref,
):
    block = pl.program_id(0)
    width = x_ref.shape[1]
    row_count = query_ref.shape[0]

    @pl.when(block == 0)
    def _():
        row = 0
        for out_ref, size in zip((gain_ref, gain2_ref, bias_ref, fc1_b_ref, fc2_b_ref), sizes):
            out_ref[...] = joined(vector_ref, row, size)
            row += -(-size // TILE)
        modulation = dot(cond_ref[...], ada_ref[...]) + bias_ref[:, : 2 * width]
        mods_ref[...] = modulation
        scale = (1.0 + modulation[:, width:]) * gain_ref[...]
        table_ref[:, :width] = pick_table(scale)
        table_ref[:, width:] = pick_table(modulation[:, :width])
        norm_ref[...] = jnp.zeros_like(norm_ref)

    def most_square(values):
        row = lax.broadcasted_iota(jnp.int32, (width, TILE), 0)
        lane = lax.broadcasted_iota(jnp.int32, (width, TILE), 1)
        heads = jnp.where(row // HEAD_DIM == lane, 1.0, 0.0).astype(BF16)
        return jnp.max(dot((values * values).astype(BF16), heads), axis=0, keepdims=True)

    @pl.when(jnp.logical_not(block_active(block, info)))
    def _():
        first_ref[...] = jnp.zeros_like(first_ref)

    @pl.when(block_active(block, info))
    def _():
        x = x_ref[...].astype(F32)
        picks = slot_picks(BLOCK, block * BLOCK, info)
        mods = dot(picks, table_ref[...])
        xh, _ = normed(x)
        first = (xh * mods[:, :width] + mods[:, width:]).astype(BF16)
        first_ref[...] = first
        cosine, sine = rotary(position_ref[block], coarse_ref, fine_ref)
        keys = dot(first, weight_ref[:, width : 2 * width])
        norm_ref[0:1, :] = jnp.maximum(norm_ref[0:1, :], most_square(keys) * 1.02)
        for tile in range(width // TILE):
            cut = slice(tile * TILE, (tile + 1) * TILE)
            keys_ref[:, cut] = turn(keys[:, cut], cosine, sine).astype(BF16)
        values_ref[...] = dot(first, weight_ref[:, 2 * width :]).astype(BF16)

        @pl.when(block * BLOCK == info[4])
        def _():
            queries = dot(first, weight_ref[:, :width])
            for tile in range(width // TILE):
                cut = slice(tile * TILE, (tile + 1) * TILE)
                turned = turn(queries[:, cut], cosine, sine).astype(BF16)
                query_ref[:, cut] = (turned.astype(F32) * HEAD_DIM**-0.5).astype(BF16)


def project(info, x_all, positions, cond, ada, vectors, sizes, weight, tables, row_count):
    total, width = x_all.shape
    rows = pl.BlockSpec((BLOCK, width), active_rows)

    def whole(array):
        return pl.BlockSpec(array.shape, lambda i, *_: (0,) * array.ndim)

    shape = jax.ShapeDtypeStruct((total, width), BF16)
    lengths = [vectors.shape[0] * size for size in sizes]
    return pl.pallas_call(
        functools.partial(project_kernel, sizes),
        grid_spec=pltpu.PrefetchScalarGridSpec(
            num_scalar_prefetch=1,
            grid=(total // BLOCK,),
            in_specs=[
                rows,
                whole(positions),
                whole(cond),
                pl.BlockSpec((ada.shape[0], 2 * width), lambda i, *_: (0, 0)),
                whole(vectors),
                whole(weight),
                whole(tables[0]),
                whole(tables[1]),
            ],
            out_specs=[
                rows,
                rows,
                pl.BlockSpec((BLOCK, width), lambda i, *_: (i, 0)),
                pl.BlockSpec((row_count, width), lambda i, *_: (0, 0)),
                pl.BlockSpec((8, TILE), lambda i, *_: (0, 0)),
                pl.BlockSpec((8, 2 * width), lambda i, *_: (0, 0)),
            ]
            + [pl.BlockSpec((1, count), lambda i, *_: (0, 0)) for count in lengths],
            scratch_shapes=[pltpu.VMEM((16, 2 * width), BF16)],
        ),
        out_shape=[
            shape, shape, shape, jax.ShapeDtypeStruct((row_count, width), BF16),
            jax.ShapeDtypeStruct((8, TILE), F32),
            jax.ShapeDtypeStruct((8, 2 * width), F32),
        ]
        + [jax.ShapeDtypeStruct((1, count), F32) for count in lengths],
        compiler_params=params(),
        name="project",
    )(info, x_all, positions, cond, ada, vectors, weight, *tables)


def fill_key_features(feature_ref, info):
    total = feature_ref.shape[0]

    @pl.loop(0, total // KEY_ROWS)
    def _(chunk):
        start = pl.multiple_of(chunk * KEY_ROWS, KEY_ROWS)
        rows = start + lax.broadcasted_iota(jnp.int32, (KEY_ROWS, TILE), 0)
        lane = lax.broadcasted_iota(jnp.int32, (KEY_ROWS, TILE), 1)
        slot = slot_of(rows, info)
        masked = jnp.where(slot == lane, 0.0, FAR)
        ones = jnp.where(lane < 8, 1.0, 0.0)
        feature_ref[pl.ds(start, KEY_ROWS), :] = jnp.where(lane < 4, masked, ones).astype(BF16)


def stacked_heads(flipped):
    sub = lax.broadcasted_iota(jnp.int32, flipped.shape, 0)
    zero = jnp.zeros_like(flipped)
    return jnp.concatenate(
        [jnp.where(sub < HEAD_DIM, flipped, zero), jnp.where(sub < HEAD_DIM, zero, flipped)],
        axis=1,
    )


def slot_rows(first, count, info):
    sub = lax.broadcasted_iota(jnp.int32, (TILE, 2 * count), 0)
    lane = lax.broadcasted_iota(jnp.int32, (TILE, 2 * count), 1)
    return jnp.where(slot_of(first + lane % count, info) == sub, 1.0, 0.0), sub


def spans(low, count, step, carried, most):
    span = most
    while span:
        times = count // span
        carried = lax.fori_loop(0, times, functools.partial(step, span, low), carried)
        low = low + times * span
        count = count - times * span
        span //= 2
    return carried


def chunk_rows(chunk):
    return pl.ds(pl.multiple_of(chunk * KEY_ROWS, KEY_ROWS), KEY_ROWS)


def with_parts(base, sub, row):
    for place, piece in enumerate(thirds(row)):
        base = jnp.where(sub == 4 + place, piece.astype(F32), base)
    return base


def attend_kernel(
    info, q_ref, k_ref, v_ref, norm_ref, out_ref, mass_ref, feature_ref, sum_ref, row_ref
):
    pair = pl.program_id(0)

    @pl.when(pair == 0)
    def _():
        fill_key_features(feature_ref, info)

    row_count = q_ref.shape[0]
    wide = 2 * QUERY_ROWS
    head = lax.broadcasted_iota(jnp.int32, (1, TILE), 1)
    longest = [
        jnp.sqrt(jnp.max(jnp.where(head == 2 * pair + which, norm_ref[0:1, :], 0.0), axis=1, keepdims=True))
        for which in range(2)
    ]
    for part in range(row_count // QUERY_ROWS):
        first = info[4] + part * QUERY_ROWS
        cut = pl.ds(part * QUERY_ROWS, QUERY_ROWS)
        flipped = q_ref[cut, :].astype(F32).T
        onehot, sub = slot_rows(first, QUERY_ROWS, info)
        stack = stacked_heads(flipped)
        start, end = key_range(first, first + QUERY_ROWS - 1, info)
        low = start // KEY_ROWS
        count = (end + KEY_ROWS - 1) // KEY_ROWS - low
        sum_ref[...] = jnp.zeros_like(sum_ref)

        def scores_of(rows, queries):
            return dot(jnp.concatenate([k_ref[rows, :], feature_ref[rows, :]], axis=1), queries)

        own_rows = chunk_rows(first // KEY_ROWS)
        near = jnp.max(
            scores_of(own_rows, jnp.concatenate([stack, onehot], axis=0).astype(BF16)),
            axis=0, keepdims=True,
        )
        square = flipped * flipped
        bound = jnp.concatenate(
            [
                jnp.sqrt(jnp.sum(square[:HEAD_DIM], axis=0, keepdims=True)) * longest[0],
                jnp.sqrt(jnp.sum(square[HEAD_DIM:], axis=0, keepdims=True)) * longest[1],
            ],
            axis=1,
        )
        shift = near + LIFT
        narrow_range = jnp.max(bound - shift) < SAFE
        queries = jnp.concatenate([stack, with_parts(onehot, sub, -shift)], axis=0).astype(BF16)

        @pl.when(narrow_range)
        def _():
            def step(span, base, index, mass):
                weights, values = [], []
                for inner in range(span):
                    rows = chunk_rows(base + index * span + inner)
                    part_weights = jnp.exp(scores_of(rows, queries))
                    mass = mass + jnp.sum(part_weights, axis=0, keepdims=True)
                    weights.append(part_weights.astype(BF16))
                    values.append(v_ref[rows, :])
                sum_ref[...] += dot(
                    jnp.concatenate(values, axis=0), jnp.concatenate(weights, axis=0), ((0,), (0,))
                )
                return mass

            row_ref[0:1, :] = shift
            row_ref[1:2, :] = spans(low, count, step, jnp.zeros((1, wide), F32), 8)

        @pl.when(jnp.logical_not(narrow_range))
        def _():
            def step(span, base, index, carried):
                most, mass = carried
                scores, values = [], []
                new_most = most
                for inner in range(span):
                    rows = chunk_rows(base + index * span + inner)
                    some = scores_of(rows, queries)
                    new_most = jnp.maximum(new_most, jnp.max(some, axis=0, keepdims=True))
                    scores.append(some)
                    values.append(v_ref[rows, :])
                shrink = jnp.exp(most - new_most)
                mass = mass * shrink
                weights = []
                for some in scores:
                    part_weights = jnp.exp(some - new_most)
                    mass = mass + jnp.sum(part_weights, axis=0, keepdims=True)
                    weights.append(part_weights.astype(BF16))
                sum_ref[...] = sum_ref[...] * shrink + dot(
                    jnp.concatenate(values, axis=0), jnp.concatenate(weights, axis=0), ((0,), (0,))
                )
                return new_most, mass

            most, mass = spans(
                low, count, step, (jnp.full((1, wide), FAR * 2, F32), jnp.zeros((1, wide), F32)), 4
            )
            row_ref[0:1, :] = most + shift
            row_ref[1:2, :] = mass

        mass = row_ref[1:2, :]
        result = sum_ref[...] / mass
        joined = jnp.concatenate(
            [result[:HEAD_DIM, :QUERY_ROWS], result[HEAD_DIM:, QUERY_ROWS:]], axis=0
        )
        out_ref[cut, :] = joined.T
        mass_ref[0, pl.ds(part, 1), :] = row_ref[0:1, :] + jnp.log(mass)


def attend(info, queries, keys, values, norms):
    row_count, width = queries.shape
    total = keys.shape[0]
    pairs = width // TILE
    parts = row_count // QUERY_ROWS
    narrow = pl.BlockSpec((row_count, TILE), lambda i, *_: (0, i))
    tall = pl.BlockSpec((total, TILE), lambda i, *_: (0, i))
    return pl.pallas_call(
        attend_kernel,
        grid_spec=pltpu.PrefetchScalarGridSpec(
            num_scalar_prefetch=1,
            grid=(pairs,),
            in_specs=[narrow, tall, tall, pl.BlockSpec(norms.shape, lambda i, *_: (0, 0))],
            out_specs=[
                narrow,
                pl.BlockSpec((1, parts, 2 * QUERY_ROWS), lambda i, *_: (i, 0, 0)),
            ],
            scratch_shapes=[
                pltpu.VMEM((total, TILE), BF16),
                pltpu.VMEM((TILE, 2 * QUERY_ROWS), F32),
                pltpu.VMEM((8, 2 * QUERY_ROWS), F32),
            ],
        ),
        out_shape=[
            jax.ShapeDtypeStruct((row_count, width), F32),
            jax.ShapeDtypeStruct((pairs, parts, 2 * QUERY_ROWS), F32),
        ],
        compiler_params=params(),
        name="attend",
    )(info, queries, keys, values, norms)


def attend_back_kernel(
    info, q_ref, k_ref, v_ref, grad_ref, out_ref, mass_ref, dq_ref, dk_ref, dv_ref,
    feature_ref, dk_sum, dv_sum, dq_sum,
):
    @pl.when(pl.program_id(0) == 0)
    def _():
        fill_key_features(feature_ref, info)

    row_count = q_ref.shape[0]
    total = k_ref.shape[0]
    low_block, high_block = active_range(info)
    for block in range(total // BLOCK):

        @pl.when(jnp.logical_and(block >= low_block, block <= high_block))
        def _():
            rows = pl.ds(block * BLOCK, BLOCK)
            dk_sum[rows, :] = jnp.zeros((BLOCK, TILE), F32)
            dv_sum[rows, :] = jnp.zeros((BLOCK, TILE), F32)

    for part in range(row_count // QUERY_ROWS):
        first = info[4] + part * QUERY_ROWS
        cut = pl.ds(part * QUERY_ROWS, QUERY_ROWS)
        q_rows = q_ref[cut, :].astype(F32)
        g_rows = grad_ref[cut, :].astype(F32)
        q_flip = q_rows.T
        g_flip = g_rows.T
        product = g_flip * out_ref[cut, :].T
        delta = jnp.concatenate(
            [
                jnp.sum(product[:HEAD_DIM], axis=0, keepdims=True),
                jnp.sum(product[HEAD_DIM:], axis=0, keepdims=True),
            ],
            axis=1,
        )
        onehot, sub = slot_rows(first, QUERY_ROWS, info)

        queries = jnp.concatenate(
            [stacked_heads(q_flip), with_parts(onehot, sub, -mass_ref[0, pl.ds(part, 1), :])], axis=0
        ).astype(BF16)
        grads = jnp.concatenate(
            [stacked_heads(g_flip), with_parts(jnp.zeros_like(onehot), sub, -delta)], axis=0
        ).astype(BF16)
        lane = lax.broadcasted_iota(jnp.int32, (QUERY_ROWS, TILE), 1)

        def stacked(rows):
            zero = jnp.zeros_like(rows)
            return jnp.concatenate(
                [jnp.where(lane < HEAD_DIM, rows, zero), jnp.where(lane < HEAD_DIM, zero, rows)],
                axis=0,
            ).astype(BF16)

        q_stack = stacked(q_rows)
        g_stack = stacked(g_rows)
        start, end = key_range(first, first + QUERY_ROWS - 1, info)
        dq_sum[...] = jnp.zeros_like(dq_sum)

        def step(span, base, index, carried):
            all_keys, all_grads = [], []
            for inner in range(span):
                rows = chunk_rows(base + index * span + inner)
                keys = k_ref[rows, :]
                features = feature_ref[rows, :]
                probs = jnp.exp(dot(jnp.concatenate([keys, features], axis=1), queries))
                change = dot(jnp.concatenate([v_ref[rows, :], features], axis=1), grads)
                grad_scores = (probs * change).astype(BF16)
                dv_sum[rows, :] += dot(probs.astype(BF16), g_stack)
                dk_sum[rows, :] += dot(grad_scores, q_stack)
                all_keys.append(keys)
                all_grads.append(grad_scores)
            dq_sum[...] += dot(
                jnp.concatenate(all_keys, axis=0), jnp.concatenate(all_grads, axis=0), ((0,), (0,))
            )
            return carried

        low = start // KEY_ROWS
        spans(low, (end + KEY_ROWS - 1) // KEY_ROWS - low, step, 0, 8)
        result = dq_sum[...]
        joined = jnp.concatenate(
            [result[:HEAD_DIM, :QUERY_ROWS], result[HEAD_DIM:, QUERY_ROWS:]], axis=0
        )
        dq_ref[cut, :] = joined.T * HEAD_DIM**-0.5

    for block in range(total // BLOCK):

        @pl.when(jnp.logical_and(block >= low_block, block <= high_block))
        def _():
            rows = pl.ds(block * BLOCK, BLOCK)
            dk_ref[rows, :] = dk_sum[rows, :].astype(BF16)
            dv_ref[rows, :] = dv_sum[rows, :].astype(BF16)

        @pl.when(jnp.logical_or(block < low_block, block > high_block))
        def _():
            rows = pl.ds(block * BLOCK, BLOCK)
            dk_ref[rows, :] = jnp.zeros((BLOCK, TILE), BF16)
            dv_ref[rows, :] = jnp.zeros((BLOCK, TILE), BF16)


def attend_back(info, queries, keys, values, grads, attended, mass):
    row_count, width = queries.shape
    total = keys.shape[0]
    pairs = width // TILE
    parts = row_count // QUERY_ROWS
    narrow = pl.BlockSpec((row_count, TILE), lambda i, *_: (0, i))
    tall = pl.BlockSpec((total, TILE), lambda i, *_: (0, i))
    return pl.pallas_call(
        attend_back_kernel,
        grid_spec=pltpu.PrefetchScalarGridSpec(
            num_scalar_prefetch=1,
            grid=(pairs,),
            in_specs=[
                narrow,
                tall,
                tall,
                narrow,
                narrow,
                pl.BlockSpec((1, parts, 2 * QUERY_ROWS), lambda i, *_: (i, 0, 0)),
            ],
            out_specs=[narrow, tall, tall],
            scratch_shapes=[
                pltpu.VMEM((total, TILE), BF16),
                pltpu.VMEM((total, TILE), F32),
                pltpu.VMEM((total, TILE), F32),
                pltpu.VMEM((TILE, 2 * QUERY_ROWS), F32),
            ],
        ),
        out_shape=[
            jax.ShapeDtypeStruct((row_count, width), F32),
            jax.ShapeDtypeStruct((total, width), BF16),
            jax.ShapeDtypeStruct((total, width), BF16),
        ],
        compiler_params=params(),
        name="attend_back",
    )(info, queries, keys, values, grads, attended, mass)


def slot_sums(first_row, info, values):
    count, width = values.shape
    slot = slot_of(first_row + lax.broadcasted_iota(jnp.int32, (count, TILE), 0), info)
    sums = []
    for which in range(4):
        mask = jnp.where(slot == which, 1.0, 0.0)
        wide_mask = jnp.concatenate([mask] * (width // TILE), axis=1)
        sums.append(jnp.sum(values * wide_mask, axis=0, keepdims=True))
    return jnp.concatenate(sums + [jnp.zeros((4, width), F32)], axis=0)


def mlp_kernel(
    info, x_ref, attended_ref, cot_ref, cond_ref, ada_ref, bias_ref, gain_ref, out_w_ref,
    fc1_ref, fc1_b_ref, fc2_ref, fc2_b_ref,
    layer_ref, g_fc1_ref, g_fc2_ref, g_out_ref, g_att_ref, g_mid_ref, early_ref,
    pack_ref, mods_ref, second_ref, second_t_ref, grad2_ref, branch_ref, middle_ref, xh_ref, inverse_ref,
    sum2_ref, gsum_ref,
):
    step = pl.program_id(0)
    width = x_ref.shape[1]
    row_count = x_ref.shape[0]
    first_row = info[4]

    def mod(which):
        picks = slot_picks(row_count, first_row, info)
        return dot(picks, mods_ref[:, which * width : (which + 1) * width])

    @pl.when(step == 0)
    def _():
        mods = dot(cond_ref[...], ada_ref[:, 2 * width :]) + bias_ref[:, 2 * width :]
        mods_ref[:, : 4 * width] = pick_table(mods)
        mods_ref[:, 4 * width :] = pick_table(
            (1.0 + mods[:, 2 * width : 3 * width]) * gain_ref[...]
        )
        attended_low = attended_ref[...].astype(BF16)
        branch = dot(attended_low, out_w_ref[...])
        branch_ref[...] = branch
        middle = x_ref[...].astype(F32) + mod(0) * branch
        middle_ref[...] = middle
        xh, inverse = normed(middle)
        xh_ref[...] = xh
        inverse_ref[...] = jnp.broadcast_to(inverse, inverse_ref.shape)
        second = xh * mod(4) + mod(1)
        second_ref[...] = second.astype(BF16)
        second_t_ref[...] = second.T.astype(BF16)
        grad2 = (cot_ref[...].astype(F32) * mod(3)).astype(BF16)
        grad2_ref[...] = grad2
        pack_ref[...] = jnp.zeros_like(pack_ref)
        pack_ref[17:18, :] = jnp.sum(grad2.astype(F32), axis=0, keepdims=True)
        lane = lax.broadcasted_iota(jnp.int32, (1, width), 1)
        table = jnp.zeros((1, width), F32)
        for slot in range(4):
            table = jnp.where(lane == slot, info[8 + slot].astype(F32), table)
        pack_ref[22:23, :] = table
        sum2_ref[...] = jnp.zeros_like(sum2_ref)
        gsum_ref[...] = jnp.zeros_like(gsum_ref)

    pre = dot(second_ref[...], fc1_ref[...]) + fc1_b_ref[...]
    root = math.sqrt(2.0 / math.pi)
    square = pre * pre
    bend = jnp.tanh(root * pre * (1.0 + 0.044715 * square))
    half = 0.5 * (1.0 + bend)
    act = (pre * half).astype(BF16)
    slope = half + 0.5 * pre * (1.0 - bend * bend) * (root * (1.0 + 0.134145 * square))
    sum2_ref[...] += dot(act, fc2_ref[...])
    grad_act = dot(grad2_ref[...], fc2_ref[...], ((1,), (1,)))
    grad_pre = (grad_act * slope).astype(BF16)
    pack_ref[pl.ds(18 + step, 1), :] = jnp.sum(grad_pre.astype(F32), axis=0, keepdims=True)
    g_fc2_ref[...] = dot(act, grad2_ref[...], ((0,), (0,))).astype(BF16)
    g_fc1_ref[...] = dot(second_t_ref[...], grad_pre).astype(BF16)
    gsum_ref[...] += dot(grad_pre, fc1_ref[...], ((1,), (1,)))

    @pl.when(step == pl.num_programs(0) - 1)
    def _():
        branch2 = sum2_ref[...] + fc2_b_ref[...]
        layer_ref[...] = (middle_ref[...] + mod(3) * branch2).astype(BF16)
        upstream = cot_ref[...].astype(F32)
        pack_ref[12:16, :] = slot_sums(first_row, info, upstream * branch2)[:4]
        grad = gsum_ref[...]
        xh = xh_ref[...]
        picks = slot_picks(row_count, first_row, info)
        pack_ref[4:8, :] = slot_sums(first_row, info, grad)[:4]
        moved = grad * xh
        pack_ref[8:12, :] = slot_sums(first_row, info, moved * gain_ref[...])[:4]
        pack_ref[16:17, :] = jnp.sum(moved * (1.0 + mod(2)), axis=0, keepdims=True)
        h = grad * mod(4)
        inverse = inverse_ref[:, 0:1]
        g_mid = upstream + inverse * (
            h - jnp.mean(h, axis=1, keepdims=True) - xh * jnp.mean(h * xh, axis=1, keepdims=True)
        )
        g_mid_ref[...] = g_mid
        pack_ref[0:4, :] = slot_sums(first_row, info, g_mid * branch_ref[...])[:4]
        early_ref[...] = pack_ref[...].astype(BF16)
        g_branch = (g_mid * mod(0)).astype(BF16)
        g_out_ref[...] = dot(attended_ref[...].astype(BF16), g_branch, ((0,), (0,))).astype(BF16)
        g_att_ref[...] = dot(g_branch, out_w_ref[...], ((1,), (1,))).astype(BF16)


def mlp(info, x, attended, cot, cond, ada, bias, gain, out_w, fc1, fc1_b, fc2, fc2_b):
    row_count, width = x.shape
    hidden = fc1.shape[1]
    chunk = CHUNK

    def whole(shape):
        return pl.BlockSpec(shape, lambda i, *_: (0,) * len(shape))

    columns = pl.BlockSpec((width, chunk), lambda i, *_: (0, i))
    lines = pl.BlockSpec((chunk, width), lambda i, *_: (i, 0))
    part = pl.BlockSpec((1, chunk), lambda i, *_: (0, i))
    rows = (row_count, width)
    return pl.pallas_call(
        mlp_kernel,
        grid_spec=pltpu.PrefetchScalarGridSpec(
            num_scalar_prefetch=1,
            grid=(hidden // chunk,),
            in_specs=[
                whole(rows), whole(rows), whole(rows), whole(cond.shape), whole(ada.shape),
                whole(bias.shape), whole(gain.shape), whole(out_w.shape), columns, part, lines,
                whole(fc2_b.shape),
            ],
            out_specs=[
                whole(rows), columns, lines, whole(out_w.shape), whole(rows), whole(rows),
                whole((32, width)),
            ],
            scratch_shapes=[
                pltpu.VMEM((32, width), F32),
                pltpu.VMEM((16, 5 * width), BF16),
                pltpu.VMEM(rows, BF16),
                pltpu.VMEM((width, row_count), BF16),
                pltpu.VMEM(rows, BF16),
                pltpu.VMEM(rows, F32),
                pltpu.VMEM(rows, F32),
                pltpu.VMEM(rows, F32),
                pltpu.VMEM((row_count, TILE), F32),
                pltpu.VMEM(rows, F32),
                pltpu.VMEM(rows, F32),
            ],
        ),
        out_shape=[
            jax.ShapeDtypeStruct(rows, BF16),
            jax.ShapeDtypeStruct(fc1.shape, BF16),
            jax.ShapeDtypeStruct(fc2.shape, BF16),
            jax.ShapeDtypeStruct(out_w.shape, BF16),
            jax.ShapeDtypeStruct(rows, BF16),
            jax.ShapeDtypeStruct(rows, F32),
            jax.ShapeDtypeStruct((32, width), BF16),
        ],
        compiler_params=params(),
        name="mlp",
    )(info, x, attended, cot, cond, ada, bias, gain, out_w, fc1, fc1_b, fc2, fc2_b)


MESH = pl.DeviceIdType.MESH


def piece_of(array, which):
    rows, columns = array
    if rows % 32 == 0 and (columns // 2) % TILE == 0:
        return (which % 2) * (rows // 2), rows // 2, (which // 2) * (columns // 2), columns // 2
    return 0, rows, which * (columns // 4), columns // 4


def cut_of(start, size, whole, unit):
    if size == whole:
        return slice(None)
    return pl.ds(pl.multiple_of(start, unit), size)


class Place:
    def __init__(self):
        self.wide = lax.axis_index("wide")
        self.narrow = lax.axis_index("narrow")
        self.z = self.narrow // 2
        self.core = self.narrow % 2
        self.quarter = self.wide % 4
        self.bit1 = 1 + self.core
        self.bit2 = 2 - self.core
        self.near = self.z + 1 - 2 * (self.z % 2)
        low = self.z < 2
        self.order = (self.near, jnp.where(low, 2, 1), jnp.where(low, 3, 0))

    def flip(self, value, bit):
        return value + bit * (1 - 2 * ((value // bit) % 2))

    def partner(self, bit):
        return (self.flip(self.wide, bit), self.narrow)

    def sibling(self):
        return (self.wide, self.narrow + 1 - 2 * self.core)

    def column(self, narrow):
        return (self.wide, narrow)

    def up(self):
        return (self.wide, jnp.minimum(self.narrow + 2, 7))

    def down(self):
        return (self.wide, jnp.maximum(self.narrow - 2, 0))


def greet(place, size):
    barrier = pltpu.get_barrier_semaphore()
    for step in range(1, size):
        pl.semaphore_signal(
            barrier, inc=1, device_id=place.column((place.narrow + step) % size), device_id_type=MESH
        )
    for bit in (1, 2):
        pl.semaphore_signal(barrier, inc=1, device_id=place.partner(bit), device_id_type=MESH)
    pl.semaphore_wait(barrier, size + 1)


def gather_kernel(shapes, size, *refs):
    count = len(shapes)
    shard_refs = refs[:count]
    x_ref, position_ref, vector_ref = refs[count : count + 3]
    full_refs = refs[count + 3 : 2 * count + 3]
    x_all, position_all, vector_all = refs[2 * count + 3 : 2 * count + 6]
    (
        own_sems, own_send, own_recv, line_send, line_recv, turn_send, turn_recv, next_send,
        next_recv, back_send, back_recv, small_send, small_recv,
    ) = refs[2 * count + 6 :]
    place = Place()
    narrow, z, core = place.narrow, place.z, place.core
    greet(place, size)

    def remote(source, target, send, recv, device):
        return pltpu.make_async_remote_copy(
            src_ref=source, dst_ref=target, send_sem=send, recv_sem=recv, device_id=device,
            device_id_type=MESH,
        )

    def region(a, owner, which):
        rows, columns = shapes[a]
        first_row, row_count, first_column, column_count = piece_of(shapes[a], which)
        start = pl.multiple_of(owner * rows + first_row, 16)
        if isinstance(first_column, int):
            return full_refs[a].at[pl.ds(start, row_count), :]
        lanes = pl.ds(pl.multiple_of(first_column, TILE), column_count)
        return full_refs[a].at[pl.ds(start, row_count), lanes]

    def shard(a, owner):
        rows, _ = shapes[a]
        return full_refs[a].at[pl.ds(pl.multiple_of(owner * rows, 16), rows), :]

    def own_piece(a):
        first_row, row_count, first_column, column_count = piece_of(shapes[a], place.quarter)
        if isinstance(first_row, int) and first_row == 0:
            rows = slice(None)
        else:
            rows = pl.ds(pl.multiple_of(first_row, 16), row_count)
        if isinstance(first_column, int):
            return shard_refs[a].at[rows, :]
        return shard_refs[a].at[rows, pl.ds(pl.multiple_of(first_column, TILE), column_count)]

    block = x_ref.shape[0]

    def tokens_of(owner):
        return x_all.at[pl.ds(pl.multiple_of(owner * block, 16), block), :]

    owner_of = [zp * 2 + core for zp in place.order]
    smalls = []
    for step in range(1, size):
        device = place.column((narrow + step) % size)
        smalls.append(
            remote(vector_ref, vector_all.at[narrow], small_send.at[0, step], small_recv.at[0, step], device)
        )
        smalls.append(
            remote(position_ref, position_all.at[narrow], small_send.at[1, step], small_recv.at[1, step], device)
        )
    for copy in smalls:
        copy.start()
    local = [
        pltpu.make_async_copy(vector_ref, vector_all.at[narrow], own_sems.at[count + 1]),
        pltpu.make_async_copy(position_ref, position_all.at[narrow], own_sems.at[count + 2]),
        pltpu.make_async_copy(x_ref, tokens_of(narrow), own_sems.at[count]),
    ]
    for a in range(count):
        local.append(pltpu.make_async_copy(shard_refs[a], shard(a, narrow), own_sems.at[a]))
    for copy in local:
        copy.start()

    def line_copies(a, owner, source, target):
        return (
            remote(source, target, line_send.at[a, owner // 2, 0], line_recv.at[a, owner // 2], place.up()),
            remote(source, target, line_send.at[a, owner // 2, 1], line_recv.at[a, owner // 2], place.down()),
        )

    def line_pair(a, owner):
        if a == count:
            target = tokens_of(owner)
            source = target
        else:
            target = region(a, owner, place.quarter)
            source = target
        return line_copies(a, owner, source, target)

    def own_pair(a):
        if a == count:
            return line_copies(a, narrow, x_ref, tokens_of(narrow))
        return line_copies(a, narrow, own_piece(a), region(a, narrow, place.quarter))

    def own_to_sibling(a):
        if a == count:
            return remote(x_ref, tokens_of(narrow), own_send.at[a], own_recv.at[a], place.sibling())
        return remote(shard_refs[a], shard(a, narrow), own_send.at[a], own_recv.at[a], place.sibling())

    def start_own(a):
        up, down = own_pair(a)
        pl.when(z < 3)(up.start)
        pl.when(z > 0)(down.start)
        own_to_sibling(a).start()

    def forwards(a, index):
        zp = place.order[index]
        if a == count:
            near = jnp.logical_and(zp - z < 2, z - zp < 2)
            return (
                jnp.logical_and(jnp.logical_and(zp < z, z < 3), near),
                jnp.logical_and(jnp.logical_and(zp > z, z > 0), near),
            )
        return jnp.logical_and(zp < z, z < 3), jnp.logical_and(zp > z, z > 0)

    def arrives(index):
        zp = place.order[index]
        return jnp.logical_and(zp - z < 3, z - zp < 3)

    def quarters(bit_first):
        first = place.flip(place.quarter, place.bit1)
        return first, place.flip(place.quarter, place.bit2), place.flip(first, place.bit2)

    def turn_copy(a, index):
        target = region(a, owner_of[index], place.quarter)
        return remote(
            target, target, turn_send.at[a, index], turn_recv.at[a, index], place.partner(place.bit1)
        )

    def next_copy(a, index, which):
        quarter = place.quarter if which == 0 else place.flip(place.quarter, place.bit1)
        target = region(a, owner_of[index], quarter)
        return remote(
            target, target, next_send.at[a, index, which], next_recv.at[a, index, which],
            place.partner(place.bit2),
        )

    def back_copy(a, index):
        if a == count:
            target = tokens_of(owner_of[index])
        else:
            target = shard(a, owner_of[index])
        return remote(
            target, target, back_send.at[a, index], back_recv.at[a, index], place.sibling()
        )

    def on_line(a, index):
        up, down = line_pair(a, owner_of[index])

        def work():
            up.wait_recv()
            goes_up, goes_down = forwards(a, index)
            pl.when(goes_up)(up.start)
            pl.when(goes_down)(down.start)
            if a == count:
                back_copy(a, index).start()
            else:
                turn_copy(a, index).start()
                next_copy(a, index, 0).start()

        if a == count:
            pl.when(arrives(index))(work)
        else:
            work()

    def turned(index):
        for a in range(count):
            turn_copy(a, index).wait_recv()
            next_copy(a, index, 1).start()

    def on_lines(index):
        for a in range(count):
            on_line(a, index)

    token_up, token_down = own_pair(count)
    for a in range(count):
        start_own(a)
    own_to_sibling(count).start()
    pl.when(z == 0)(token_up.start)
    pl.when(z == 3)(token_down.start)
    on_lines(0)
    pl.when(z == 1)(token_up.start)
    pl.when(z == 2)(token_down.start)
    on_lines(1)
    turned(0)
    on_lines(2)
    pl.when(z == 2)(token_up.start)
    pl.when(z == 1)(token_down.start)
    turned(1)
    turned(2)
    for index in range(3):
        on_line(count, index)
    for index in range(3):
        for a in range(count):
            next_copy(a, index, 0).wait_recv()
            next_copy(a, index, 1).wait_recv()
            back_copy(a, index).start()
    for a in range(count):
        for index in range(3):
            back_copy(a, index).wait_recv()
    for a in range(count + 1):
        own_to_sibling(a).wait()
        up, down = own_pair(a)
        pl.when(z < 3)(up.wait_send)
        pl.when(z > 0)(down.wait_send)
    for index in range(3):

        @pl.when(arrives(index))
        def _():
            back_copy(count, index).wait()
            goes_up, goes_down = forwards(count, index)
            up, down = line_pair(count, owner_of[index])
            pl.when(goes_up)(up.wait_send)
            pl.when(goes_down)(down.wait_send)

        for a in range(count):
            goes_up, goes_down = forwards(a, index)
            up, down = line_pair(a, owner_of[index])
            pl.when(goes_up)(up.wait_send)
            pl.when(goes_down)(down.wait_send)
            turn_copy(a, index).wait_send()
            next_copy(a, index, 0).wait_send()
            next_copy(a, index, 1).wait_send()
            back_copy(a, index).wait_send()
    for copy in local:
        copy.wait()
    for copy in smalls:
        copy.wait()


def gather_all(x, positions, vector, shards, size):
    count = len(shards)
    shapes = tuple(shard.shape for shard in shards)
    anywhere = pl.BlockSpec(memory_space=pl.ANY)
    dma = pltpu.SemaphoreType.DMA
    out_shape = [
        jax.ShapeDtypeStruct((size * shard.shape[0], shard.shape[1]), shard.dtype) for shard in shards
    ] + [
        jax.ShapeDtypeStruct((size * x.shape[0], x.shape[1]), x.dtype),
        jax.ShapeDtypeStruct((size, *positions.shape), positions.dtype),
        jax.ShapeDtypeStruct((size, *vector.shape), vector.dtype),
    ]
    return pl.pallas_call(
        functools.partial(gather_kernel, shapes, size),
        out_shape=out_shape,
        in_specs=[anywhere] * (count + 3),
        out_specs=[anywhere] * (count + 3),
        scratch_shapes=[
            dma((count + 3,)),
            dma((count + 1,)),
            dma((count + 1,)),
            dma((count + 1, 4, 2)),
            dma((count + 1, 4)),
            dma((count, 3)),
            dma((count, 3)),
            dma((count, 3, 2)),
            dma((count, 3, 2)),
            dma((count + 1, 3)),
            dma((count + 1, 3)),
            dma((2, size)),
            dma((2, size)),
        ],
        compiler_params=pltpu.CompilerParams(collective_id=1, has_side_effects=True),
        name="gather_all",
    )(*shards, x, positions, vector)


def add_into(target, source):
    rows = target.shape[-2]
    step = 32 if rows % 32 == 0 else 16
    lead = target.shape[:-2]

    @pl.loop(0, rows // step)
    def _(turn_index):
        cut = pl.ds(pl.multiple_of(turn_index * step, 16), step)
        for index in np.ndindex(*lead):
            at = (*index, cut, slice(None))
            target[at] = target[at] + source[at]


def finish_rows(info, grad, x, g_mid, mods, gain):
    width = x.shape[1]
    first_row = info[4]
    scale = 1.0 + mods[:, width:]
    picks = slot_picks(x.shape[0], first_row, info)
    xh, inverse = normed(x.astype(F32))
    moved = grad * xh
    sums = jnp.concatenate(
        [slot_sums(first_row, info, grad), slot_sums(first_row, info, moved * gain)], axis=1
    )
    g_gain = jnp.sum(moved * dot(picks, pick_table(scale)), axis=0, keepdims=True)
    h = grad * dot(picks, pick_table(scale * gain))
    tokens = g_mid + inverse * (
        h - jnp.mean(h, axis=1, keepdims=True) - xh * jnp.mean(h * xh, axis=1, keepdims=True)
    )
    return tokens, sums, g_gain


def folded(values, columns):
    return jnp.concatenate(
        [values[:, at : at + columns] for at in range(0, values.shape[1], columns)], axis=0
    )


def reduce_kernel(shapes, summed, size, groups, info, *refs):
    count, made = len(shapes), summed - 1
    refs = list(refs)
    grad_refs = [refs.pop(0) for _ in range(count - 1)]
    grad_refs.insert(made, None)
    (
        first_ref, dk_ref, dv_ref, early_ref, dq_ref, weight_ref, position_ref, coarse_ref, fine_ref,
        x_ref, g_mid_ref, mods_ref, gain_ref,
    ) = (refs.pop(0) for _ in range(13))
    out_refs = [refs.pop(0) for _ in range(count)]
    tokens_ref, early_all, late_all = (refs.pop(0) for _ in range(3))
    rest = refs
    own, turned, nexted, far = ([rest.pop(0) for _ in range(count)] for _ in range(4))
    side, upward, downward = ([rest.pop(0) for _ in range(summed)] for _ in range(3))
    (
        first_in, dk_in, dv_in, dw_sum, made_out, dx_out,
        dx_own, dx_side, dx_up, dx_down, late_ref, early_in, late_in, early_sum, late_sum,
        own_sem, side_send, side_recv, turn_send, turn_recv, next_send, next_recv, line_send,
        line_recv, far_send, far_recv, share_send, share_recv, final_sem,
        block_sem, dx_side_send, dx_side_recv, dx_send, dx_recv,
        pack_send, pack_recv, wide_send, wide_recv, pack_own,
    ) = rest
    place = Place()
    z, core, narrow = place.z, place.core, place.narrow
    barrier = pltpu.get_barrier_semaphore()
    for step in range(1, size):
        pl.semaphore_signal(
            barrier, inc=1, device_id=place.column((narrow + step) % size), device_id_type=MESH
        )
    for step in range(1, groups):
        pl.semaphore_signal(
            barrier, inc=1, device_id=((place.wide + step) % groups, narrow), device_id_type=MESH
        )
    pl.semaphore_wait(barrier, size + groups - 2)

    def remote(source, target, send, recv, device):
        return pltpu.make_async_remote_copy(
            src_ref=source, dst_ref=target, send_sem=send, recv_sem=recv, device_id=device,
            device_id_type=MESH,
        )

    def piece(ref, a, which, lead):
        rows, columns = shapes[a]
        first_row, row_count, first_column, column_count = piece_of(shapes[a], which)
        return ref.at[
            (*lead, cut_of(first_row, row_count, rows, 16), cut_of(first_column, column_count, columns, TILE))
        ]

    quarter = place.quarter
    other1 = place.flip(quarter, place.bit1)
    other2 = place.flip(quarter, place.bit2)
    every = (slice(None),)

    def pack_copies(which, source, target):
        return [
            remote(
                source, target.at[narrow], pack_send.at[which, step], pack_recv.at[which, step],
                place.column((narrow + step) % size),
            )
            for step in range(1, size)
        ]

    def wide_copies(which, source, target):
        return [
            remote(
                source, target.at[place.wide], wide_send.at[which, step], wide_recv.at[which, step],
                ((place.wide + step) % groups, narrow),
            )
            for step in range(1, groups)
        ]

    early_copies = pack_copies(0, early_ref, early_in)
    early_own = pltpu.make_async_copy(early_ref, early_in.at[narrow], pack_own.at[0])
    early_own.start()

    side_copy, own_copy = [], []
    for a in range(count):
        if a == made:
            side_copy.append(
                remote(made_out, side[a], side_send.at[a], side_recv.at[a], place.sibling())
            )
            own_copy.append(None)
            continue
        if a < summed:
            side_copy.append(
                remote(grad_refs[a].at[:, 1 - core], side[a], side_send.at[a], side_recv.at[a], place.sibling())
            )
            own_copy.append(pltpu.make_async_copy(grad_refs[a].at[:, core], own[a], own_sem.at[a]))
            side_copy[a].start()
        else:
            own_copy.append(pltpu.make_async_copy(grad_refs[a], own[a].at[0], own_sem.at[a]))
        own_copy[a].start()

    def dx_copy(upwards, slot):
        zp = jnp.clip(z + 1 + slot if upwards else z - 1 - slot, 0, 3)
        way = 0 if upwards else 1
        landing = dx_up if upwards else dx_down
        return remote(
            dx_own.at[zp], landing.at[slot], dx_send.at[way, slot], dx_recv.at[way, slot],
            place.up() if upwards else place.down(),
        )

    def dx_middle():
        @pl.when(z < 3)
        def _():
            @pl.when(z > 0)
            def _():
                dx_copy(True, 1).wait_recv()
                add_into(dx_own.at[jnp.minimum(z + 1, 3)], dx_up.at[1])

            dx_copy(True, 0).start()

        @pl.when(z > 0)
        def _():
            @pl.when(z < 3)
            def _():
                dx_copy(False, 1).wait_recv()
                add_into(dx_own.at[jnp.maximum(z - 1, 0)], dx_down.at[1])

            dx_copy(False, 0).start()

    def dx_end():
        @pl.when(z > 0)
        def _():
            dx_copy(True, 0).wait_recv()
            add_into(dx_own.at[z], dx_up.at[0])

        @pl.when(z < 3)
        def _():
            dx_copy(False, 0).wait_recv()
            add_into(dx_own.at[z], dx_down.at[0])

        pl.when(z < 3)(dx_copy(True, 0).wait_send)
        pl.when(z < 2)(dx_copy(True, 1).wait_send)
        pl.when(z > 0)(dx_copy(False, 0).wait_send)
        pl.when(z > 1)(dx_copy(False, 1).wait_send)

    def turn_copy(a):
        rows, columns = shapes[a]
        out = []
        for bit in (1, 2):
            if bit == 1:
                there = (slice(None), pl.ds(pl.multiple_of((1 - quarter % 2) * (rows // 2), 16), rows // 2), slice(None))
                landing = turned[a].at[:, pl.ds(0, rows // 2), :]
            else:
                there = (slice(None), slice(None), pl.ds(pl.multiple_of((1 - quarter // 2) * (columns // 2), TILE), columns // 2))
                landing = turned[a].at[:, :, pl.ds(0, columns // 2)]
            out.append(
                remote(own[a].at[there], landing, turn_send.at[a], turn_recv.at[a], place.partner(bit))
            )
        return out

    def by_core(copies, what):
        pl.when(core == 0)(getattr(copies[0], what))
        pl.when(core == 1)(getattr(copies[1], what))

    def join(a):
        if a != made:
            own_copy[a].wait()
        if a < summed:
            side_copy[a].wait_recv()
            add_into(own[a], side[a])

    def start_turn(a):
        by_core(turn_copy(a), "start")

    def next_copy(a):
        return remote(
            piece(own[a], a, other2, every), nexted[a], next_send.at[a], next_recv.at[a],
            place.partner(place.bit2),
        )

    def start_next(a):
        rows, columns = shapes[a]
        by_core(turn_copy(a), "wait_recv")

        @pl.when(core == 0)
        def _():
            add_into(
                own[a].at[:, pl.ds(pl.multiple_of((quarter % 2) * (rows // 2), 16), rows // 2), :],
                turned[a].at[:, pl.ds(0, rows // 2), :],
            )

        @pl.when(core == 1)
        def _():
            add_into(
                own[a].at[:, :, pl.ds(pl.multiple_of((quarter // 2) * (columns // 2), TILE), columns // 2)],
                turned[a].at[:, :, pl.ds(0, columns // 2)],
            )

        next_copy(a).start()

    def line_copy(a, zp, upwards, source):
        if upwards:
            return remote(source, upward[a].at[zp], line_send.at[a, zp, 0], line_recv.at[a, zp, 0], place.up())
        return remote(source, downward[a].at[zp], line_send.at[a, zp, 1], line_recv.at[a, zp, 1], place.down())

    def start_line(a):
        next_copy(a).wait_recv()
        add_into(piece(own[a], a, quarter, every), nexted[a])
        if a >= summed:
            return
        for zp in (3, 2, 1):
            pl.when(z == 0)(line_copy(a, zp, True, piece(own[a], a, quarter, (zp,))).start)
            low = 3 - zp
            pl.when(z == 3)(line_copy(a, low, False, piece(own[a], a, quarter, (low,))).start)

    def middle_line(a):
        if a >= summed:
            return
        for zp in (3, 2, 1):

            @pl.when(jnp.logical_and(z > 0, z < zp))
            def _():
                copy = line_copy(a, zp, True, upward[a].at[zp])
                copy.wait_recv()
                add_into(upward[a].at[zp], piece(own[a], a, quarter, (zp,)))
                copy.start()

            low = 3 - zp

            @pl.when(jnp.logical_and(z < 3, z > low))
            def _():
                copy = line_copy(a, low, False, downward[a].at[low])
                copy.wait_recv()
                add_into(downward[a].at[low], piece(own[a], a, quarter, (low,)))
                copy.start()

    def share_copy(a, which, bit_place, slot):
        source = piece(out_refs[a], a, which, ())
        return remote(source, source, share_send.at[a, slot], share_recv.at[a, slot], place.partner(bit_place))

    def kept(a):
        return piece(own[a], a, quarter, (z,) if a < summed else (0,))

    def final_copy(a):
        return pltpu.make_async_copy(
            kept(a), piece(out_refs[a], a, quarter, ()), final_sem.at[a]
        )

    def far_copy(a, which, bit):
        return remote(
            kept(a), far[a].at[which], far_send.at[a, which],
            far_recv.at[a, which], (place.flip(place.wide, bit), narrow),
        )

    def end_line(a):
        mine = kept(a)
        if a < summed:

            @pl.when(z > 0)
            def _():
                line_copy(a, z, True, mine).wait_recv()
                add_into(mine, upward[a].at[z])

            @pl.when(z < 3)
            def _():
                line_copy(a, z, False, mine).wait_recv()
                add_into(mine, downward[a].at[z])

        bit, which = 4, 0
        while bit < groups:
            copy = far_copy(a, which, bit)
            copy.start()
            copy.wait()
            add_into(mine, far[a].at[which])
            bit, which = bit * 2, which + 1
        final_copy(a).start()

    def start_share(a):
        final_copy(a).wait()
        share_copy(a, quarter, place.bit1, 0).start()
        share_copy(a, quarter, place.bit2, 1).start()

    def pass_share(a):
        share_copy(a, quarter, place.bit1, 0).wait_recv()
        share_copy(a, other1, place.bit2, 2).start()

    def close(a):
        share_copy(a, quarter, place.bit2, 1).wait_recv()
        share_copy(a, other1, place.bit2, 2).wait_recv()
        share_copy(a, quarter, place.bit1, 0).wait_send()
        share_copy(a, quarter, place.bit2, 1).wait_send()
        share_copy(a, other1, place.bit2, 2).wait_send()
        by_core(turn_copy(a), "wait_send")
        next_copy(a).wait_send()
        if a >= summed:
            return
        side_copy[a].wait_send()
        for zp in range(4):
            mine = piece(own[a], a, quarter, (zp,))
            pl.when(z < zp)(line_copy(a, zp, True, mine).wait_send)
            pl.when(z > zp)(line_copy(a, zp, False, mine).wait_send)

    def column_total(landed):
        total = landed[0].astype(F32)
        for step in range(1, size):
            total = total + landed[step].astype(F32)
        return total.astype(BF16)

    width = x_ref.shape[1]
    block_rows = x_ref.shape[0]

    def zp_of(step):
        near = place.near
        return jnp.where(
            step == 0, (z + 2) % 4, jnp.where(step == 1, near, jnp.where(step == 2, (near + 2) % 4, z))
        )

    def needed(step):
        zp = zp_of(step)
        return jnp.logical_and(zp - z < 3, z - zp < 3)

    def fetch(turn_index):
        parity = turn_index % 2
        owner = zp_of(turn_index // 2) * 2 + jnp.where(parity == 0, 1 - core, core)
        rows = pl.ds(pl.multiple_of(owner * block_rows, block_rows), block_rows)
        return [
            pltpu.make_async_copy(ref.at[rows, :], landing.at[parity], block_sem.at[which, parity])
            for which, (ref, landing) in enumerate(((first_ref, first_in), (dk_ref, dk_in), (dv_ref, dv_in)))
        ]

    def dx_side_copy(step):
        return remote(
            dx_out.at[step % 2], dx_side.at[zp_of(step)], dx_side_send.at[step], dx_side_recv.at[step],
            place.sibling(),
        )

    def turned_back(values, cosine, sine):
        tiles = []
        for tile in range(width // TILE):
            cut = slice(tile * TILE, (tile + 1) * TILE)
            tiles.append(turn_back(values[:, cut].astype(F32), cosine, sine).astype(BF16))
        return jnp.concatenate(tiles, axis=1)

    dw_sum[...] = jnp.zeros_like(dw_sum)
    for copy in fetch(0):
        copy.start()

    @pl.loop(0, 8)
    def _(turn_index):
        step = turn_index // 2
        parity = turn_index % 2
        zp = zp_of(step)
        owner = zp * 2 + jnp.where(parity == 0, 1 - core, core)

        @pl.when(turn_index < 7)
        def _():
            for copy in fetch(turn_index + 1):
                copy.start()

        for copy in fetch(turn_index):
            copy.wait()

        @pl.when(needed(step))
        def _():
            cosine, sine = rotary(position_ref[owner], coarse_ref, fine_ref)
            both = jnp.concatenate(
                [turned_back(dk_in[parity], cosine, sine), dv_in[parity]], axis=1
            )
            dw_sum[:, width:] += dot(first_in[parity], both, ((0,), (0,)))
            total = dot(both, weight_ref[:, width:], ((1,), (1,))).astype(BF16)

            @pl.when(parity == 0)
            def _():
                @pl.when(jnp.logical_and(step > 1, needed(step - 2)))
                def _():
                    dx_side_copy(step - 2).wait_send()

                dx_out[step % 2] = total
                dx_side_copy(step).start()

            @pl.when(parity == 1)
            def _():
                dx_own[zp] = total
                dx_side_copy(step).wait_recv()
                add_into(dx_own.at[zp], dx_side.at[zp])

        @pl.when(turn_index == 1)
        def _():
            pl.when(z < 2)(dx_copy(True, 1).start)
            pl.when(z > 1)(dx_copy(False, 1).start)
            join(0)
            start_turn(0)

        @pl.when(turn_index == 3)
        def _():
            for a in range(1, count):
                if a != made:
                    join(a)
                    start_turn(a)

    cosine, sine = rotary(position_ref[narrow], coarse_ref, fine_ref)
    dq = turned_back(dq_ref[...], cosine, sine)
    dw_sum[:, :width] = dot(first_in[1], dq, ((0,), (0,)))
    dx_own[z] = (
        dx_own[z].astype(F32) + dot(dq, weight_ref[:, :width], ((1,), (1,)))
    ).astype(BF16)
    shard_rows = shapes[made][0]

    @pl.loop(0, 4)
    def _(zp):
        mine = pl.ds(pl.multiple_of((2 * zp + core) * shard_rows, 16), shard_rows)
        other = pl.ds(pl.multiple_of((2 * zp + 1 - core) * shard_rows, 16), shard_rows)
        own[made][zp] = dw_sum[mine, :].astype(BF16)
        made_out[zp] = dw_sum[other, :].astype(BF16)

    side_copy[made].start()
    dx_middle()
    for a in range(count):
        if a != made:
            start_next(a)
    join(made)
    start_turn(made)
    for copy in early_copies:
        copy.start()
    for a in range(made):
        start_line(a)
    for a in range(summed, count):
        start_line(a)
        end_line(a)
        start_share(a)
    start_next(made)
    for a in range(made):
        middle_line(a)
    dx_end()
    for a in range(made):
        end_line(a)
        start_share(a)
    start_line(made)
    tokens, sums, g_gain = finish_rows(
        info, dx_own[z].astype(F32), x_ref[...], g_mid_ref[...], mods_ref[...], gain_ref[...]
    )
    tokens_ref[...] = tokens
    quarter_width = sums.shape[1] // 4
    late_ref[...] = jnp.concatenate(
        [
            folded(sums[:4], quarter_width),
            folded(g_gain, quarter_width),
            jnp.zeros((14, quarter_width), F32),
        ],
        axis=0,
    ).astype(BF16)
    late_copies = pack_copies(1, late_ref, late_in)
    for copy in late_copies:
        copy.start()
    late_own = pltpu.make_async_copy(late_ref, late_in.at[narrow], pack_own.at[1])
    late_own.start()
    middle_line(made)
    for a in range(count):
        if a != made:
            pass_share(a)
    end_line(made)
    start_share(made)
    for copy in early_copies:
        copy.wait_recv()
    early_own.wait()
    early_sum[...] = column_total(early_in)
    early_wide = wide_copies(0, early_sum, early_all)
    for copy in early_wide:
        copy.start()
    early_final = pltpu.make_async_copy(early_sum, early_all.at[place.wide], pack_own.at[2])
    early_final.start()
    for copy in late_copies:
        copy.wait_recv()
    late_own.wait()
    late_sum[...] = column_total(late_in)
    late_wide = wide_copies(1, late_sum, late_all)
    for copy in late_wide:
        copy.start()
    late_final = pltpu.make_async_copy(late_sum, late_all.at[place.wide], pack_own.at[3])
    late_final.start()
    pass_share(made)
    for a in range(count):
        close(a)
    for step in (2, 3):
        pl.when(needed(step))(dx_side_copy(step).wait_send)
    pl.when(jnp.logical_and(needed(0), jnp.logical_not(needed(2))))(dx_side_copy(0).wait_send)
    pl.when(jnp.logical_and(needed(1), jnp.logical_not(needed(3))))(dx_side_copy(1).wait_send)
    early_final.wait()
    late_final.wait()
    for copy in early_copies + late_copies:
        copy.wait_send()
    for copy in early_wide + late_wide:
        copy.wait()


def reduce_all(
    info, grads, summed, first, dk, dv, early, dq, weight, positions, tables, x, g_mid, mods, gain,
    size, groups,
):
    shapes = tuple((grad.shape[0] // size, grad.shape[1]) for grad in (*grads, weight)) + tuple(
        shard.shape for shard in summed
    )
    count, full = len(shapes), len(grads) + 1
    row_count, width = x.shape
    anywhere = pl.BlockSpec(memory_space=pl.ANY)
    vmem = pl.BlockSpec(memory_space=pltpu.VMEM)
    dma = pltpu.SemaphoreType.DMA

    def scratch(*shape):
        return pltpu.VMEM(shape, BF16)

    pieces = [(piece_of(shape, 0)[1], piece_of(shape, 0)[3]) for shape in shapes]
    leads = [4] * full + [1] * len(summed)
    late = (32, 2 * width // 4)
    turns = max(1, int(math.log2(groups)) - 2)
    scratch_shapes = (
        [scratch(lead, *shape) for lead, shape in zip(leads, shapes)]
        + [scratch(lead, *shape) for lead, shape in zip(leads, shapes)]
        + [scratch(lead, *piece) for lead, piece in zip(leads, pieces)]
        + [scratch(turns, *piece) for piece in pieces]
        + [scratch(4, *shape) for shape in shapes[:full]]
        + [scratch(4, *piece) for piece in pieces[:full]] * 2
        + [
            scratch(2, row_count, width), scratch(2, row_count, width),
            scratch(2, row_count, width), pltpu.VMEM(weight.shape, F32),
            scratch(4, *shapes[full - 1]), scratch(2, row_count, width),
            scratch(4, row_count, width), scratch(4, row_count, width),
            scratch(2, row_count, width), scratch(2, row_count, width),
            scratch(*late), scratch(size, *early.shape), scratch(size, *late),
            scratch(*early.shape), scratch(*late),
            dma((count,)), dma((count,)), dma((count,)), dma((count,)), dma((count,)),
            dma((count,)), dma((count,)), dma((count, 4, 2)), dma((count, 4, 2)),
            dma((count, turns)), dma((count, turns)), dma((count, 3)), dma((count, 3)),
            dma((count,)), dma((3, 2)), dma((4,)), dma((4,)), dma((2, 2)), dma((2, 2)),
            dma((2, size)), dma((2, size)), dma((2, groups)), dma((2, groups)), dma((4,)),
        ]
    )
    views = [grad.reshape(4, 2, *shape) for grad, shape in zip(grads, shapes)]
    return pl.pallas_call(
        functools.partial(reduce_kernel, shapes, full, size, groups),
        out_shape=[jax.ShapeDtypeStruct(shape, BF16) for shape in shapes]
        + [
            jax.ShapeDtypeStruct(x.shape, F32),
            jax.ShapeDtypeStruct((groups, *early.shape), BF16),
            jax.ShapeDtypeStruct((groups, *late), BF16),
        ],
        in_specs=[pl.BlockSpec(memory_space=pltpu.SMEM)]
        + [anywhere] * (count + 3)
        + [vmem] * 9,
        out_specs=[anywhere] * count + [vmem, anywhere, anywhere],
        scratch_shapes=scratch_shapes,
        compiler_params=pltpu.CompilerParams(
            collective_id=2, has_side_effects=True, vmem_limit_bytes=REDUCE_VMEM
        ),
        name="reduce_all",
        )(
        info, *views, *summed, first, dk, dv, early, dq, weight, positions, *tables, x, g_mid, mods, gain,
    )


def tail_kernel(
    g0_ref, g1_ref, g2_ref, g3_ref, early_ref, late_ref, time_ref, ada_ref,
    o0_ref, o1_ref, o2_ref, o3_ref, g_ada_ref, g_bias_ref, g_time_ref, norm1_ref, norm2_ref, fc1_b_ref,
    fc2_b_ref, mod_ref, cond_ref, turned_ref, full_ref,
):
    for source, target in ((g0_ref, o0_ref), (g1_ref, o1_ref), (g2_ref, o2_ref), (g3_ref, o3_ref)):
        target[...] = source[...].astype(F32)
    me = lax.axis_index("narrow")
    groups, _, width = early_ref.shape
    seqs = time_ref.shape[0]
    vectors = jnp.zeros((16, width), F32)
    norm1 = jnp.zeros((2, width // 2), F32)
    picks = []
    for group in range(groups):
        early = early_ref[group].astype(F32)
        late = late_ref[group].astype(F32)
        vectors = vectors + early[16:32]
        norm1 = norm1 + late[16:18]
        rows = jnp.concatenate(
            [late[4 * at : 4 * at + 4] for at in range(4)] + [early[4 * at : 4 * at + 4] for at in range(4)],
            axis=1,
        )
        mod_ref[4 * group : 4 * group + 4, :] = rows
        sub = lax.broadcasted_iota(jnp.int32, (seqs, TILE), 0).astype(F32)
        lane = lax.broadcasted_iota(jnp.int32, (seqs, TILE), 1)
        pick = jnp.where(jnp.logical_and(sub == early[22:23, :TILE], lane < 4), 1.0, 0.0)
        picks.append(pick)
        cond_ref[4 * group : 4 * group + 4, :] = dot(
            pick.astype(BF16), time_ref[...], ((0,), (0,))
        )[:4]
    g_mod = mod_ref[...]

    def mine(row, size):
        lanes = row.shape[1]
        block = jnp.broadcast_to(row, (8, lanes))
        return pltpu.roll(block, lax.rem(lanes - me * size, lanes), 1)[:1, :size]

    g_bias_ref[...] = mine(jnp.sum(g_mod, axis=0, keepdims=True), g_bias_ref.shape[1])
    norm1_ref[...] = mine(jnp.concatenate([norm1[0:1], norm1[1:2]], axis=1), norm1_ref.shape[1])
    norm2_ref[...] = mine(vectors[0:1], norm2_ref.shape[1])
    fc2_b_ref[...] = mine(vectors[1:2], fc2_b_ref.shape[1])
    fc1_b_ref[...] = mine(
        jnp.concatenate([vectors[2 + at : 3 + at] for at in range(4)], axis=1), fc1_b_ref.shape[1]
    )
    turned_ref[...] = cond_ref[...].T
    own_rows = g_ada_ref.shape[0]
    parts = jnp.concatenate(thirds(g_mod), axis=0)
    own_cond = turned_ref[pl.ds(pl.multiple_of(me * own_rows, 8), own_rows), :].astype(BF16)
    g_ada_ref[...] = dot(jnp.concatenate([own_cond] * 3, axis=1), parts)
    g_cond = dot(parts, ada_ref[...], ((1,), (1,)))
    count = 4 * groups
    g_cond = g_cond[:count] + g_cond[count : 2 * count] + g_cond[2 * count :]
    total = jnp.zeros((seqs, TILE), F32)
    for group in range(groups):
        part = jnp.concatenate([g_cond[4 * group : 4 * group + 4], jnp.zeros((TILE - 4, TILE), F32)], axis=0)
        total = total + dot(picks[group], part, precision=HIGH)
    full_ref[...] = total
    own_seqs = g_time_ref.shape[0]
    g_time_ref[...] = full_ref[pl.ds(me * own_seqs, own_seqs), :]


def tail(grads, early, late, time_emb, ada, sizes):
    vmem = pl.BlockSpec(memory_space=pltpu.VMEM)
    groups = early.shape[0]
    devices = ada.shape[1] // sizes[2]
    return pl.pallas_call(
        tail_kernel,
        out_shape=[jax.ShapeDtypeStruct(grad.shape, F32) for grad in grads]
        + [
            jax.ShapeDtypeStruct((ada.shape[0] // devices, ada.shape[1]), F32),
            jax.ShapeDtypeStruct((1, sizes[2]), F32),
            jax.ShapeDtypeStruct((time_emb.shape[0] // devices, time_emb.shape[1]), F32),
        ]
        + [jax.ShapeDtypeStruct((1, sizes[which]), F32) for which in (0, 1, 3, 4)],
        in_specs=[vmem] * (len(grads) + 4),
        out_specs=[vmem] * (len(grads) + 7),
        scratch_shapes=[
            pltpu.VMEM((4 * groups, ada.shape[1]), F32),
            pltpu.VMEM((4 * groups, ada.shape[0]), F32),
            pltpu.VMEM((ada.shape[0], 4 * groups), F32),
            pltpu.VMEM(time_emb.shape, F32),
        ],
        compiler_params=pltpu.CompilerParams(vmem_limit_bytes=VMEM_LIMIT),
        name="tail",
    )(*grads, early, late, time_emb, ada)


def body(
    tokens, cotangent, time_emb, seq_table, lengths, positions, norm1_gain, norm2_gain,
    ada_weight, ada_bias, qkv_weight, out_weight, fc1_weight, fc1_bias, fc2_weight, fc2_bias,
):
    row_count, width = tokens.shape
    me = lax.axis_index("narrow")
    size, groups = lax.axis_size("narrow"), lax.axis_size("wide")
    slots = lengths.shape[1]
    below = np.zeros((16, slots), np.int32)
    below[:slots] = np.tril(np.ones((slots, slots), np.int32))
    table = np.zeros((16, slots), np.int32)
    table[8 : 8 + slots] = np.eye(slots, dtype=np.int32)
    info = (
        jnp.sum(
            jnp.asarray(below) * lengths[0][None, :]
            + jnp.asarray(table) * jnp.where(me == 0, seq_table, 0)[None, :],
            axis=1,
        )
        + (jnp.arange(16) == 4) * (me * row_count)
    ).astype(jnp.int32)
    seqs = jnp.pad(seq_table, (0, 8 - slots), constant_values=-1)
    onehot_table = (
        seqs[:, None] == jnp.arange(time_emb.shape[0], dtype=jnp.int32)[None, :]
    ).astype(BF16)
    cond8 = jnp.dot(onehot_table, time_emb, preferred_element_type=F32).astype(BF16)
    tables = tuple(jnp.asarray(t) for t in rotary_constants())
    pieces = (norm1_gain, norm2_gain, ada_bias, fc1_bias, fc2_bias)
    sizes = tuple(piece.size for piece in pieces)

    def spread_gather(shard):
        part = shard.shape[0] // groups
        mine = lax.dynamic_slice_in_dim(shard, lax.axis_index("wide") * part, part, 0)
        return lax.all_gather(mine, ("narrow", "wide"), axis=0, tiled=True)

    out_w, fc1 = (spread_gather(shard) for shard in (out_weight, fc1_weight))
    ada, qkv_w, fc2, x_all, position_all, vectors = gather_all(
        tokens, positions.reshape(-1, TILE), packed(pieces), (ada_weight, qkv_weight, fc2_weight), size
    )
    keys, values, first, queries, norms, mods1, gain1, gain2, bias, fc1_b, fc2_b = project(
        info, x_all, position_all, cond8, ada, vectors, sizes, qkv_w, tables, row_count
    )
    attended, mass = attend(info, queries, keys, values, norms)
    layer_out, g_fc1, g_fc2, g_out, g_att, g_mid, early = mlp(
        info, tokens, attended, cotangent, cond8, ada, bias, gain2, out_w, fc1, fc1_b, fc2, fc2_b
    )
    dq, dk, dv = attend_back(info, queries, keys, values, g_att, attended, mass)
    g_fc1 = lax.psum_scatter(g_fc1, "narrow", scatter_dimension=0, tiled=True)
    g_fc2, g_out, g_qkv, g_fc1, grad_tokens, early_all, late_all = reduce_all(
        info, (g_fc2, g_out), (g_fc1,), first, dk, dv, early, dq, qkv_w, position_all, tables, tokens,
        g_mid, mods1, gain1, size, groups,
    )
    g_fc2, g_out, g_qkv, g_fc1, g_ada, g_ada_bias, g_time, g_norm1, g_norm2, g_fc1_b, g_fc2_b = tail(
        (g_fc2, g_out, g_qkv, g_fc1), early_all, late_all, time_emb, ada, sizes
    )
    return (
        layer_out, grad_tokens, g_time, g_norm1.reshape(-1), g_norm2.reshape(-1), g_ada,
        g_ada_bias.reshape(-1), g_qkv, g_out, g_fc1, g_fc1_b.reshape(-1), g_fc2, g_fc2_b.reshape(-1),
    )


def solution(mesh):
    both = P(("wide", "narrow"), None)
    row = P("narrow")
    table = P("narrow", None)
    return jax.shard_map(
        body,
        mesh=mesh,
        in_specs=(
            both, both, P(), P("wide"), P("wide", None), P(("wide", "narrow")), row, row,
            table, row, table, table, table, row, table, row,
        ),
        out_specs=(both, both, table, row, row, table, row, table, table, table, row, table, row),
        check_vma=False,
    )
```
